32 devices in a mesh: dp: 8 (over z, y), tensor: 4 (over x, core).
Axes of the slice: x: 2, y: 2, z: 4, core: 2. Of those that a mesh axis runs over, the one named last changes fastest.
Arguments:
- block_input: bfloat16 [6656, 1024], P('dp'), may hold values from -6 to 6
- norm_first: float32 [1024], replicated, may hold values from 0.5 to 1.5
- norm_second: float32 [1024], replicated, may hold values from 0.5 to 1.5
- w_query: bfloat16 [1024, 1024], P(None, 'tensor'), may hold values from -0.1875 to 0.1875
- w_key: bfloat16 [1024, 512], P(None, 'tensor'), may hold values from -0.1875 to 0.1875
- w_value: bfloat16 [1024, 512], P(None, 'tensor'), may hold values from -0.1875 to 0.1875
- w_out: bfloat16 [1024, 1024], P('tensor'), may hold values from -4 to 4
- w_gate: bfloat16 [32, 1024, 512], P(None, None, 'tensor'), may hold values from -0.1875 to 0.1875
- w_up: bfloat16 [32, 1024, 512], P(None, None, 'tensor'), may hold values from -0.1875 to 0.1875
- w_down: bfloat16 [32, 512, 1024], P(None, 'tensor'), may hold values from -0.75 to 0.75
- routes: int32 [6656, 8], P('dp'), may hold values from 0 to 31, all different within a row; in each aligned block of 832 rows (0 to 831, 832 to 1663, ...) at most 264 rows name the same one
- gates: float32 [6656, 8], P('dp'), may hold values from 0.05 to 0.25
- parents: int32 [8, 13], P('dp'), may hold values from -1 to 12, as said below
- clip_limits: float32 [16], P('tensor'), may hold values from 1 to 8
- cotangent: bfloat16 [6656, 1024], P('dp'), may hold values from -6 to 6
Outputs:
- block_out: bfloat16 [6656, 1024], P('dp')
- grad_x: float32 [6656, 1024], P(('dp', 'tensor'))
- grad_norm_first: float32 [1024], P('dp')
- grad_norm_second: float32 [1024], P('dp')
- grad_query: float32 [1024, 1024], P('dp', 'tensor')
- grad_key: float32 [1024, 512], P('dp', 'tensor')
- grad_value: float32 [1024, 512], P('dp', 'tensor')
- grad_out_proj: float32 [1024, 1024], P('dp', 'tensor')
- grad_gate: float32 [32, 1024, 512], P('dp', None, 'tensor')
- grad_up: float32 [32, 1024, 512], P('dp', None, 'tensor')
- grad_down: float32 [32, 512, 1024], P('dp', 'tensor')
- clip_factors: float32 [16], P('tensor')
- query_scaled: bfloat16 [1024, 1024], P(None, 'tensor')
- key_scaled: bfloat16 [1024, 512], P(None, 'tensor')
The draws below stay inside these ranges and needn't reach their ends.
Inputs may be any that keep to these rules, and one draw needn't show every extreme that they name: `parents`: in every tree (row) entry 0 is -1; of entries 1 to 12, four have parent 0 and each of these four is the parent of exactly two others. `routes`: in the rows of one tree no expert is named by more than 264 rows, a bound that some block reaches.
All inputs are finite; a program needn't handle non-finite values.
Results may differ from the reference program's by a relative error of at most 0.013.
The reference program's roundings to bfloat16 on the way count: a program that leaves them out, or rounds other values in their place, can miss the bound.
Values sent between devices are 32-bit elements; how exact they have to be, the bound alone decides.
A program may use at most 384 MiB of HBM per device.

```python
import math
import jax
import jax.numpy as jnp
import numpy as np
from jax import lax

D = 1024
HEADS = 16
KV_HEADS = 8
HEAD_DIM = 64
EXPERTS = 32
TOPK = 8
FF = 512
TRUNK = 256
SEG = 48
SEGS = 13
TOK_DEV = 832
TREES = 8
TOKENS = 6656
CAP = 264


def draw_parents(key, part):

    def one_tree(subkey):
        roles = jax.random.permutation(subkey, SEGS - 1).astype(jnp.int32)
        places = (jnp.argsort(roles) + 1).astype(jnp.int32)
        branch_of = jnp.clip((roles - 4) // 2, 0, 3).astype(jnp.int32)
        rest = jnp.where(roles < 4, 0, places[branch_of]).astype(jnp.int32)
        return jnp.concatenate([jnp.full((1,), -1, jnp.int32), rest])
    return jax.vmap(one_tree)(jax.random.split(key, TREES))


def levels(rng, dims, shards, least, top_value):
    def one(dim, shards_of):
        steps = jax.random.uniform(jax.random.fold_in(jax.random.fold_in(rng, 6), dim), (shards_of,), jnp.float32, least / len(shards), top_value / len(shards))
        return jnp.repeat(jnp.exp(steps), dims[dim] // shards_of).reshape((-1,) + (1,) * (len(dims) - dim - 1))

    gain = one(*shards[0])
    for cut in shards[1:]:
        gain = gain * one(*cut)
    return gain


def shared_out(own_key, own, number, rows, number_of, top, most, slope):
    order = jax.random.permutation(own_key, number_of)
    packed, usual = portions_of(number_of, rows * top, most, slope, True), portions_of(number_of, rows * top, most, slope, False)
    places = jnp.arange(number_of)

    def named(lengths, rotation):
        used = int((lengths > 0).sum())
        fixed = max(1, used // 4)
        shifted = fixed + (places - fixed + rotation * (used - fixed)) % max(1, number_of - fixed)
        return jnp.zeros((number_of,), jnp.int32).at[order[jnp.where(places < fixed, places, shifted)]].set(jnp.asarray(lengths, jnp.int32))

    lengths = jnp.where(number % 4 == 0, named(packed, number // 4), named(usual, number - number // 4 - 1))
    mixed = jax.random.permutation(jax.random.fold_in(own, 3), number_of)
    giver, receiver = mixed[0:number_of // 2 * 2:2], mixed[1:number_of // 2 * 2:2]
    slack = jnp.minimum(lengths[giver] - 1, most - lengths[receiver]) // 2
    slack = jnp.where((giver == order[0]) | (receiver == order[0]) | (lengths[receiver] == 0), 0, jnp.maximum(slack, 0))
    shifted = jax.random.randint(jax.random.fold_in(own, 4), (number_of // 2,), 0, 1 << 20) % (slack + 1)
    lengths = lengths.at[giver].add(-shifted).at[receiver].add(shifted)
    items = jnp.searchsorted(jnp.cumsum(lengths), jnp.arange(rows * top), side="right").astype(jnp.int32)
    table = items.reshape(top, rows).T
    table = table[jax.random.permutation(jax.random.fold_in(own, 1), rows)]
    rotation = jax.random.randint(jax.random.fold_in(own, 2), (rows, 1), 0, top)
    return jnp.take_along_axis(table, (jnp.arange(top)[None, :] + rotation) % top, axis=1)


def portions_of(amount, total, most, lean, full):
    portions = [(1 << 20) // math.isqrt(rank ** lean) + 1 for rank in range(1, amount + 1)]
    largest = most if full else min(most, max(-(-total // amount), total * portions[0] // sum(portions)))
    least = 1 if total - largest >= amount - 1 else 0
    counts, surplus = [largest] + [least] * (amount - 1), total - largest - least * (amount - 1)
    while surplus > 0:
        free = [i for i in range(1, amount) if counts[i] < largest] or [i for i in range(1, amount) if counts[i] < most]
        whole, budget = sum([portions[i] for i in free]), surplus
        for i in free:
            more = min(most - counts[i], max(1, budget * portions[i] // whole), surplus)
            counts[i] = counts[i] + more
            surplus = surplus - more
    return np.array(counts)


def bell_draw(own_key, shape, deviation, bound, cuts=(), kind=jnp.bfloat16):
    values = jax.random.normal(own_key, shape, jnp.float32) * deviation
    if len(cuts) > 0:
        values = levels(own_key, shape, cuts, -0.22, 0.18) * values
    return jnp.clip(values, min=-bound, max=bound).astype(kind)


def setup_inputs(seed: int = 0) -> dict:
    key_of = jax.random.split(jax.random.key(seed), 16)
    block_input = bell_draw(key_of[0], (TOKENS, D), 1.0, 6.0, ((0, 8),))
    norm_first = jnp.clip(1.0 + 0.1 * jax.random.normal(key_of[1], (D,), jnp.float32), 0.5, 1.5)
    norm_second = jnp.clip(1.0 + 0.1 * jax.random.normal(key_of[2], (D,), jnp.float32), 0.5, 1.5)
    w_query = bell_draw(key_of[3], (D, HEADS * HEAD_DIM), D ** -0.5, 0.1875, ((1, 4),))
    w_key = bell_draw(key_of[4], (D, KV_HEADS * HEAD_DIM), D ** -0.5, 0.1875, ((1, 4),))
    w_value = bell_draw(key_of[5], (D, KV_HEADS * HEAD_DIM), D ** -0.5, 0.1875, ((1, 4),))
    w_out = bell_draw(key_of[6], (HEADS * HEAD_DIM, D), (max(HEADS * HEAD_DIM // 512, 1)) ** -0.5, 4.0, ((0, 4),))
    w_gate = bell_draw(key_of[7], (EXPERTS, D, FF), D ** -0.5, 0.1875, ((2, 4),))
    w_up = bell_draw(key_of[8], (EXPERTS, D, FF), D ** -0.5, 0.1875, ((2, 4),))
    w_down = bell_draw(key_of[9], (EXPERTS, FF, D), (FF // 8) ** -0.5, 0.75, ((1, 4),))
    routes_keys = jax.random.split(jax.random.fold_in(key_of[10], 1), TOKENS // TOK_DEV)
    routes_turns = jax.random.permutation(jax.random.fold_in(key_of[10], 3), TOKENS // TOK_DEV)
    routes = jax.vmap(lambda own, number: shared_out(jax.random.fold_in(key_of[10], 2), own, number, TOK_DEV, EXPERTS, TOPK, CAP, 1))(routes_keys, routes_turns).reshape((TOKENS, TOPK))
    gates = jnp.clip(0.05 + 0.2 * jax.random.uniform(key_of[11], (TOKENS, TOPK), jnp.float32) ** levels(key_of[11], (TOKENS, TOPK), ((0, 8),), -0.2, 0.2), 0.05, 0.25)
    parents = draw_parents(jax.random.fold_in(key_of[15], 71), 0)
    clip_limits = jnp.clip(1.0 + 7.0 * jax.random.uniform(key_of[13], (HEADS,), jnp.float32) ** levels(key_of[13], (HEADS,), ((0, 4),), -0.2, 0.2), 1.0, 8.0)
    cotangent = bell_draw(key_of[14], (TOKENS, D), 1.0, 6.0, ((0, 8),))
    return dict(block_input=block_input, norm_first=norm_first, norm_second=norm_second, w_query=w_query, w_key=w_key, w_value=w_value, w_out=w_out, w_gate=w_gate, w_up=w_up, w_down=w_down, routes=routes, gates=gates, parents=parents, clip_limits=clip_limits, cotangent=cotangent)


@jax.custom_vjp
def low(v):
    return lax.optimization_barrier(v.astype(jnp.bfloat16)).astype(jnp.float32)

@jax.custom_vjp
def low_back(v):
    return v

def low_keep(v):
    return (low(v), None)

def low_pass(kept, grad):
    return (grad,)

def back_keep(v):
    return (v, None)

def back_low(kept, grad):
    return (low(grad),)
low.defvjp(low_keep, low_pass)
low_back.defvjp(back_keep, back_low)
epsilon = 1e-06
theta_base = 10000.0

def tree_tables(parent_row, count):
    slot_ids = jnp.arange(SEGS, dtype=jnp.int32)
    safe_parent = jnp.maximum(parent_row, 0)
    hot_parent = (safe_parent[:, None] == slot_ids[None, :]).astype(jnp.int32)
    grand_raw = lax.optimization_barrier(jnp.sum(hot_parent * parent_row[None, :], axis=1)).astype(jnp.int32)
    grand_parent = jnp.where(parent_row >= 0, grand_raw, -1).astype(jnp.int32)
    visible = (slot_ids[:, None] == slot_ids[None, :]) | (slot_ids[None, :] == parent_row[:, None]) | (slot_ids[None, :] == grand_parent[:, None])
    depth = (parent_row >= 0).astype(jnp.int32) + (grand_parent >= 0).astype(jnp.int32)
    token_ids = jnp.arange(count, dtype=jnp.int32)
    segment = jnp.where(token_ids < TRUNK, 0, 1 + (token_ids - TRUNK) // SEG).astype(jnp.int32)
    local_index = jnp.where(token_ids < TRUNK, token_ids, (token_ids - TRUNK) % SEG).astype(jnp.int32)
    seg_match = segment[:, None] == slot_ids[None, :]
    token_depth = lax.optimization_barrier(jnp.sum(seg_match.astype(jnp.int32) * depth[None, :], axis=1)).astype(jnp.int32)
    position = jnp.where(segment == 0, token_ids, TRUNK + (token_depth - 1) * SEG + local_index).astype(jnp.int32)
    return (segment, position, visible.astype(jnp.float32), seg_match.astype(jnp.float32), token_ids)

def rotary_tables(position, head_dim):
    half = head_dim // 2
    inverse = theta_base ** (-(jnp.arange(half, dtype=jnp.float32) * 2.0 / head_dim))
    angle = position.astype(jnp.float32)[:, None] * inverse[None, :]
    return (jnp.cos(angle), jnp.sin(angle))

def rotate(values, cosine, sine):
    half = values.shape[-1] // 2
    first = values[..., :half]
    second = values[..., half:]
    return jnp.concatenate([first * cosine - second * sine, second * cosine + first * sine], axis=-1)

def expert_slots(route_rows, gate_rows):
    flat = route_rows.reshape(-1).astype(jnp.int32)
    total = flat.shape[0]
    expert_ids = jnp.arange(EXPERTS, dtype=jnp.int32)
    onehot = (flat[:, None] == expert_ids[None, :]).astype(jnp.int32)
    rank = (lax.optimization_barrier(jnp.sum(jnp.cumsum(onehot, axis=0) * onehot, axis=1)) - 1).astype(jnp.int32)
    slot_assign = jnp.full((EXPERTS, CAP), total, jnp.int32).at[flat, rank].set(jnp.arange(total, dtype=jnp.int32))
    slot_token = (slot_assign // TOPK).astype(jnp.int32)
    padded = jnp.concatenate([gate_rows.reshape(-1), jnp.zeros((1,), gate_rows.dtype)])
    return (slot_token, padded[slot_assign])

def tree_block(weights, tree_x, route_rows, gate_rows, parent_row):
    gain_first, gain_second, wq, wk, wv, wo, wg, wu, wd = weights
    highest = lax.Precision.HIGHEST
    count = tree_x.shape[0]
    segment, position, visible, seg_hot, token_ids = tree_tables(parent_row, count)
    reach = jnp.dot(seg_hot, visible)
    mask = (jnp.dot(reach, seg_hot.T) > 0.5) & ((segment[:, None] != segment[None, :]) | (token_ids[:, None] >= token_ids[None, :]))
    cosine, sine = rotary_tables(position, HEAD_DIM)
    cosine = cosine[:, None, :]
    sine = sine[:, None, :]
    normal_first = tree_x * lax.rsqrt(lax.optimization_barrier(jnp.mean(tree_x * tree_x, axis=-1, keepdims=True)) + epsilon)
    input_first = low(normal_first * gain_first)
    queries = low(rotate(low_back(jnp.dot(input_first, wq, precision=highest)).reshape(count, HEADS, HEAD_DIM), cosine, sine))
    keys = low(rotate(low_back(jnp.dot(input_first, wk, precision=highest)).reshape(count, KV_HEADS, HEAD_DIM), cosine, sine))
    values = low(low_back(jnp.dot(input_first, wv, precision=highest))).reshape(count, KV_HEADS, HEAD_DIM)
    group = HEADS // KV_HEADS
    scale_factor = HEAD_DIM ** (-0.5)
    query_heads = queries.reshape(count, KV_HEADS, group, HEAD_DIM).transpose(1, 0, 2, 3)
    key_heads = keys.transpose(1, 0, 2)
    value_heads = values.transpose(1, 0, 2)

    def head_pair(inputs):
        query_group, key_one, value_one = inputs
        raw = low_back(jnp.einsum('qgd,kd->gqk', query_group, key_one, precision=highest))
        scores = jnp.where(mask[None], raw * scale_factor, -1e+30)
        top = lax.optimization_barrier(jnp.max(scores, axis=-1, keepdims=True))
        expo = jnp.exp(scores - top)
        probs = expo / lax.optimization_barrier(jnp.sum(expo, axis=-1, keepdims=True))
        attended = jnp.einsum('gqk,kd->qgd', low(probs), value_one, precision=highest)
        return (attended, lax.optimization_barrier(jnp.max(top[..., 0], axis=-1)))
    attended, peaks = lax.map(jax.checkpoint(head_pair), (query_heads, key_heads, value_heads))
    attended = attended.transpose(1, 0, 2, 3).reshape(count, HEADS * HEAD_DIM)
    attended = low(low_back(attended))
    hidden = tree_x + low_back(jnp.dot(attended, wo, precision=highest))
    normal_second = hidden * lax.rsqrt(lax.optimization_barrier(jnp.mean(hidden * hidden, axis=-1, keepdims=True)) + epsilon)
    input_second = low(normal_second * gain_second)
    slot_token, slot_gate = expert_slots(route_rows, gate_rows)
    padded = jnp.concatenate([input_second, jnp.zeros((1, D), input_second.dtype)], axis=0)
    slot_rows = padded[slot_token]
    gate_pre = low_back(jnp.einsum('ecd,edf->ecf', slot_rows, wg, precision=highest))
    up_pre = low_back(jnp.einsum('ecd,edf->ecf', slot_rows, wu, precision=highest))
    act = low(jax.nn.silu(gate_pre) * up_pre)
    expert_rows = low_back(jnp.einsum('ecf,efd->ecd', act, wd, precision=highest))
    mixture = jnp.zeros((count + 1, D), hidden.dtype).at[slot_token].add(expert_rows * slot_gate[..., None])[:count]
    return (hidden + mixture, peaks.reshape(HEADS))

def reference(block_input, norm_first, norm_second, w_query, w_key, w_value, w_out, w_gate, w_up, w_down, routes, gates, parents, clip_limits, cotangent):

    def forward(x_float, gain_first, gain_second, wq, wk, wv, wo, wg, wu, wd):
        weights = (gain_first, gain_second, wq, wk, wv, wo, wg, wu, wd)
        tree_inputs = x_float.reshape(TREES, TOK_DEV, D)
        tree_routes = routes.reshape(TREES, TOK_DEV, TOPK)
        tree_gates = gates.reshape(TREES, TOK_DEV, TOPK)

        def one_tree(inputs):
            return tree_block(weights, inputs[0], inputs[1], inputs[2], inputs[3])
        outputs, peaks = lax.map(jax.checkpoint(one_tree), (tree_inputs, tree_routes, tree_gates, parents))
        return (outputs.reshape(TOKENS, D), lax.optimization_barrier(jnp.max(peaks, axis=0)))
    primals = (block_input.astype(jnp.float32), norm_first.astype(jnp.float32), norm_second.astype(jnp.float32), w_query.astype(jnp.float32), w_key.astype(jnp.float32), w_value.astype(jnp.float32), w_out.astype(jnp.float32), w_gate.astype(jnp.float32), w_up.astype(jnp.float32), w_down.astype(jnp.float32))
    result, backward, peaks = jax.vjp(forward, *primals, has_aux=True)
    grads = backward(cotangent.astype(jnp.float32))
    factors = clip_limits / jnp.maximum(peaks, clip_limits)
    group = HEADS // KV_HEADS
    query_scale = jnp.repeat(jnp.sqrt(factors), HEAD_DIM)
    key_scale = jnp.repeat(jnp.sqrt(lax.optimization_barrier(jnp.min(factors.reshape(KV_HEADS, group), axis=1))), HEAD_DIM)
    query_scaled = (primals[3] * query_scale[None, :]).astype(jnp.bfloat16)
    key_scaled = (primals[4] * key_scale[None, :]).astype(jnp.bfloat16)
    return (result.astype(jnp.bfloat16), grads[0], grads[1], grads[2], grads[3], grads[4], grads[5], grads[6].T, grads[7], grads[8], grads[9], factors, query_scaled, key_scaled)
```

```python
import functools

import jax
import jax.numpy as jnp
from jax import lax
from jax.experimental import pallas as pl
from jax.experimental.pallas import tpu as pltpu
from jax.sharding import PartitionSpec as P

HEAD_DIM = 64
EXPERTS = 32
TOPK = 8
TRUNK = 256
SEG = 48
SEGS = 13


epsilon = 1e-06
theta_base = 10000.0
expert_group = 4


def tree_tables(parent_row, count):
    slot_ids = jnp.arange(SEGS, dtype=jnp.int32)
    safe_parent = jnp.maximum(parent_row, 0)
    hot_parent = (safe_parent[:, None] == slot_ids[None, :]).astype(jnp.int32)
    grand_raw = jnp.sum(hot_parent * parent_row[None, :], axis=1)
    grand_parent = jnp.where(parent_row >= 0, grand_raw, -1)
    visible = (
        (slot_ids[:, None] == slot_ids[None, :])
        | (slot_ids[None, :] == parent_row[:, None])
        | (slot_ids[None, :] == grand_parent[:, None])
    )
    depth = (parent_row >= 0).astype(jnp.int32) + (grand_parent >= 0).astype(jnp.int32)
    token_ids = jnp.arange(count, dtype=jnp.int32)
    segment = jnp.where(token_ids < TRUNK, 0, 1 + (token_ids - TRUNK) // SEG)
    local_index = jnp.where(token_ids < TRUNK, token_ids, (token_ids - TRUNK) % SEG)
    seg_match = segment[:, None] == slot_ids[None, :]
    token_depth = jnp.sum(seg_match.astype(jnp.int32) * depth[None, :], axis=1)
    position = jnp.where(segment == 0, token_ids, TRUNK + (token_depth - 1) * SEG + local_index)
    return (
        segment,
        position,
        visible.astype(jnp.float32),
        seg_match.astype(jnp.float32),
        token_ids,
    )


def rotary_tables(position, head_dim):
    half = head_dim // 2
    inverse = theta_base ** (-(jnp.arange(half, dtype=jnp.float32) * 2.0 / head_dim))
    angle = position.astype(jnp.float32)[:, None] * inverse[None, :]
    return (jnp.cos(angle)[:, None, :], jnp.sin(angle)[:, None, :])


def rotate(values, cosine, sine):
    half = values.shape[-1] // 2
    first = values[..., :half]
    second = values[..., half:]
    return jnp.concatenate(
        [first * cosine - second * sine, second * cosine + first * sine], axis=-1
    )


def rotate_back(grads, cosine, sine):
    half = grads.shape[-1] // 2
    first = grads[..., :half]
    second = grads[..., half:]
    return jnp.concatenate(
        [first * cosine + second * sine, second * cosine - first * sine], axis=-1
    )


F32=jnp.float32; BF=jnp.bfloat16
def dot(a,b): return jnp.dot(a,b,preferred_element_type=F32)
def dot_t(a,b): return lax.dot_general(a,b,(((1,),(1,)),((),())),preferred_element_type=F32)
def dot_l(a,b): return lax.dot_general(a,b,(((0,),(0,)),((),())),preferred_element_type=F32)

def expert_core(x, c, g, wcat, wdcat, n):
    f=wdcat.shape[0]
    GU=dot(x,wcat)
    G=GU[:,:f]; U=GU[:,f:]
    D=dot_t(c,wdcat)
    ge=jnp.concatenate([jnp.broadcast_to(v,(x.shape[0],f//n)) for v in g],axis=1)
    sg=jax.nn.sigmoid(G)
    si=G*sg
    act=((si*U).astype(BF).astype(F32)*ge).astype(BF)
    da=D*ge
    dG=(da*U*(sg+si*(1.0-sg))).astype(BF)
    dU=(da*si).astype(BF)
    return act,jnp.concatenate([dG,dU],axis=1)

def local_kernel(x_ref,c_ref,g_ref,wg_ref,wu_ref,wd_ref,mix_ref,d2_ref,wc_ref,*,n,rows):
    step = pl.program_id(0)
    f=wg_ref.shape[2]
    for i in range(n):
        wc_ref[:,i*f:(i+1)*f]=wg_ref[i]
        wc_ref[:,(n+i)*f:(n+i+1)*f]=wu_ref[i]
    wd=wd_ref[...].reshape(n*f,wd_ref.shape[2])
    @pl.when(step==0)
    def _():
        mix_ref[...]=jnp.zeros_like(mix_ref)
        d2_ref[...]=jnp.zeros_like(d2_ref)
    T=x_ref.shape[0]
    def body(i,_):
        r=pl.ds(pl.multiple_of(i*rows,rows),rows)
        g=[g_ref[0,r,j:j+1] for j in range(n)]
        act,dgu=expert_core(x_ref[r,:],c_ref[r,:],g,wc_ref[...],wd,n)
        mix_ref[r,:]+=dot(act,wd)
        d2_ref[r,:]+=dot_t(dgu,wc_ref[...])
        return 0
    lax.fori_loop(0,T//rows,body,0)

def moe_local(x,c,gd,wg,wu,wd,n=4,rows=416):
    T,Dm=x.shape; E,_,f=wg.shape
    g3=gd.reshape(T,E//n,n).transpose(1,0,2)
    return pl.pallas_call(
        functools.partial(local_kernel,n=n,rows=rows),
        grid=(E//n,),
        in_specs=[pl.BlockSpec((T,Dm),lambda i:(0,0)),pl.BlockSpec((T,Dm),lambda i:(0,0)),
                  pl.BlockSpec((1,T,n),lambda i:(i,0,0)),
                  pl.BlockSpec((n,Dm,f),lambda i:(i,0,0)),pl.BlockSpec((n,Dm,f),lambda i:(i,0,0)),
                  pl.BlockSpec((n,f,Dm),lambda i:(i,0,0))],
        out_specs=[pl.BlockSpec((T,Dm),lambda i:(0,0))]*2,
        out_shape=[jax.ShapeDtypeStruct((T,Dm),F32)]*2,
        scratch_shapes=[pltpu.VMEM((Dm,2*n*f),BF)],
        compiler_params=pltpu.CompilerParams(vmem_limit_bytes=56*2**20),
    )(x,c,g3,wg,wu,wd)

def owner_kernel(x_ref,c_ref,g_ref,wg_ref,wu_ref,wd_ref,gg_ref,gu_ref,gdn_ref,wc_ref,acc_ref,accd_ref,*,n,steps):
    step = pl.program_id(0)
    f=wg_ref.shape[2]
    @pl.when(step==0)
    def _():
        for i in range(n):
            wc_ref[:,i*f:(i+1)*f]=wg_ref[i]
            wc_ref[:,(n+i)*f:(n+i+1)*f]=wu_ref[i]
        acc_ref[...]=jnp.zeros_like(acc_ref)
        accd_ref[...]=jnp.zeros_like(accd_ref)
    wd=wd_ref[...].reshape(n*f,wd_ref.shape[2])
    x=x_ref[...].astype(BF); c=c_ref[...].astype(BF)
    g=[g_ref[:,j:j+1] for j in range(n)]
    act,dgu=expert_core(x,c,g,wc_ref[...],wd,n)
    acc_ref[...]+=dot_l(x,dgu)
    accd_ref[...]+=dot_l(act,c)
    @pl.when(step==steps-1)
    def _():
        for i in range(n):
            gg_ref[i]=acc_ref[:,i*f:(i+1)*f]
            gu_ref[i]=acc_ref[:,(n+i)*f:(n+i+1)*f]
            gdn_ref[i]=accd_ref[i*f:(i+1)*f,:]

def moe_owner(x,c,g,wg,wu,wd,rows=832):
    T,Dm=x.shape; n,_,f=wg.shape
    steps=T//rows
    return pl.pallas_call(
        functools.partial(owner_kernel,n=n,steps=steps),
        grid=(steps,),
        in_specs=[pl.BlockSpec((rows,Dm),lambda i:(i,0)),pl.BlockSpec((rows,Dm),lambda i:(i,0)),
                  pl.BlockSpec((rows,n),lambda i:(i,0)),
                  pl.BlockSpec((n,Dm,f),lambda i:(0,0,0)),pl.BlockSpec((n,Dm,f),lambda i:(0,0,0)),
                  pl.BlockSpec((n,f,Dm),lambda i:(0,0,0))],
        out_specs=[pl.BlockSpec((n,Dm,f),lambda i:(0,0,0)),pl.BlockSpec((n,Dm,f),lambda i:(0,0,0)),
                  pl.BlockSpec((n,f,Dm),lambda i:(0,0,0))],
        out_shape=[jax.ShapeDtypeStruct((n,Dm,f),F32)]*2+[jax.ShapeDtypeStruct((n,f,Dm),F32)],
        scratch_shapes=[pltpu.VMEM((Dm,2*n*f),BF),pltpu.VMEM((Dm,2*n*f),F32),pltpu.VMEM((n*f,Dm),F32)],
        compiler_params=pltpu.CompilerParams(vmem_limit_bytes=60*2**20),
    )(x,c,g,wg,wu,wd)


def local(
    block_input,
    norm_first,
    norm_second,
    w_query,
    w_key,
    w_value,
    w_out,
    w_gate,
    w_up,
    w_down,
    routes,
    gates,
    parents,
    clip_limits,
    cotangent,
):
    count, width = block_input.shape
    head_dim = HEAD_DIM
    query_cols = w_query.shape[1]
    key_cols = w_key.shape[1]
    query_heads = query_cols // head_dim
    kv_heads = key_cols // head_dim
    group = query_heads // kv_heads
    scale_factor = head_dim ** (-0.5)
    segment, position, visible, seg_hot, token_ids = tree_tables(parents[0], count)
    reach = jnp.dot(seg_hot, visible)
    cosine, sine = rotary_tables(position, head_dim)

    def mask_for():
        near = jnp.dot(reach, seg_hot.T) > 0.5
        return near & (
            (segment[:, None] != segment[None, :]) | (token_ids[:, None] >= token_ids[None, :])
        )

    share_rows = count // lax.axis_size("tensor")
    row_begin = lax.axis_index("tensor") * share_rows
    cot_all = lax.all_gather(
        lax.dynamic_slice_in_dim(cotangent, row_begin, share_rows, 0).astype(jnp.float32),
        ("dp", "tensor"),
        tiled=True,
    )
    x_float = block_input.astype(jnp.float32)
    inverse_first = lax.rsqrt(jnp.mean(x_float * x_float, axis=-1, keepdims=True) + epsilon)
    normal_first = x_float * inverse_first
    input_first = (normal_first * norm_first).astype(jnp.bfloat16)
    query_pre = jnp.dot(input_first, w_query, preferred_element_type=jnp.float32).reshape(
        count, query_heads, head_dim
    )
    key_pre = jnp.dot(input_first, w_key, preferred_element_type=jnp.float32).reshape(
        count, kv_heads, head_dim
    )
    queries = rotate(query_pre, cosine, sine).astype(jnp.bfloat16).reshape(count, query_cols)
    keys_view = rotate(key_pre, cosine, sine).astype(jnp.bfloat16)
    values_view = (
        jnp.dot(input_first, w_value, preferred_element_type=jnp.float32)
        .astype(jnp.bfloat16)
        .reshape(count, kv_heads, head_dim)
    )

    def scores_for():
        query_block = queries.reshape(count, kv_heads, group, head_dim)
        raw = (
            jnp.einsum("qgrd,kgd->grqk", query_block, keys_view, preferred_element_type=jnp.float32)
            * scale_factor
        )
        return (query_block, jnp.where(mask_for()[None, None], raw, -1e30))

    head_peaks = jnp.full((kv_heads, group), -1e30, jnp.float32)
    query_block, scores = scores_for()
    top = jnp.max(scores, axis=-1, keepdims=True)
    expo = jnp.exp(scores - top)
    totals = jnp.sum(expo, axis=-1, keepdims=True)
    probs = (expo / totals).astype(jnp.bfloat16)
    log_norms = [(top + jnp.log(totals))[..., 0]]
    head_peaks = jnp.maximum(head_peaks, jnp.max(top[..., 0], axis=-1))
    attended_block = jnp.einsum(
        "grqk,kgd->qgrd", probs, values_view, preferred_element_type=jnp.float32
    )
    attended_parts = attended_block.astype(jnp.bfloat16).reshape(count, query_cols)
    peaks_local = head_peaks.reshape(query_heads)
    attn_part = jnp.dot(attended_parts, w_out, preferred_element_type=jnp.float32)
    attn_whole = lax.psum(attn_part, "tensor")
    hidden = x_float + attn_whole
    inverse_second = lax.rsqrt(jnp.mean(hidden * hidden, axis=-1, keepdims=True) + epsilon)
    normal_second = hidden * inverse_second
    input_second = (normal_second * norm_second).astype(jnp.bfloat16)
    peaks_all = lax.pmax(peaks_local, "dp")
    routed = routes[:, :, None] == jnp.arange(EXPERTS, dtype=jnp.int32)[None, None, :]
    dense_gates = jnp.sum(jnp.where(routed, gates[:, :, None], 0.0), axis=1)
    own = EXPERTS // lax.axis_size("dp")
    own_begin = lax.axis_index("dp") * own
    own_gates = lax.all_to_all(dense_gates, "dp", 1, 0, tiled=True)
    mixture_part, d_part = moe_local(input_second, cotangent, dense_gates, w_gate, w_up, w_down)
    x_all = lax.all_gather(
        lax.dynamic_slice_in_dim(input_second, row_begin, share_rows, 0).astype(jnp.float32),
        ("dp", "tensor"),
        tiled=True,
    )
    gate_shard, up_shard, down_shard = moe_owner(
        x_all,
        cot_all,
        own_gates,
        lax.dynamic_slice_in_dim(w_gate, own_begin, own, 0),
        lax.dynamic_slice_in_dim(w_up, own_begin, own, 0),
        lax.dynamic_slice_in_dim(w_down, own_begin, own, 0),
    )
    mixture = lax.psum(mixture_part, "tensor")
    block_out = (hidden + mixture).astype(jnp.bfloat16)
    cot_float = cotangent.astype(jnp.float32)
    d_second = lax.psum(d_part, "tensor")
    scaled_second = d_second * norm_second
    grad_gain_second = jnp.sum(d_second * normal_second, axis=0)
    d_hidden = cot_float + inverse_second * (
        scaled_second
        - normal_second * jnp.mean(scaled_second * normal_second, axis=-1, keepdims=True)
    )
    d_branch = d_hidden.astype(jnp.bfloat16)
    grad_out_local = jnp.einsum(
        "td,tc->dc", d_branch, attended_parts, preferred_element_type=jnp.float32
    )
    d_attended = jnp.einsum(
        "td,cd->tc", d_branch, w_out, preferred_element_type=jnp.float32
    ).astype(jnp.bfloat16)
    d_keys = jnp.zeros((count, kv_heads, head_dim), jnp.float32)
    d_values = jnp.zeros((count, kv_heads, head_dim), jnp.float32)
    d_query_parts = []
    for block_index, row_start in enumerate(range(0, count, count)):
        query_block, scores = scores_for()
        probs = jnp.exp(scores - log_norms[block_index][..., None])
        d_att_block = d_attended.reshape(count, kv_heads, group, head_dim)
        d_probs = jnp.einsum(
            "qgrd,kgd->grqk", d_att_block, values_view, preferred_element_type=jnp.float32
        )
        row_dot = jnp.sum(probs * d_probs, axis=-1, keepdims=True)
        d_scores = (probs * (d_probs - row_dot) * scale_factor).astype(jnp.bfloat16)
        d_query_parts.append(
            jnp.einsum(
                "grqk,kgd->qgrd", d_scores, keys_view, preferred_element_type=jnp.float32
            ).reshape(count, query_heads, head_dim)
        )
        d_keys = jnp.einsum(
            "grqk,qgrd->kgd", d_scores, query_block, preferred_element_type=jnp.float32
        )
        d_values = jnp.einsum(
            "grqk,qgrd->kgd",
            probs.astype(jnp.bfloat16),
            d_att_block,
            preferred_element_type=jnp.float32,
        )
    d_query_pre = (
        rotate_back(d_query_parts[0], cosine, sine).astype(jnp.bfloat16).reshape(count, query_cols)
    )
    d_key_pre = rotate_back(d_keys, cosine, sine).astype(jnp.bfloat16).reshape(count, key_cols)
    d_value_low = d_values.astype(jnp.bfloat16).reshape(count, key_cols)
    grad_query_local = jnp.einsum(
        "td,tc->dc", input_first, d_query_pre, preferred_element_type=jnp.float32
    )
    grad_key_local = jnp.einsum(
        "td,tc->dc", input_first, d_key_pre, preferred_element_type=jnp.float32
    )
    grad_value_local = jnp.einsum(
        "td,tc->dc", input_first, d_value_low, preferred_element_type=jnp.float32
    )
    d_first = jnp.einsum("tc,dc->td", d_query_pre, w_query, preferred_element_type=jnp.float32)
    d_first = d_first + jnp.einsum(
        "tc,dc->td", d_key_pre, w_key, preferred_element_type=jnp.float32
    )
    d_first = d_first + jnp.einsum(
        "tc,dc->td", d_value_low, w_value, preferred_element_type=jnp.float32
    )
    d_first_rows = lax.psum_scatter(d_first, "tensor", scatter_dimension=0, tiled=True)
    normal_rows = lax.dynamic_slice_in_dim(normal_first, row_begin, share_rows, 0)
    inverse_rows = lax.dynamic_slice_in_dim(inverse_first, row_begin, share_rows, 0)
    hidden_grad_rows = lax.dynamic_slice_in_dim(d_hidden, row_begin, share_rows, 0)
    scaled_first = d_first_rows * norm_first
    grad_gain_first_part = jnp.sum(d_first_rows * normal_rows, axis=0)
    grad_x = hidden_grad_rows + inverse_rows * (
        scaled_first - normal_rows * jnp.mean(scaled_first * normal_rows, axis=-1, keepdims=True)
    )
    (
        query_shard,
        key_shard,
        value_shard,
        out_shard,
        first_shard,
        second_shard,
    ) = (
        lax.psum_scatter(grad_query_local, "dp", scatter_dimension=0, tiled=True),
        lax.psum_scatter(grad_key_local, "dp", scatter_dimension=0, tiled=True),
        lax.psum_scatter(grad_value_local, "dp", scatter_dimension=0, tiled=True),
        lax.psum_scatter(grad_out_local, "dp", scatter_dimension=0, tiled=True),
        lax.psum_scatter(grad_gain_first_part, "dp", scatter_dimension=0, tiled=True),
        lax.psum_scatter(grad_gain_second, "dp", scatter_dimension=0, tiled=True),
    )
    first_gain_grad = lax.psum(first_shard, "tensor")
    factors = clip_limits / jnp.maximum(peaks_all, clip_limits)
    query_scale = jnp.repeat(jnp.sqrt(factors), head_dim)
    key_scale = jnp.repeat(jnp.sqrt(jnp.min(factors.reshape(kv_heads, group), axis=1)), head_dim)
    query_scaled = (w_query.astype(jnp.float32) * query_scale[None, :]).astype(jnp.bfloat16)
    key_scaled = (w_key.astype(jnp.float32) * key_scale[None, :]).astype(jnp.bfloat16)
    return (
        block_out,
        grad_x,
        first_gain_grad,
        second_shard,
        query_shard,
        key_shard,
        value_shard,
        out_shard,
        gate_shard,
        up_shard,
        down_shard,
        factors,
        query_scaled,
        key_scaled,
    )


def solution(mesh):
    placed = (
        P("dp", None),
        P(),
        P(),
        P(None, "tensor"),
        P(None, "tensor"),
        P(None, "tensor"),
        P("tensor", None),
        P(None, None, "tensor"),
        P(None, None, "tensor"),
        P(None, "tensor", None),
        P("dp", None),
        P("dp", None),
        P("dp", None),
        P("tensor"),
        P("dp", None),
    )
    return jax.shard_map(
        local,
        mesh=mesh,
        in_specs=placed,
        out_specs=(
            P("dp", None),
            P(("dp", "tensor"), None),
            P("dp"),
            P("dp"),
            P("dp", "tensor"),
            P("dp", "tensor"),
            P("dp", "tensor"),
            P("dp", "tensor"),
            P("dp", None, "tensor"),
            P("dp", None, "tensor"),
            P("dp", "tensor", None),
            P("tensor"),
            P(None, "tensor"),
            P(None, "tensor"),
        ),
        check_vma=False,
    )
```

```python
import functools

import jax
import jax.numpy as jnp
from jax import lax
from jax.experimental import pallas as pl
from jax.experimental.pallas import tpu as pltpu
from jax.sharding import PartitionSpec as P

HEAD_DIM = 64
EXPERTS = 32
TOPK = 8
TRUNK = 256
SEG = 48
SEGS = 13


epsilon = 1e-06
theta_base = 10000.0
expert_group = 4


def tree_tables(parent_row, count):
    slot_ids = jnp.arange(SEGS, dtype=jnp.int32)
    safe_parent = jnp.maximum(parent_row, 0)
    hot_parent = (safe_parent[:, None] == slot_ids[None, :]).astype(jnp.int32)
    grand_raw = jnp.sum(hot_parent * parent_row[None, :], axis=1)
    grand_parent = jnp.where(parent_row >= 0, grand_raw, -1)
    visible = (
        (slot_ids[:, None] == slot_ids[None, :])
        | (slot_ids[None, :] == parent_row[:, None])
        | (slot_ids[None, :] == grand_parent[:, None])
    )
    depth = (parent_row >= 0).astype(jnp.int32) + (grand_parent >= 0).astype(jnp.int32)
    token_ids = jnp.arange(count, dtype=jnp.int32)
    segment = jnp.where(token_ids < TRUNK, 0, 1 + (token_ids - TRUNK) // SEG)
    local_index = jnp.where(token_ids < TRUNK, token_ids, (token_ids - TRUNK) % SEG)
    seg_match = segment[:, None] == slot_ids[None, :]
    token_depth = jnp.sum(seg_match.astype(jnp.int32) * depth[None, :], axis=1)
    position = jnp.where(segment == 0, token_ids, TRUNK + (token_depth - 1) * SEG + local_index)
    return (
        segment,
        position,
        visible.astype(jnp.float32),
        seg_match.astype(jnp.float32),
        token_ids,
    )


def rotary_tables(position, head_dim):
    half = head_dim // 2
    inverse = theta_base ** (-(jnp.arange(half, dtype=jnp.float32) * 2.0 / head_dim))
    angle = position.astype(jnp.float32)[:, None] * inverse[None, :]
    return (jnp.cos(angle)[:, None, :], jnp.sin(angle)[:, None, :])


def rotate(values, cosine, sine):
    half = values.shape[-1] // 2
    first = values[..., :half]
    second = values[..., half:]
    return jnp.concatenate(
        [first * cosine - second * sine, second * cosine + first * sine], axis=-1
    )


def rotate_back(grads, cosine, sine):
    half = grads.shape[-1] // 2
    first = grads[..., :half]
    second = grads[..., half:]
    return jnp.concatenate(
        [first * cosine + second * sine, second * cosine - first * sine], axis=-1
    )


F32 = jnp.float32
BF = jnp.bfloat16
MESH = pl.DeviceIdType.MESH
CHUNK = 64
PART = 8
BOTH = 16
EG = 4
LAG = 4


def dot(a, b):
    return jnp.dot(a, b, preferred_element_type=F32)


def dot_t(a, b):
    return lax.dot_general(a, b, (((1,), (1,)), ((), ())), preferred_element_type=F32)


def dot_l(a, b):
    return lax.dot_general(a, b, (((0,), (0,)), ((), ())), preferred_element_type=F32)


def expert_core(x, c, g, wcat, wdcat):
    n = len(g)
    f = wdcat.shape[0]
    both = dot(x, wcat)
    gate = both[:, :f]
    up = both[:, f:]
    d_act = dot_t(c, wdcat)
    wide = jnp.concatenate([jnp.broadcast_to(v, (x.shape[0], f // n)) for v in g], axis=1)
    sigma = jax.nn.sigmoid(gate)
    silu = gate * sigma
    act = ((silu * up).astype(BF).astype(F32) * wide).astype(BF)
    d_act = d_act * wide
    d_gate = (d_act * up * (sigma + silu * (1.0 - sigma))).astype(BF)
    d_up = (d_act * silu).astype(BF)
    return act, jnp.concatenate([d_gate, d_up], axis=1)


def experts_kernel(
    pair_ref,
    x_ref,
    c_ref,
    g_ref,
    og_ref,
    wg_ref,
    wu_ref,
    wd_ref,
    all_ref,
    mix_ref,
    sum_ref,
    gg_ref,
    gu_ref,
    gd_ref,
    wbg,
    wbu,
    wbd,
    wc,
    mixp,
    part,
    half_in,
    quarter_in,
    owg,
    owu,
    owd,
    owc,
    acc,
    accd,
    ubuf,
    w_sem,
    ow_sem,
    load_sem,
    own_sem,
    out_sem,
    send_sem,
    recv_sem,
    ssend,
    srecv,
):
    T, D = x_ref.shape
    A = all_ref.shape[0]
    E, _, f = wg_ref.shape
    n_own = owg.shape[0]
    chunks = T // CHUNK
    p = lax.axis_index("dp")
    t = lax.axis_index("tensor")
    a = p // 2
    b = p % 2
    xq = t // 2
    c = t % 2
    y_dev = (a * 2 + 1 - b, t)
    x_dev = (p, (1 - xq) * 2 + c)
    c_dev = (p, xq * 2 + 1 - c)
    z_devs = [(((a + j) % A) * 2 + b, t) for j in range(1, A)]

    barrier = pltpu.get_barrier_semaphore()
    for dev in z_devs + [y_dev, x_dev, c_dev]:
        pl.semaphore_signal(barrier, inc=1, device_id=dev, device_id_type=MESH)
    pl.semaphore_wait(barrier, A + 2)

    def rows1(k):
        return pl.ds(pl.multiple_of(k * CHUNK + (c * 2 + xq) * PART, 8), PART)

    def rows_pair(k):
        return pl.ds(pl.multiple_of(k * CHUNK + c * 2 * PART, 8), 2 * PART)

    def rows2(k):
        return pl.ds(pl.multiple_of(k * CHUNK + 4 * PART + c * BOTH, 8), BOTH)

    def remote(src, dst, stage, k, dev):
        return pltpu.make_async_remote_copy(
            src_ref=src,
            dst_ref=dst,
            send_sem=send_sem.at[stage, k],
            recv_sem=recv_sem.at[stage, k],
            device_id=dev,
            device_id_type=MESH,
        )

    def wait_bytes(ref, sem):
        pltpu.make_async_copy(ref, ref, sem).wait()

    def z_start(k):
        for rows in (rows1(k), rows2(k)):
            for dev in z_devs:
                remote(pair_ref.at[:, rows], all_ref.at[a, b, :, rows], 0, k, dev).start()

    def z_wait(k):
        wait_bytes(all_ref.at[pl.ds(0, A - 1), 0, :, pl.ds(0, PART + BOTH)], recv_sem.at[0, k])

    def y_start(k):
        for rows in (rows1(k), rows2(k)):
            remote(all_ref.at[:, b, :, rows], all_ref.at[:, b, :, rows], 1, k, y_dev).start()

    def y_wait(k):
        wait_bytes(all_ref.at[:, 0, :, pl.ds(0, PART + BOTH)], recv_sem.at[1, k])

    def x_start(k):
        rows = rows1(k)
        remote(all_ref.at[:, :, :, rows], all_ref.at[:, :, :, rows], 2, k, x_dev).start()

    def x_wait(k):
        wait_bytes(all_ref.at[:, :, :, pl.ds(0, PART)], recv_sem.at[2, k])

    def c_start(k):
        for rows in (rows_pair(k), rows2(k)):
            remote(all_ref.at[:, :, :, rows], all_ref.at[:, :, :, rows], 3, k, c_dev).start()

    def c_wait(k):
        wait_bytes(all_ref.at[:, :, :, pl.ds(0, 2 * PART + BOTH)], recv_sem.at[3, k])

    def own_copy(k, i):
        rows = (rows1(k), rows2(k))[i]
        return pltpu.make_async_copy(pair_ref.at[:, rows], all_ref.at[a, b, :, rows], own_sem.at[i, k])

    def pump(s):
        k = s - 3

        @pl.when((k >= 0) & (k < chunks))
        def _():
            x_wait(k)
            c_start(k)

        k2 = s - 2

        @pl.when((k2 >= 0) & (k2 < chunks))
        def _():
            y_wait(k2)
            x_start(k2)

        k1 = s - 1

        @pl.when((k1 >= 0) & (k1 < chunks))
        def _():
            z_wait(k1)
            own_copy(k1, 0).wait()
            own_copy(k1, 1).wait()
            y_start(k1)

        k0 = s + 1

        @pl.when(k0 < chunks)
        def _():
            z_start(k0)

    z_start(0)

    def copies(k, _):
        own_copy(k, 0).start()
        own_copy(k, 1).start()
        return 0

    lax.fori_loop(0, chunks, copies, 0)

    first_own = p * n_own
    own_loads = [
        pltpu.make_async_copy(src.at[pl.ds(first_own, n_own)], dst, ow_sem.at[i])
        for i, (src, dst) in enumerate(((wg_ref, owg), (wu_ref, owu), (wd_ref, owd)))
    ]
    for copy in own_loads:
        copy.start()

    def w_loads(i, slot):
        return [
            pltpu.make_async_copy(src.at[pl.ds(i * EG, EG)], dst.at[slot], w_sem.at[j, slot])
            for j, (src, dst) in enumerate(((wg_ref, wbg), (wu_ref, wbu), (wd_ref, wbd)))
        ]

    for copy in w_loads(0, 0):
        copy.start()
    part[...] = jnp.zeros_like(part)
    mixp[...] = jnp.zeros_like(mixp)
    groups = E // EG
    rows_at = T // 2

    def group_step(i, _):
        slot = i % 2

        @pl.when(i + 1 < groups)
        def _():
            for copy in w_loads(i + 1, 1 - slot):
                copy.start()

        @pl.when(i % 2 == 0)
        def _():
            pump(i // 2)

        for copy in w_loads(i, slot):
            copy.wait()
        for j in range(EG):
            wc[:, j * f : (j + 1) * f] = wbg[slot, j]
            wc[:, (EG + j) * f : (EG + j + 1) * f] = wbu[slot, j]
        wd = wbd[slot].reshape(EG * f, D)

        def rows_step(r, _):
            rows = pl.ds(pl.multiple_of(r * rows_at, 16), rows_at)
            g = [g_ref[i, rows, j : j + 1] for j in range(EG)]
            act, dgu = expert_core(x_ref[rows, :], c_ref[rows, :], g, wc[...], wd)
            mixp[rows, :] += dot(act, wd)
            part[rows, :] += dot_t(dgu, wc[...])
            return 0

        lax.fori_loop(0, 2, rows_step, 0)
        return 0

    lax.fori_loop(0, groups, group_step, 0)

    for copy in own_loads:
        copy.wait()
    for j in range(n_own):
        owc[:, j * f : (j + 1) * f] = owg[j]
        owc[:, (n_own + j) * f : (n_own + j + 1) * f] = owu[j]
    acc[...] = jnp.zeros_like(acc)
    accd[...] = jnp.zeros_like(accd)

    half = T // 2
    quarter = T // 4
    keep = pl.ds(pl.multiple_of(c * half, 16), half)
    give = pl.ds(pl.multiple_of((1 - c) * half, 16), half)
    keep_q = pl.ds(pl.multiple_of(c * half + xq * quarter, 16), quarter)
    give_q = pl.ds(pl.multiple_of(c * half + (1 - xq) * quarter, 16), quarter)

    def summing(src, dst, i, dev):
        return pltpu.make_async_remote_copy(
            src_ref=src,
            dst_ref=dst,
            send_sem=ssend.at[i],
            recv_sem=srecv.at[i],
            device_id=dev,
            device_id_type=MESH,
        )

    sum_copies = [
        summing(part.at[give], half_in, 0, c_dev),
        summing(part.at[give_q], quarter_in, 1, x_dev),
        summing(part.at[keep_q], sum_ref.at[keep_q], 2, x_dev),
        summing(sum_ref.at[keep], sum_ref.at[keep], 3, c_dev),
    ]
    own_sum = pltpu.make_async_copy(part.at[keep_q], sum_ref.at[keep_q], own_sem.at[0, chunks])

    mix_out = pltpu.make_async_copy(mixp, mix_ref, own_sem.at[1, chunks])
    mix_out.start()

    first = groups // 2
    units = A // 4
    group_trees = A // units

    def load(k, u, slot):
        return pltpu.make_async_copy(
            all_ref.at[pl.ds(u * group_trees, group_trees), :, :, pl.ds(pl.multiple_of(k * CHUNK, 8), CHUNK)],
            ubuf.at[slot],
            load_sem.at[slot],
        )

    wdo = owd[...].reshape(n_own * f, D)

    def own_unit(k, u, slot):
        load(k, u, slot).wait()
        size = group_trees * 2 * CHUNK
        xs = ubuf[slot, :, :, 0].reshape(size, D).astype(BF)
        cs = ubuf[slot, :, :, 1].reshape(size, D).astype(BF)
        g = [og_ref[k, pl.ds(u * size, size), j : j + 1] for j in range(n_own)]
        act, dgu = expert_core(xs, cs, g, owc[...], wdo)
        acc[...] += dot_l(xs, dgu)
        accd[...] += dot_l(act, cs)

    def slot_step(s, _):
        pump(s)

        @pl.when(s == first)
        def _():
            sum_copies[0].start()

        @pl.when(s == first + 1)
        def _():
            sum_copies[0].wait()
            part[keep, :] += half_in[...]
            sum_copies[1].start()

        @pl.when(s == first + 3)
        def _():
            sum_copies[1].wait()
            part[keep_q, :] += quarter_in[...]
            own_sum.start()
            sum_copies[2].start()

        @pl.when(s == first + 5)
        def _():
            own_sum.wait()
            sum_copies[2].wait()
            sum_copies[3].start()

        @pl.when(s == first + 7)
        def _():
            sum_copies[3].wait()

        k = s - LAG

        @pl.when((k >= 0) & (k < chunks))
        def _():
            c_wait(k)
            load(k, 0, 0).start()
            for u in range(units):
                if u + 1 < units:
                    load(k, u + 1, (u + 1) % 2).start()
                own_unit(k, u, u % 2)

        return 0

    lax.fori_loop(first, chunks + LAG, slot_step, 0)

    outs = []
    for j in range(n_own):
        outs += [
            pltpu.make_async_copy(acc.at[:, pl.ds(j * f, f)], gg_ref.at[j], out_sem.at[0, j]),
            pltpu.make_async_copy(acc.at[:, pl.ds((n_own + j) * f, f)], gu_ref.at[j], out_sem.at[1, j]),
            pltpu.make_async_copy(accd.at[pl.ds(j * f, f)], gd_ref.at[j], out_sem.at[2, j]),
        ]
    for copy in outs:
        copy.start()

    def sends(k, _):
        wait_bytes(all_ref.at[pl.ds(0, A - 1), 0, :, pl.ds(0, PART + BOTH)], send_sem.at[0, k])
        wait_bytes(all_ref.at[:, 0, :, pl.ds(0, PART + BOTH)], send_sem.at[1, k])
        wait_bytes(all_ref.at[:, :, :, pl.ds(0, PART)], send_sem.at[2, k])
        wait_bytes(all_ref.at[:, :, :, pl.ds(0, 2 * PART + BOTH)], send_sem.at[3, k])
        return 0

    lax.fori_loop(0, chunks, sends, 0)
    mix_out.wait()
    for copy in outs:
        copy.wait()


def experts(pair, x, c, dense_gates, own_gates, wg, wu, wd, trees):
    T, D = x.shape
    E, _, f = wg.shape
    own = E // trees
    chunks = T // CHUNK
    A = trees // 2
    gates_in = dense_gates.reshape(T, E // EG, EG).transpose(1, 0, 2)
    og = own_gates.reshape(trees, chunks, CHUNK, own).transpose(1, 0, 2, 3)
    og = og.reshape(chunks, trees * CHUNK, own)
    vmem = pl.BlockSpec(memory_space=pltpu.VMEM)
    hbm = pl.BlockSpec(memory_space=pl.ANY)
    DMA = pltpu.SemaphoreType.DMA
    slots = 2 if A > 4 else 1
    out = pl.pallas_call(
        experts_kernel,
        in_specs=[hbm, vmem, vmem, vmem, vmem, hbm, hbm, hbm],
        out_specs=[hbm] * 6,
        out_shape=[
            jax.ShapeDtypeStruct((A, 2, 2, T, D), F32),
            jax.ShapeDtypeStruct((T, D), F32),
            jax.ShapeDtypeStruct((T, D), F32),
            jax.ShapeDtypeStruct((own, D, f), F32),
            jax.ShapeDtypeStruct((own, D, f), F32),
            jax.ShapeDtypeStruct((own, f, D), F32),
        ],
        scratch_shapes=[
            pltpu.VMEM((2, EG, D, f), BF),
            pltpu.VMEM((2, EG, D, f), BF),
            pltpu.VMEM((2, EG, f, D), BF),
            pltpu.VMEM((D, 2 * EG * f), BF),
            pltpu.VMEM((T, D), F32),
            pltpu.VMEM((T, D), F32),
            pltpu.VMEM((T // 2, D), F32),
            pltpu.VMEM((T // 4, D), F32),
            pltpu.VMEM((own, D, f), BF),
            pltpu.VMEM((own, D, f), BF),
            pltpu.VMEM((own, f, D), BF),
            pltpu.VMEM((D, 2 * own * f), BF),
            pltpu.VMEM((D, 2 * own * f), F32),
            pltpu.VMEM((own * f, D), F32),
            pltpu.VMEM((slots, 4, 2, 2, CHUNK, D), F32),
            DMA((3, 2)),
            DMA((3,)),
            DMA((2,)),
            DMA((2, chunks + 1)),
            DMA((3, own)),
            DMA((4, chunks)),
            DMA((4, chunks)),
            DMA((4,)),
            DMA((4,)),
        ],
        compiler_params=pltpu.CompilerParams(
            collective_id=0, has_side_effects=True, vmem_limit_bytes=60 * 2**20
        ),
    )(pair, x, c, gates_in, og, wg, wu, wd)
    return out[1:]


VMEM = pl.BlockSpec(memory_space=pltpu.VMEM)
HBM = pl.BlockSpec(memory_space=pl.ANY)
DMA = pltpu.SemaphoreType.DMA


def sync_with(devices):
    barrier = pltpu.get_barrier_semaphore()
    for dev in devices:
        pl.semaphore_signal(barrier, inc=1, device_id=dev, device_id_type=MESH)
    pl.semaphore_wait(barrier, len(devices))


def send(src, dst, out_sem, in_sem, dev):
    return pltpu.make_async_remote_copy(
        src_ref=src,
        dst_ref=dst,
        send_sem=out_sem,
        recv_sem=in_sem,
        device_id=dev,
        device_id_type=MESH,
    )


def hidden_kernel(
    att_ref,
    wo_ref,
    x_ref,
    c_ref,
    gain_ref,
    msg_ref,
    hidden_ref,
    xb_ref,
    pair_ref,
    got_ref,
    others,
    ssem,
    rsem,
    msend,
    mrecv,
    csem,
    *,
    trees,
):
    T, D = x_ref.shape
    width = att_ref.shape[1]
    half = T // 2
    p = lax.axis_index("dp")
    t = lax.axis_index("tensor")
    xq = t // 2
    c = t % 2
    x_dev = (p, (1 - xq) * 2 + c)
    c_dev = (p, xq * 2 + 1 - c)
    peers = [((p + j) % trees, t) for j in range(1, trees)]
    sync_with(peers + [x_dev, c_dev])
    rows = [pl.ds(i * half, half) for i in range(2)]
    to_x = [send(att_ref.at[r], others.at[1, r], ssem.at[0, i], rsem.at[0, i], x_dev) for i, r in enumerate(rows)]
    to_c = [send(att_ref.at[r], others.at[0, r], ssem.at[1, i], rsem.at[1, i], c_dev) for i, r in enumerate(rows)]
    on = [send(others.at[1, r], others.at[2, r], ssem.at[2, i], rsem.at[2, i], c_dev) for i, r in enumerate(rows)]
    for copy in to_x + to_c:
        copy.start()
    messages = [
        send(msg_ref.at[dev[0]], got_ref.at[j], msend.at[j], mrecv.at[j], dev) for j, dev in enumerate(peers, 1)
    ]
    for copy in messages:
        copy.start()
    mine = pltpu.make_async_copy(msg_ref.at[p], got_ref.at[0], csem)
    mine.start()
    pair_ref[1] = c_ref[...].astype(F32)

    def proj(block, owner):
        w = wo_ref[pl.ds(pl.multiple_of(owner * width, 128), width), :].astype(BF)
        return dot(block.astype(BF), w)

    for i, r in enumerate(rows):
        hidden_ref[r, :] = x_ref[r, :].astype(F32) + proj(att_ref[r, :], t)
    for i, r in enumerate(rows):
        to_c[i].wait()
        hidden_ref[r, :] += proj(others[0, r, :], xq * 2 + 1 - c)
    for i, r in enumerate(rows):
        to_x[i].wait()
        on[i].start()
        hidden_ref[r, :] += proj(others[1, r, :], (1 - xq) * 2 + c)
    for i, r in enumerate(rows):
        on[i].wait()
        hidden = hidden_ref[r, :] + proj(others[2, r, :], (1 - xq) * 2 + 1 - c)
        hidden_ref[r, :] = hidden
        inverse = lax.rsqrt(jnp.mean(hidden * hidden, axis=-1, keepdims=True) + epsilon)
        low = (hidden * inverse * gain_ref[...]).astype(BF)
        xb_ref[r, :] = low
        pair_ref[0, r, :] = low.astype(F32)
    for copy in messages:
        copy.wait()
    mine.wait()


def hidden_step(att, wo_all, x, c, gain, msgs):
    T, D = x.shape
    trees = msgs.shape[0]
    return pl.pallas_call(
        functools.partial(hidden_kernel, trees=trees),
        in_specs=[VMEM] * 6,
        out_specs=[VMEM] * 4,
        out_shape=[
            jax.ShapeDtypeStruct((T, D), F32),
            jax.ShapeDtypeStruct((T, D), BF),
            jax.ShapeDtypeStruct((2, T, D), F32),
            jax.ShapeDtypeStruct(msgs.shape, F32),
        ],
        scratch_shapes=[
            pltpu.VMEM((3,) + att.shape, F32),
            DMA((3, 2)),
            DMA((3, 2)),
            DMA((trees,)),
            DMA((trees,)),
            DMA(()),
        ],
        compiler_params=pltpu.CompilerParams(
            collective_id=1, has_side_effects=True, vmem_limit_bytes=50 * 2**20
        ),
    )(att, wo_all, x, c, gain.reshape(1, D), msgs)


def finish_kernel(
    x_ref,
    hid_ref,
    dh_ref,
    xn_ref,
    dq_ref,
    dk_ref,
    dv_ref,
    att_ref,
    db_ref,
    wq_ref,
    wk_ref,
    wv_ref,
    mix_ref,
    gain_ref,
    gs_ref,
    out_ref,
    gx_ref,
    g1_ref,
    g2_ref,
    gq_ref,
    gk_ref,
    gv_ref,
    go_ref,
    grads,
    ybuf,
    zbuf,
    first,
    mixp,
    tot,
    half_in,
    mhalf_in,
    quarter_in,
    mquarter_in,
    xrows,
    dhrows,
    hid,
    gvec,
    gvec_in,
    msg,
    msg_in,
    ysem,
    yrsem,
    zsem,
    zrsem,
    tsem,
    trsem,
    vsem,
    vrsem,
    msem,
    mrsem,
    lsem,
):
    trees, R = msg.shape[0], msg.shape[2]
    A = grads.shape[1]
    T, D = xn_ref.shape
    Q = T // 4
    p = lax.axis_index("dp")
    t = lax.axis_index("tensor")
    a = p // 2
    b = p % 2
    xq = t // 2
    c = t % 2
    y_dev = (a * 2 + 1 - b, t)
    x_dev = (p, (1 - xq) * 2 + c)
    c_dev = (p, xq * 2 + 1 - c)
    f_dev = (p, (1 - xq) * 2 + 1 - c)
    peers = [((p + j) % trees, t) for j in range(1, trees)]
    sync_with(peers + [x_dev, c_dev, f_dev])
    my_rows = pl.ds(pl.multiple_of(t * Q, 16), Q)
    loads = [
        pltpu.make_async_copy(x_ref.at[my_rows], xrows, lsem.at[0]),
        pltpu.make_async_copy(dh_ref.at[my_rows], dhrows, lsem.at[1]),
        pltpu.make_async_copy(hid_ref, hid, lsem.at[2]),
        pltpu.make_async_copy(mix_ref, mixp, lsem.at[3]),
    ]
    for copy in reversed(loads):
        copy.start()

    W = grads.shape[4]
    to_y = [send(grads.at[i, :, 1 - b], ybuf.at[i], ysem.at[i], yrsem.at[i], y_dev) for i in range(3)]

    def z_sends(i):
        return [
            send(
                grads.at[i, (a + j) % A, b],
                zbuf.at[i, j - 1],
                zsem.at[i, j - 1],
                zrsem.at[i, j - 1],
                (((a + j) % A) * 2 + b, t),
            )
            for j in range(1, A)
        ]

    dqkv = jnp.concatenate([dq_ref[...], dk_ref[...], dv_ref[...]], axis=1)
    out_grad = dot_l(db_ref[...], att_ref[...])
    grads[0] = out_grad.reshape(A, 2, R, W)
    to_y[0].start()
    loads[3].wait()
    core_mix = send(mixp.at[:, 1 - c], mhalf_in, tsem.at[4], trsem.at[4], c_dev)
    core_mix.start()
    grads[1] = dot_l(xn_ref[...], dq_ref[...]).reshape(A, 2, R, W)
    to_y[1].start()
    first_all = dot_t(dq_ref[...], wq_ref[...])
    first_all += dot_t(dk_ref[...], wk_ref[...])
    first_all += dot_t(dv_ref[...], wv_ref[...])
    first[...] = first_all.reshape(2, 2, Q, D)
    core_first = send(first.at[:, 1 - c], half_in, tsem.at[0], trsem.at[0], c_dev)
    core_first.start()
    grads[2] = dot_l(xn_ref[...], dqkv[:, W:]).reshape(A, 2, R, W)
    to_y[2].start()
    core_first.wait()
    first[:, c] += half_in[...]
    x_first = send(first.at[1 - xq, c], quarter_in, tsem.at[1], trsem.at[1], x_dev)
    x_first.start()
    core_mix.wait()
    mixp[:, c] += mhalf_in[...]
    x_mix = send(mixp.at[1 - xq, c], mquarter_in, tsem.at[5], trsem.at[5], x_dev)
    x_mix.start()

    def y_done(i):
        to_y[i].wait()
        grads[i, :, b] += ybuf[i]
        copies = z_sends(i)
        for copy in copies:
            copy.start()
        return copies

    pending = [y_done(0)]
    loads[0].wait()
    loads[1].wait()
    x_first.wait()
    d_first = first[xq, c] + quarter_in[...]
    x32 = xrows[...].astype(F32)
    inverse = lax.rsqrt(jnp.mean(x32 * x32, axis=-1, keepdims=True) + epsilon)
    normal = x32 * inverse
    scaled = d_first * gain_ref[...]
    gx_ref[...] = dhrows[...] + inverse * (
        scaled - normal * jnp.mean(scaled * normal, axis=-1, keepdims=True)
    )
    gvec[0:1, :] = jnp.sum(d_first * normal, axis=0, keepdims=True)
    v_sends = [
        send(gvec, gvec_in.at[j], vsem.at[j], vrsem.at[j], dev) for j, dev in enumerate((x_dev, c_dev, f_dev))
    ]
    for copy in v_sends:
        copy.start()
    pending.append(y_done(1))
    x_mix.wait()
    tot[xq, c] = mixp[xq, c] + mquarter_in[...]
    back_x = send(tot.at[xq, c], tot.at[xq, c], tsem.at[6], trsem.at[6], x_dev)
    back_x.start()
    for copy in v_sends:
        copy.wait()
    total = gvec[0:1, :] + gvec_in[0, 0:1, :] + gvec_in[1, 0:1, :] + gvec_in[2, 0:1, :]
    for i in range(trees):
        msg[i, 0:1, :] = total[:, i * R : (i + 1) * R]
        msg[i, 1:2, :] = gs_ref[0:1, i * R : (i + 1) * R]
    m_sends = [
        send(msg.at[dev[0]], msg_in.at[j], msem.at[j], mrsem.at[j], dev) for j, dev in enumerate(peers)
    ]
    for copy in m_sends:
        copy.start()
    pending.append(y_done(2))

    def z_done(i):
        for copy in pending[i]:
            copy.wait()
        whole = grads[i, a, b]
        for j in range(A - 1):
            whole += zbuf[i, j]
        return whole

    go_ref[...] = z_done(0)
    gq_ref[...] = z_done(1)
    back_x.wait()
    back_c = send(tot.at[:, c], tot.at[:, c], tsem.at[7], trsem.at[7], c_dev)
    back_c.start()
    loads[2].wait()
    for copy in m_sends:
        copy.wait()
    mine = msg[p]
    for j in range(trees - 1):
        mine += msg_in[j]
    g1_ref[...] = mine[0:1]
    g2_ref[...] = mine[1:2]
    back_c.wait()
    out_ref[...] = (hid[...] + tot[...]).astype(BF)
    kv = z_done(2)
    gk_ref[...] = kv[:, : W // 2]
    gv_ref[...] = kv[:, W // 2 :]


def finish(x, hidden, d_hidden, xn, dq, dk, dv, att, db, wq, wk, wv, mix, gain, gain_second, trees):
    T, D = x.shape
    W = wq.shape[1]
    A = trees // 2
    R = D // trees
    Q = T // 4
    S = jax.ShapeDtypeStruct
    outs = pl.pallas_call(
        finish_kernel,
        in_specs=[HBM] * 3 + [VMEM] * 9 + [HBM] + [VMEM] * 2,
        out_specs=[VMEM] * 8,
        out_shape=[
            S((2, 2, Q, D), BF),
            S((Q, D), F32),
            S((1, R), F32),
            S((1, R), F32),
            S((R, W), F32),
            S((R, W // 2), F32),
            S((R, W // 2), F32),
            S((R, W), F32),
        ],
        scratch_shapes=[
            pltpu.VMEM((3, A, 2, R, W), F32),
            pltpu.VMEM((3, A, R, W), F32),
            pltpu.VMEM((3, A - 1, R, W), F32),
            pltpu.VMEM((2, 2, Q, D), F32),
            pltpu.VMEM((2, 2, Q, D), F32),
            pltpu.VMEM((2, 2, Q, D), F32),
            pltpu.VMEM((2, Q, D), F32),
            pltpu.VMEM((2, Q, D), F32),
            pltpu.VMEM((Q, D), F32),
            pltpu.VMEM((Q, D), F32),
            pltpu.VMEM((Q, D), BF),
            pltpu.VMEM((Q, D), F32),
            pltpu.VMEM((2, 2, Q, D), F32),
            pltpu.VMEM((8, D), F32),
            pltpu.VMEM((3, 8, D), F32),
            pltpu.VMEM((trees, 8, R), F32),
            pltpu.VMEM((trees - 1, 8, R), F32),
            DMA((3,)),
            DMA((3,)),
            DMA((3, A - 1)),
            DMA((3, A - 1)),
            DMA((8,)),
            DMA((8,)),
            DMA((3,)),
            DMA((3,)),
            DMA((trees - 1,)),
            DMA((trees - 1,)),
            DMA((4,)),
        ],
        compiler_params=pltpu.CompilerParams(
            collective_id=2, has_side_effects=True, vmem_limit_bytes=58 * 2**20
        ),
    )(
        x,
        hidden.reshape(2, 2, Q, D),
        d_hidden,
        xn,
        dq,
        dk,
        dv,
        att,
        db,
        wq,
        wk,
        wv,
        mix.reshape(2, 2, Q, D),
        gain.reshape(1, D),
        gain_second.reshape(1, D),
    )
    block_out, grad_x, g1, g2, gq, gk, gv, go = outs
    return block_out.reshape(T, D), grad_x, g1.reshape(R), g2.reshape(R), gq, gk, gv, go


def local(
    block_input,
    norm_first,
    norm_second,
    w_query,
    w_key,
    w_value,
    w_out,
    w_gate,
    w_up,
    w_down,
    routes,
    gates,
    parents,
    clip_limits,
    cotangent,
):
    count, width = block_input.shape
    head_dim = HEAD_DIM
    query_cols = w_query.shape[1]
    key_cols = w_key.shape[1]
    query_heads = query_cols // head_dim
    kv_heads = key_cols // head_dim
    group = query_heads // kv_heads
    scale_factor = head_dim ** (-0.5)
    segment, position, visible, seg_hot, token_ids = tree_tables(parents[0], count)
    reach = jnp.dot(seg_hot, visible)
    cosine, sine = rotary_tables(position, head_dim)

    def mask_for():
        near = jnp.dot(reach, seg_hot.T) > 0.5
        return near & (
            (segment[:, None] != segment[None, :]) | (token_ids[:, None] >= token_ids[None, :])
        )

    wo_all = lax.all_gather(w_out.astype(jnp.float32), "tensor", tiled=True)
    routed = routes[:, :, None] == jnp.arange(EXPERTS, dtype=jnp.int32)[None, None, :]
    dense_gates = jnp.sum(jnp.where(routed, gates[:, :, None], 0.0), axis=1)
    trees = lax.axis_size("dp")
    own = EXPERTS // trees
    x_float = block_input.astype(jnp.float32)
    inverse_first = lax.rsqrt(jnp.mean(x_float * x_float, axis=-1, keepdims=True) + epsilon)
    normal_first = x_float * inverse_first
    input_first = (normal_first * norm_first).astype(jnp.bfloat16)
    query_pre = jnp.dot(input_first, w_query, preferred_element_type=jnp.float32).reshape(
        count, query_heads, head_dim
    )
    key_pre = jnp.dot(input_first, w_key, preferred_element_type=jnp.float32).reshape(
        count, kv_heads, head_dim
    )
    queries = rotate(query_pre, cosine, sine).astype(jnp.bfloat16).reshape(count, query_cols)
    keys_view = rotate(key_pre, cosine, sine).astype(jnp.bfloat16)
    values_view = (
        jnp.dot(input_first, w_value, preferred_element_type=jnp.float32)
        .astype(jnp.bfloat16)
        .reshape(count, kv_heads, head_dim)
    )

    def scores_for():
        query_block = queries.reshape(count, kv_heads, group, head_dim)
        raw = (
            jnp.einsum("qgrd,kgd->grqk", query_block, keys_view, preferred_element_type=jnp.float32)
            * scale_factor
        )
        return (query_block, jnp.where(mask_for()[None, None], raw, -1e30))

    head_peaks = jnp.full((kv_heads, group), -1e30, jnp.float32)
    query_block, scores = scores_for()
    top = jnp.max(scores, axis=-1, keepdims=True)
    expo = jnp.exp(scores - top)
    totals = jnp.sum(expo, axis=-1, keepdims=True)
    probs = (expo / totals).astype(jnp.bfloat16)
    log_norms = [(top + jnp.log(totals))[..., 0]]
    head_peaks = jnp.maximum(head_peaks, jnp.max(top[..., 0], axis=-1))
    attended_block = jnp.einsum(
        "grqk,kgd->qgrd", probs, values_view, preferred_element_type=jnp.float32
    )
    attended_parts = attended_block.astype(jnp.bfloat16).reshape(count, query_cols)
    peaks_local = head_peaks.reshape(query_heads)
    msgs = jnp.concatenate(
        [
            dense_gates.T.reshape(trees, own, count),
            jnp.zeros((trees, 7 - own, count), jnp.float32),
            jnp.broadcast_to(
                jnp.pad(peaks_local, (0, count - query_heads))[None, None, :], (trees, 1, count)
            ),
        ],
        axis=1,
    )
    hidden, input_second, pair, got = hidden_step(
        attended_parts.astype(jnp.float32), wo_all, block_input, cotangent, norm_second, msgs
    )
    inverse_second = lax.rsqrt(jnp.mean(hidden * hidden, axis=-1, keepdims=True) + epsilon)
    normal_second = hidden * inverse_second
    peaks_all = jnp.max(got[:, 7, :query_heads], axis=0)
    order = (lax.axis_index("dp") - jnp.arange(trees)) % trees
    hot = (order[:, None] == jnp.arange(trees)[None, :]).astype(jnp.float32)
    own_gates = jnp.sum(hot[:, :, None, None] * got[:, None, :own, :], axis=0)
    own_gates = own_gates.transpose(0, 2, 1).reshape(trees * count, own)
    cot_float = cotangent.astype(jnp.float32)
    mixture_part, d_second, gate_shard, up_shard, down_shard = experts(
        pair, input_second, cotangent, dense_gates, own_gates, w_gate, w_up, w_down, trees
    )
    scaled_second = d_second * norm_second
    grad_gain_second = jnp.sum(d_second * normal_second, axis=0)
    d_hidden = cot_float + inverse_second * (
        scaled_second
        - normal_second * jnp.mean(scaled_second * normal_second, axis=-1, keepdims=True)
    )
    d_branch = d_hidden.astype(jnp.bfloat16)
    d_attended = jnp.einsum(
        "td,cd->tc", d_branch, w_out, preferred_element_type=jnp.float32
    ).astype(jnp.bfloat16)
    d_keys = jnp.zeros((count, kv_heads, head_dim), jnp.float32)
    d_values = jnp.zeros((count, kv_heads, head_dim), jnp.float32)
    d_query_parts = []
    for block_index, row_start in enumerate(range(0, count, count)):
        query_block, scores = scores_for()
        probs = jnp.exp(scores - log_norms[block_index][..., None])
        d_att_block = d_attended.reshape(count, kv_heads, group, head_dim)
        d_probs = jnp.einsum(
            "qgrd,kgd->grqk", d_att_block, values_view, preferred_element_type=jnp.float32
        )
        row_dot = jnp.sum(probs * d_probs, axis=-1, keepdims=True)
        d_scores = (probs * (d_probs - row_dot) * scale_factor).astype(jnp.bfloat16)
        d_query_parts.append(
            jnp.einsum(
                "grqk,kgd->qgrd", d_scores, keys_view, preferred_element_type=jnp.float32
            ).reshape(count, query_heads, head_dim)
        )
        d_keys = jnp.einsum(
            "grqk,qgrd->kgd", d_scores, query_block, preferred_element_type=jnp.float32
        )
        d_values = jnp.einsum(
            "grqk,qgrd->kgd",
            probs.astype(jnp.bfloat16),
            d_att_block,
            preferred_element_type=jnp.float32,
        )
    d_query_pre = (
        rotate_back(d_query_parts[0], cosine, sine).astype(jnp.bfloat16).reshape(count, query_cols)
    )
    d_key_pre = rotate_back(d_keys, cosine, sine).astype(jnp.bfloat16).reshape(count, key_cols)
    d_value_low = d_values.astype(jnp.bfloat16).reshape(count, key_cols)
    (
        block_out,
        grad_x,
        first_gain_grad,
        second_shard,
        query_shard,
        key_shard,
        value_shard,
        out_shard,
    ) = finish(
        block_input,
        hidden,
        d_hidden,
        input_first,
        d_query_pre,
        d_key_pre,
        d_value_low,
        attended_parts,
        d_branch,
        w_query,
        w_key,
        w_value,
        mixture_part,
        norm_first,
        grad_gain_second,
        trees,
    )
    factors = clip_limits / jnp.maximum(peaks_all, clip_limits)
    query_scale = jnp.repeat(jnp.sqrt(factors), head_dim)
    key_scale = jnp.repeat(jnp.sqrt(jnp.min(factors.reshape(kv_heads, group), axis=1)), head_dim)
    query_scaled = (w_query.astype(jnp.float32) * query_scale[None, :]).astype(jnp.bfloat16)
    key_scaled = (w_key.astype(jnp.float32) * key_scale[None, :]).astype(jnp.bfloat16)
    return (
        block_out,
        grad_x,
        first_gain_grad,
        second_shard,
        query_shard,
        key_shard,
        value_shard,
        out_shard,
        gate_shard,
        up_shard,
        down_shard,
        factors,
        query_scaled,
        key_scaled,
    )


def solution(mesh):
    placed = (
        P("dp", None),
        P(),
        P(),
        P(None, "tensor"),
        P(None, "tensor"),
        P(None, "tensor"),
        P("tensor", None),
        P(None, None, "tensor"),
        P(None, None, "tensor"),
        P(None, "tensor", None),
        P("dp", None),
        P("dp", None),
        P("dp", None),
        P("tensor"),
        P("dp", None),
    )
    return jax.shard_map(
        local,
        mesh=mesh,
        in_specs=placed,
        out_specs=(
            P("dp", None),
            P(("dp", "tensor"), None),
            P("dp"),
            P("dp"),
            P("dp", "tensor"),
            P("dp", "tensor"),
            P("dp", "tensor"),
            P("dp", "tensor"),
            P("dp", None, "tensor"),
            P("dp", None, "tensor"),
            P("dp", "tensor", None),
            P("tensor"),
            P(None, "tensor"),
            P(None, "tensor"),
        ),
        check_vma=False,
    )
```

```python
import functools

import jax
import jax.numpy as jnp
from jax import lax
from jax.experimental import pallas as pl
from jax.experimental.pallas import tpu as pltpu
from jax.sharding import PartitionSpec as P

HEAD_DIM = 64
EXPERTS = 32
TOPK = 8
TRUNK = 256
SEG = 48
SEGS = 13


epsilon = 1e-06
theta_base = 10000.0
expert_group = 4


def tree_tables(parent_row, count):
    slot_ids = jnp.arange(SEGS, dtype=jnp.int32)
    safe_parent = jnp.maximum(parent_row, 0)
    hot_parent = (safe_parent[:, None] == slot_ids[None, :]).astype(jnp.int32)
    grand_raw = jnp.sum(hot_parent * parent_row[None, :], axis=1)
    grand_parent = jnp.where(parent_row >= 0, grand_raw, -1)
    visible = (
        (slot_ids[:, None] == slot_ids[None, :])
        | (slot_ids[None, :] == parent_row[:, None])
        | (slot_ids[None, :] == grand_parent[:, None])
    )
    depth = (parent_row >= 0).astype(jnp.int32) + (grand_parent >= 0).astype(jnp.int32)
    token_ids = jnp.arange(count, dtype=jnp.int32)
    segment = jnp.where(token_ids < TRUNK, 0, 1 + (token_ids - TRUNK) // SEG)
    local_index = jnp.where(token_ids < TRUNK, token_ids, (token_ids - TRUNK) % SEG)
    seg_match = segment[:, None] == slot_ids[None, :]
    token_depth = jnp.sum(seg_match.astype(jnp.int32) * depth[None, :], axis=1)
    position = jnp.where(segment == 0, token_ids, TRUNK + (token_depth - 1) * SEG + local_index)
    return (
        segment,
        position,
        visible.astype(jnp.float32),
        seg_match.astype(jnp.float32),
        token_ids,
    )


def rotary_tables(position, head_dim):
    half = head_dim // 2
    inverse = theta_base ** (-(jnp.arange(half, dtype=jnp.float32) * 2.0 / head_dim))
    angle = position.astype(jnp.float32)[:, None] * inverse[None, :]
    return (jnp.cos(angle)[:, None, :], jnp.sin(angle)[:, None, :])


def rotate(values, cosine, sine):
    half = values.shape[-1] // 2
    first = values[..., :half]
    second = values[..., half:]
    return jnp.concatenate(
        [first * cosine - second * sine, second * cosine + first * sine], axis=-1
    )


def rotate_back(grads, cosine, sine):
    half = grads.shape[-1] // 2
    first = grads[..., :half]
    second = grads[..., half:]
    return jnp.concatenate(
        [first * cosine + second * sine, second * cosine - first * sine], axis=-1
    )


F32 = jnp.float32
BF = jnp.bfloat16
MESH = pl.DeviceIdType.MESH
CHUNK = 64
PART = 8
BOTH = 16
EG = 4
LAG = 4


def dot(a, b):
    return jnp.dot(a, b, preferred_element_type=F32)


def dot_t(a, b):
    return lax.dot_general(a, b, (((1,), (1,)), ((), ())), preferred_element_type=F32)


def dot_l(a, b):
    return lax.dot_general(a, b, (((0,), (0,)), ((), ())), preferred_element_type=F32)


def expert_core(x, c, g, wcat, wdcat):
    n = len(g)
    f = wdcat.shape[0]
    both = dot(x, wcat)
    gate = both[:, :f]
    up = both[:, f:]
    d_act = dot_t(c, wdcat)
    wide = jnp.concatenate([jnp.broadcast_to(v, (x.shape[0], f // n)) for v in g], axis=1)
    sigma = jax.nn.sigmoid(gate)
    silu = gate * sigma
    act = ((silu * up).astype(BF).astype(F32) * wide).astype(BF)
    d_act = d_act * wide
    d_gate = (d_act * up * (sigma + silu * (1.0 - sigma))).astype(BF)
    d_up = (d_act * silu).astype(BF)
    return act, jnp.concatenate([d_gate, d_up], axis=1)


def experts_kernel(
    pair_ref,
    x_ref,
    c_ref,
    g_ref,
    og_ref,
    wg_ref,
    wu_ref,
    wd_ref,
    hid_ref,
    gain_ref,
    q_ref,
    k_ref,
    v_ref,
    lse_ref,
    bias_ref,
    wo_ref,
    all_ref,
    mix_ref,
    dh_ref,
    g2_ref,
    db_ref,
    dq_ref,
    dk_ref,
    dv_ref,
    gg_ref,
    gu_ref,
    gd_ref,
    wbg,
    wbu,
    wbd,
    wc,
    mixp,
    part,
    half_in,
    quarter_in,
    tot,
    hidq,
    d_att,
    owg,
    owu,
    owd,
    owc,
    acc,
    accd,
    ubuf,
    w_sem,
    ow_sem,
    load_sem,
    own_sem,
    out_sem,
    send_sem,
    recv_sem,
    ssend,
    srecv,
):
    T, D = x_ref.shape
    A = all_ref.shape[0]
    E, _, f = wg_ref.shape
    n_own = owg.shape[0]
    chunks = T // CHUNK
    p = lax.axis_index("dp")
    t = lax.axis_index("tensor")
    a = p // 2
    b = p % 2
    xq = t // 2
    c = t % 2
    y_dev = (a * 2 + 1 - b, t)
    x_dev = (p, (1 - xq) * 2 + c)
    c_dev = (p, xq * 2 + 1 - c)
    z_devs = [(((a + j) % A) * 2 + b, t) for j in range(1, A)]

    barrier = pltpu.get_barrier_semaphore()
    for dev in z_devs + [y_dev, x_dev, c_dev]:
        pl.semaphore_signal(barrier, inc=1, device_id=dev, device_id_type=MESH)
    pl.semaphore_wait(barrier, A + 2)

    def rows1(k):
        return pl.ds(pl.multiple_of(k * CHUNK + (c * 2 + xq) * PART, 8), PART)

    def rows_pair(k):
        return pl.ds(pl.multiple_of(k * CHUNK + c * 2 * PART, 8), 2 * PART)

    def rows2(k):
        return pl.ds(pl.multiple_of(k * CHUNK + 4 * PART + c * BOTH, 8), BOTH)

    def remote(src, dst, stage, k, dev):
        return pltpu.make_async_remote_copy(
            src_ref=src,
            dst_ref=dst,
            send_sem=send_sem.at[stage, k],
            recv_sem=recv_sem.at[stage, k],
            device_id=dev,
            device_id_type=MESH,
        )

    def wait_bytes(ref, sem):
        pltpu.make_async_copy(ref, ref, sem).wait()

    def z_start(k):
        for rows in (rows1(k), rows2(k)):
            for dev in z_devs:
                remote(pair_ref.at[:, rows], all_ref.at[a, b, :, rows], 0, k, dev).start()

    def z_wait(k):
        wait_bytes(all_ref.at[pl.ds(0, A - 1), 0, :, pl.ds(0, PART + BOTH)], recv_sem.at[0, k])

    def y_start(k):
        for rows in (rows1(k), rows2(k)):
            remote(all_ref.at[:, b, :, rows], all_ref.at[:, b, :, rows], 1, k, y_dev).start()

    def y_wait(k):
        wait_bytes(all_ref.at[:, 0, :, pl.ds(0, PART + BOTH)], recv_sem.at[1, k])

    def x_start(k):
        rows = rows1(k)
        remote(all_ref.at[:, :, :, rows], all_ref.at[:, :, :, rows], 2, k, x_dev).start()

    def x_wait(k):
        wait_bytes(all_ref.at[:, :, :, pl.ds(0, PART)], recv_sem.at[2, k])

    def c_start(k):
        for rows in (rows_pair(k), rows2(k)):
            remote(all_ref.at[:, :, :, rows], all_ref.at[:, :, :, rows], 3, k, c_dev).start()

    def c_wait(k):
        wait_bytes(all_ref.at[:, :, :, pl.ds(0, 2 * PART + BOTH)], recv_sem.at[3, k])

    def own_copy(k, i):
        rows = (rows1(k), rows2(k))[i]
        return pltpu.make_async_copy(pair_ref.at[:, rows], all_ref.at[a, b, :, rows], own_sem.at[i, k])

    def pump(s):
        k = s - 3

        @pl.when((k >= 0) & (k < chunks))
        def _():
            x_wait(k)
            c_start(k)

        k2 = s - 2

        @pl.when((k2 >= 0) & (k2 < chunks))
        def _():
            y_wait(k2)
            x_start(k2)

        k1 = s - 1

        @pl.when((k1 >= 0) & (k1 < chunks))
        def _():
            z_wait(k1)
            own_copy(k1, 0).wait()
            own_copy(k1, 1).wait()
            y_start(k1)

        k0 = s + 1

        @pl.when(k0 < chunks)
        def _():
            z_start(k0)

    z_start(0)

    def copies(k, _):
        own_copy(k, 0).start()
        own_copy(k, 1).start()
        return 0

    lax.fori_loop(0, chunks, copies, 0)

    first_own = p * n_own
    own_loads = [
        pltpu.make_async_copy(src.at[pl.ds(first_own, n_own)], dst, ow_sem.at[i])
        for i, (src, dst) in enumerate(((wg_ref, owg), (wu_ref, owu), (wd_ref, owd)))
    ]
    for copy in own_loads:
        copy.start()

    def w_loads(i, slot):
        return [
            pltpu.make_async_copy(src.at[pl.ds(i * EG, EG)], dst.at[slot], w_sem.at[j, slot])
            for j, (src, dst) in enumerate(((wg_ref, wbg), (wu_ref, wbu), (wd_ref, wbd)))
        ]

    for copy in w_loads(0, 0):
        copy.start()
    part[...] = jnp.zeros_like(part)
    mixp[...] = jnp.zeros_like(mixp)
    groups = E // EG
    rows_at = T // 2
    lanes = g_ref.shape[1]

    def group_step(i, _):
        slot = i % 2

        @pl.when(i + 1 < groups)
        def _():
            for copy in w_loads(i + 1, 1 - slot):
                copy.start()

        @pl.when(i % 2 == 0)
        def _():
            pump(i // 2)

        for copy in w_loads(i, slot):
            copy.wait()
        for j in range(EG):
            wc[:, j * f : (j + 1) * f] = wbg[slot, j]
            wc[:, (EG + j) * f : (EG + j + 1) * f] = wbu[slot, j]
        wd = wbd[slot].reshape(EG * f, D)

        def rows_step(r, _):
            rows = pl.ds(pl.multiple_of(r * rows_at, 16), rows_at)
            turned = pltpu.roll(g_ref[rows, :], lanes - i * EG, 1)
            g = [turned[:, j : j + 1] for j in range(EG)]
            act, dgu = expert_core(x_ref[rows, :], c_ref[rows, :], g, wc[...], wd)
            mixp[rows, :] += dot(act, wd)
            part[r] += dot_t(dgu, wc[...]).reshape(2, rows_at // 2, D)
            return 0

        lax.fori_loop(0, 2, rows_step, 0)
        return 0

    lax.fori_loop(0, groups, group_step, 0)

    for copy in own_loads:
        copy.wait()
    for j in range(n_own):
        owc[:, j * f : (j + 1) * f] = owg[j]
        owc[:, (n_own + j) * f : (n_own + j + 1) * f] = owu[j]
    acc[...] = jnp.zeros_like(acc)
    accd[...] = jnp.zeros_like(accd)

    Q = T // 4
    my_rows = pl.ds(pl.multiple_of(t * Q, 16), Q)
    hid_load = pltpu.make_async_copy(hid_ref.at[my_rows], hidq, ow_sem.at[3])
    hid_load.start()

    def summing(src, dst, i, dev):
        return pltpu.make_async_remote_copy(
            src_ref=src,
            dst_ref=dst,
            send_sem=ssend.at[i],
            recv_sem=srecv.at[i],
            device_id=dev,
            device_id_type=MESH,
        )

    sum_copies = [
        summing(part.at[:, 1 - c], half_in, 0, c_dev),
        summing(part.at[1 - xq, c], quarter_in, 1, x_dev),
        summing(dh_ref, tot.at[xq, c], 2, x_dev),
        summing(tot.at[:, c], tot.at[:, c], 3, c_dev),
    ]
    mix_out = pltpu.make_async_copy(mixp, mix_ref, own_sem.at[1, chunks])
    mix_out.start()

    first = groups // 2
    units = A // 4
    group_trees = A // units

    def load(k, u, slot):
        return pltpu.make_async_copy(
            all_ref.at[pl.ds(u * group_trees, group_trees), :, :, pl.ds(pl.multiple_of(k * CHUNK, 8), CHUNK)],
            ubuf.at[slot],
            load_sem.at[slot],
        )

    wdo = owd[...].reshape(n_own * f, D)

    def own_unit(k, u, slot):
        load(k, u, slot).wait()
        size = group_trees * 2 * CHUNK
        xs = ubuf[slot, :, :, 0].reshape(size, D).astype(BF)
        cs = ubuf[slot, :, :, 1].reshape(size, D).astype(BF)
        turned = og_ref[k, u].T
        g = [turned[:, j : j + 1] for j in range(n_own)]
        act, dgu = expert_core(xs, cs, g, owc[...], wdo)
        acc[...] += dot_l(xs, dgu)
        accd[...] += dot_l(act, cs)

    heads, _, hd = q_ref.shape
    group = heads // k_ref.shape[0]
    scale = hd ** (-0.5)
    dk_ref[...] = jnp.zeros_like(dk_ref)
    dv_ref[...] = jnp.zeros_like(dv_ref)

    def attention_back(h):
        g = h // group

        def block(i, _):
            rows = pl.ds(pl.multiple_of(i * Q, 16), Q)
            q = q_ref[h, rows, :]
            da = d_att[h, rows, :]
            lse = pltpu.roll(lse_ref[rows, :], lse_ref.shape[1] - h, 1)[:, 0:1]
            scores = dot_t(q, k_ref[g]) * scale + bias_ref[rows, :].astype(F32)
            probs = jnp.exp(scores - lse)
            d_probs = dot_t(da, v_ref[g])
            row_dot = jnp.sum(probs * d_probs, axis=-1, keepdims=True)
            d_scores = (probs * (d_probs - row_dot) * scale).astype(BF)
            dq_ref[h, rows, :] = dot(d_scores, k_ref[g])
            dk_ref[g] += dot_l(d_scores, q)
            dv_ref[g] += dot_l(probs.astype(BF), da)
            return 0

        lax.fori_loop(0, 4, block, 0)

    def slot_step(s, _):
        pump(s)

        @pl.when(s == first)
        def _():
            sum_copies[0].start()

        @pl.when(s == first + 1)
        def _():
            sum_copies[0].wait()
            part[:, c] += half_in[...]
            sum_copies[1].start()

        @pl.when(s == first + 3)
        def _():
            sum_copies[1].wait()
            hid_load.wait()
            hidden = hidq[...]
            inverse = lax.rsqrt(jnp.mean(hidden * hidden, axis=-1, keepdims=True) + epsilon)
            normal = hidden * inverse
            d_in = part[xq, c] + quarter_in[...]
            g2_ref[...] = jnp.sum(d_in * normal, axis=0, keepdims=True)
            scaled = d_in * gain_ref[...]
            d_hidden = c_ref[my_rows, :].astype(F32) + inverse * (
                scaled - normal * jnp.mean(scaled * normal, axis=-1, keepdims=True)
            )
            dh_ref[...] = d_hidden
            tot[xq, c] = d_hidden
            sum_copies[2].start()

        @pl.when(s == first + 5)
        def _():
            sum_copies[2].wait()
            sum_copies[3].start()

        @pl.when(s == first + 6)
        def _():
            sum_copies[3].wait()
            db_ref[...] = tot[...].reshape(T, D).astype(BF)
            for h in range(heads):
                w = wo_ref[h * hd : (h + 1) * hd, :]
                d_att[h] = dot_t(db_ref[...], w).astype(BF)

        h = s - (first + 6)

        @pl.when((h >= 0) & (h < heads))
        def _():
            attention_back(h)

        k = s - LAG

        @pl.when((k >= 0) & (k < chunks))
        def _():
            c_wait(k)
            load(k, 0, 0).start()
            for u in range(units):
                if u + 1 < units:
                    load(k, u + 1, (u + 1) % 2).start()
                own_unit(k, u, u % 2)

        return 0

    lax.fori_loop(first, chunks + LAG, slot_step, 0)

    outs = []
    for j in range(n_own):
        outs += [
            pltpu.make_async_copy(acc.at[:, pl.ds(j * f, f)], gg_ref.at[j], out_sem.at[0, j]),
            pltpu.make_async_copy(acc.at[:, pl.ds((n_own + j) * f, f)], gu_ref.at[j], out_sem.at[1, j]),
            pltpu.make_async_copy(accd.at[pl.ds(j * f, f)], gd_ref.at[j], out_sem.at[2, j]),
        ]
    for copy in outs:
        copy.start()

    def sends(k, _):
        wait_bytes(all_ref.at[pl.ds(0, A - 1), 0, :, pl.ds(0, PART + BOTH)], send_sem.at[0, k])
        wait_bytes(all_ref.at[:, 0, :, pl.ds(0, PART + BOTH)], send_sem.at[1, k])
        wait_bytes(all_ref.at[:, :, :, pl.ds(0, PART)], send_sem.at[2, k])
        wait_bytes(all_ref.at[:, :, :, pl.ds(0, 2 * PART + BOTH)], send_sem.at[3, k])
        return 0

    lax.fori_loop(0, chunks, sends, 0)
    mix_out.wait()
    for copy in outs:
        copy.wait()


def experts(pair, x, c, dense_gates, own_gates, wg, wu, wd, hidden, gain, q, k, v, lse, bias, wo, trees):
    T, D = x.shape
    E, _, f = wg.shape
    own = E // trees
    chunks = T // CHUNK
    A = trees // 2
    gates_in = jnp.pad(dense_gates, ((0, 0), (0, 128 - E)))
    units = A // 4
    og = jnp.pad(own_gates, ((0, 0), (0, 8 - own), (0, 0)))
    og = og.reshape(units, trees // units, 8, chunks, CHUNK).transpose(3, 0, 2, 1, 4)
    og = og.reshape(chunks, units, 8, trees // units * CHUNK)
    lse = jnp.pad(lse, ((0, 0), (0, 128 - lse.shape[1])))
    vmem = pl.BlockSpec(memory_space=pltpu.VMEM)
    hbm = pl.BlockSpec(memory_space=pl.ANY)
    DMA = pltpu.SemaphoreType.DMA
    slots = 2 if A > 4 else 1
    out = pl.pallas_call(
        experts_kernel,
        in_specs=[hbm] + [vmem] * 4 + [hbm] * 4 + [vmem] * 7,
        out_specs=[hbm] * 2 + [vmem] * 6 + [hbm] * 3,
        out_shape=[
            jax.ShapeDtypeStruct((A, 2, 2, T, D), F32),
            jax.ShapeDtypeStruct((T, D), F32),
            jax.ShapeDtypeStruct((T // 4, D), F32),
            jax.ShapeDtypeStruct((1, D), F32),
            jax.ShapeDtypeStruct((T, D), BF),
            jax.ShapeDtypeStruct(q.shape, F32),
            jax.ShapeDtypeStruct(k.shape, F32),
            jax.ShapeDtypeStruct(v.shape, F32),
            jax.ShapeDtypeStruct((own, D, f), F32),
            jax.ShapeDtypeStruct((own, D, f), F32),
            jax.ShapeDtypeStruct((own, f, D), F32),
        ],
        scratch_shapes=[
            pltpu.VMEM((2, EG, D, f), BF),
            pltpu.VMEM((2, EG, D, f), BF),
            pltpu.VMEM((2, EG, f, D), BF),
            pltpu.VMEM((D, 2 * EG * f), BF),
            pltpu.VMEM((T, D), F32),
            pltpu.VMEM((2, 2, T // 4, D), F32),
            pltpu.VMEM((2, T // 4, D), F32),
            pltpu.VMEM((T // 4, D), F32),
            pltpu.VMEM((2, 2, T // 4, D), F32),
            pltpu.VMEM((T // 4, D), F32),
            pltpu.VMEM(q.shape, BF),
            pltpu.VMEM((own, D, f), BF),
            pltpu.VMEM((own, D, f), BF),
            pltpu.VMEM((own, f, D), BF),
            pltpu.VMEM((D, 2 * own * f), BF),
            pltpu.VMEM((D, 2 * own * f), F32),
            pltpu.VMEM((own * f, D), F32),
            pltpu.VMEM((slots, 4, 2, 2, CHUNK, D), F32),
            DMA((3, 2)),
            DMA((4,)),
            DMA((2,)),
            DMA((2, chunks + 1)),
            DMA((3, own)),
            DMA((4, chunks)),
            DMA((4, chunks)),
            DMA((4,)),
            DMA((4,)),
        ],
        compiler_params=pltpu.CompilerParams(
            collective_id=0, has_side_effects=True, vmem_limit_bytes=60 * 2**20
        ),
    )(pair, x, c, gates_in, og, wg, wu, wd, hidden, gain.reshape(1, D), q, k, v, lse, bias, wo)
    return out[1:]


VMEM = pl.BlockSpec(memory_space=pltpu.VMEM)
HBM = pl.BlockSpec(memory_space=pl.ANY)
DMA = pltpu.SemaphoreType.DMA


def sync_with(devices):
    barrier = pltpu.get_barrier_semaphore()
    for dev in devices:
        pl.semaphore_signal(barrier, inc=1, device_id=dev, device_id_type=MESH)
    pl.semaphore_wait(barrier, len(devices))


def send(src, dst, out_sem, in_sem, dev):
    return pltpu.make_async_remote_copy(
        src_ref=src,
        dst_ref=dst,
        send_sem=out_sem,
        recv_sem=in_sem,
        device_id=dev,
        device_id_type=MESH,
    )


def hidden_kernel(
    att_ref,
    wo_ref,
    x_ref,
    c_ref,
    gain_ref,
    msg_ref,
    hidden_ref,
    xb_ref,
    pair_ref,
    got_ref,
    others,
    ssem,
    rsem,
    msend,
    mrecv,
    csem,
    *,
    trees,
):
    T, D = x_ref.shape
    width = att_ref.shape[1]
    half = T // 2
    p = lax.axis_index("dp")
    t = lax.axis_index("tensor")
    xq = t // 2
    c = t % 2
    x_dev = (p, (1 - xq) * 2 + c)
    c_dev = (p, xq * 2 + 1 - c)
    peers = [((p + j) % trees, t) for j in range(1, trees)]
    sync_with(peers + [x_dev, c_dev])
    rows = [pl.ds(i * half, half) for i in range(2)]
    to_x = [send(att_ref.at[r], others.at[1, r], ssem.at[0, i], rsem.at[0, i], x_dev) for i, r in enumerate(rows)]
    to_c = [send(att_ref.at[r], others.at[0, r], ssem.at[1, i], rsem.at[1, i], c_dev) for i, r in enumerate(rows)]
    on = [send(others.at[1, r], others.at[2, r], ssem.at[2, i], rsem.at[2, i], c_dev) for i, r in enumerate(rows)]
    for copy in to_x + to_c:
        copy.start()
    messages = [
        send(msg_ref.at[dev[0]], got_ref.at[j], msend.at[j], mrecv.at[j], dev) for j, dev in enumerate(peers, 1)
    ]
    for copy in messages:
        copy.start()
    mine = pltpu.make_async_copy(msg_ref.at[p], got_ref.at[0], csem)
    mine.start()
    pair_ref[1] = c_ref[...].astype(F32)

    def proj(block, owner):
        w = wo_ref[pl.ds(pl.multiple_of(owner * width, 128), width), :].astype(BF)
        return dot(block.astype(BF), w)

    for i, r in enumerate(rows):
        hidden_ref[r, :] = x_ref[r, :].astype(F32) + proj(att_ref[r, :], t)
    for i, r in enumerate(rows):
        to_c[i].wait()
        hidden_ref[r, :] += proj(others[0, r, :], xq * 2 + 1 - c)
    for i, r in enumerate(rows):
        to_x[i].wait()
        on[i].start()
        hidden_ref[r, :] += proj(others[1, r, :], (1 - xq) * 2 + c)
    for i, r in enumerate(rows):
        on[i].wait()
        hidden = hidden_ref[r, :] + proj(others[2, r, :], (1 - xq) * 2 + 1 - c)
        hidden_ref[r, :] = hidden
        inverse = lax.rsqrt(jnp.mean(hidden * hidden, axis=-1, keepdims=True) + epsilon)
        low = (hidden * inverse * gain_ref[...]).astype(BF)
        xb_ref[r, :] = low
        pair_ref[0, r, :] = low.astype(F32)
    for copy in messages:
        copy.wait()
    mine.wait()


def hidden_step(att, wo_all, x, c, gain, msgs):
    T, D = x.shape
    trees = msgs.shape[0]
    return pl.pallas_call(
        functools.partial(hidden_kernel, trees=trees),
        in_specs=[VMEM] * 6,
        out_specs=[VMEM] * 4,
        out_shape=[
            jax.ShapeDtypeStruct((T, D), F32),
            jax.ShapeDtypeStruct((T, D), BF),
            jax.ShapeDtypeStruct((2, T, D), F32),
            jax.ShapeDtypeStruct(msgs.shape, F32),
        ],
        scratch_shapes=[
            pltpu.VMEM((3,) + att.shape, F32),
            DMA((3, 2)),
            DMA((3, 2)),
            DMA((trees,)),
            DMA((trees,)),
            DMA(()),
        ],
        compiler_params=pltpu.CompilerParams(
            collective_id=1, has_side_effects=True, vmem_limit_bytes=50 * 2**20
        ),
    )(att, wo_all, x, c, gain.reshape(1, D), msgs)


def finish_kernel(
    x_ref,
    hid_ref,
    dhrows,
    xn_ref,
    dq_ref,
    dk_ref,
    dv_ref,
    att_ref,
    db_ref,
    wq_ref,
    wk_ref,
    wv_ref,
    mix_ref,
    gain_ref,
    gs_ref,
    out_ref,
    gx_ref,
    g1_ref,
    g2_ref,
    gq_ref,
    gk_ref,
    gv_ref,
    go_ref,
    grads,
    ybuf,
    zbuf,
    first,
    mixp,
    tot,
    half_in,
    mhalf_in,
    quarter_in,
    mquarter_in,
    xrows,
    hid,
    gvec,
    gvec_in,
    msg,
    msg_in,
    ysem,
    yrsem,
    zsem,
    zrsem,
    tsem,
    trsem,
    vsem,
    vrsem,
    msem,
    mrsem,
    lsem,
):
    trees, R = msg.shape[0], msg.shape[2]
    A = grads.shape[1]
    T, D = xn_ref.shape
    Q = T // 4
    p = lax.axis_index("dp")
    t = lax.axis_index("tensor")
    a = p // 2
    b = p % 2
    xq = t // 2
    c = t % 2
    y_dev = (a * 2 + 1 - b, t)
    x_dev = (p, (1 - xq) * 2 + c)
    c_dev = (p, xq * 2 + 1 - c)
    f_dev = (p, (1 - xq) * 2 + 1 - c)
    peers = [((p + j) % trees, t) for j in range(1, trees)]
    sync_with(peers + [x_dev, c_dev, f_dev])
    my_rows = pl.ds(pl.multiple_of(t * Q, 16), Q)
    loads = [
        pltpu.make_async_copy(x_ref.at[my_rows], xrows, lsem.at[0]),
        pltpu.make_async_copy(hid_ref, hid, lsem.at[2]),
        pltpu.make_async_copy(mix_ref, mixp, lsem.at[3]),
    ]
    for copy in reversed(loads):
        copy.start()

    W = grads.shape[4]
    to_y = [send(grads.at[i, :, 1 - b], ybuf.at[i], ysem.at[i], yrsem.at[i], y_dev) for i in range(3)]

    def z_sends(i):
        return [
            send(
                grads.at[i, (a + j) % A, b],
                zbuf.at[i, j - 1],
                zsem.at[i, j - 1],
                zrsem.at[i, j - 1],
                (((a + j) % A) * 2 + b, t),
            )
            for j in range(1, A)
        ]

    dqkv = jnp.concatenate([dq_ref[...], dk_ref[...], dv_ref[...]], axis=1)
    out_grad = dot_l(db_ref[...], att_ref[...])
    grads[0] = out_grad.reshape(A, 2, R, W)
    to_y[0].start()
    loads[2].wait()
    core_mix = send(mixp.at[:, 1 - c], mhalf_in, tsem.at[4], trsem.at[4], c_dev)
    core_mix.start()
    grads[1] = dot_l(xn_ref[...], dq_ref[...]).reshape(A, 2, R, W)
    to_y[1].start()
    first_all = dot_t(dq_ref[...], wq_ref[...])
    first_all += dot_t(dk_ref[...], wk_ref[...])
    first_all += dot_t(dv_ref[...], wv_ref[...])
    first[...] = first_all.reshape(2, 2, Q, D)
    core_first = send(first.at[:, 1 - c], half_in, tsem.at[0], trsem.at[0], c_dev)
    core_first.start()
    grads[2] = dot_l(xn_ref[...], dqkv[:, W:]).reshape(A, 2, R, W)
    to_y[2].start()
    core_first.wait()
    first[:, c] += half_in[...]
    x_first = send(first.at[1 - xq, c], quarter_in, tsem.at[1], trsem.at[1], x_dev)
    x_first.start()
    core_mix.wait()
    mixp[:, c] += mhalf_in[...]
    x_mix = send(mixp.at[1 - xq, c], mquarter_in, tsem.at[5], trsem.at[5], x_dev)
    x_mix.start()

    def y_done(i):
        to_y[i].wait()
        grads[i, :, b] += ybuf[i]
        copies = z_sends(i)
        for copy in copies:
            copy.start()
        return copies

    pending = [y_done(0)]
    loads[0].wait()
    x_first.wait()
    d_first = first[xq, c] + quarter_in[...]
    x32 = xrows[...].astype(F32)
    inverse = lax.rsqrt(jnp.mean(x32 * x32, axis=-1, keepdims=True) + epsilon)
    normal = x32 * inverse
    scaled = d_first * gain_ref[...]
    gx_ref[...] = dhrows[...] + inverse * (
        scaled - normal * jnp.mean(scaled * normal, axis=-1, keepdims=True)
    )
    gvec[1:2, :] = gs_ref[...]
    gvec[0:1, :] = jnp.sum(d_first * normal, axis=0, keepdims=True)
    v_sends = [
        send(gvec, gvec_in.at[j], vsem.at[j], vrsem.at[j], dev) for j, dev in enumerate((x_dev, c_dev, f_dev))
    ]
    for copy in v_sends:
        copy.start()
    pending.append(y_done(1))
    x_mix.wait()
    tot[xq, c] = mixp[xq, c] + mquarter_in[...]
    back_x = send(tot.at[xq, c], tot.at[xq, c], tsem.at[6], trsem.at[6], x_dev)
    back_x.start()
    for copy in v_sends:
        copy.wait()
    total = gvec[0:2, :] + gvec_in[0, 0:2, :] + gvec_in[1, 0:2, :] + gvec_in[2, 0:2, :]
    for i in range(trees):
        msg[i, 0:2, :] = total[:, i * R : (i + 1) * R]
    m_sends = [
        send(msg.at[dev[0]], msg_in.at[j], msem.at[j], mrsem.at[j], dev) for j, dev in enumerate(peers)
    ]
    for copy in m_sends:
        copy.start()
    pending.append(y_done(2))

    def z_done(i):
        for copy in pending[i]:
            copy.wait()
        whole = grads[i, a, b]
        for j in range(A - 1):
            whole += zbuf[i, j]
        return whole

    go_ref[...] = z_done(0)
    gq_ref[...] = z_done(1)
    back_x.wait()
    back_c = send(tot.at[:, c], tot.at[:, c], tsem.at[7], trsem.at[7], c_dev)
    back_c.start()
    loads[1].wait()
    for copy in m_sends:
        copy.wait()
    mine = msg[p]
    for j in range(trees - 1):
        mine += msg_in[j]
    g1_ref[...] = mine[0:1]
    g2_ref[...] = mine[1:2]
    back_c.wait()
    out_ref[...] = (hid[...] + tot[...]).astype(BF)
    kv = z_done(2)
    gk_ref[...] = kv[:, : W // 2]
    gv_ref[...] = kv[:, W // 2 :]


def finish(x, hidden, d_hidden, xn, dq, dk, dv, att, db, wq, wk, wv, mix, gain, gain_second, trees):
    T, D = x.shape
    W = wq.shape[1]
    A = trees // 2
    R = D // trees
    Q = T // 4
    S = jax.ShapeDtypeStruct
    outs = pl.pallas_call(
        finish_kernel,
        in_specs=[HBM] * 2 + [VMEM] * 10 + [HBM] + [VMEM] * 2,
        out_specs=[VMEM] * 8,
        out_shape=[
            S((2, 2, Q, D), BF),
            S((Q, D), F32),
            S((1, R), F32),
            S((1, R), F32),
            S((R, W), F32),
            S((R, W // 2), F32),
            S((R, W // 2), F32),
            S((R, W), F32),
        ],
        scratch_shapes=[
            pltpu.VMEM((3, A, 2, R, W), F32),
            pltpu.VMEM((3, A, R, W), F32),
            pltpu.VMEM((3, A - 1, R, W), F32),
            pltpu.VMEM((2, 2, Q, D), F32),
            pltpu.VMEM((2, 2, Q, D), F32),
            pltpu.VMEM((2, 2, Q, D), F32),
            pltpu.VMEM((2, Q, D), F32),
            pltpu.VMEM((2, Q, D), F32),
            pltpu.VMEM((Q, D), F32),
            pltpu.VMEM((Q, D), F32),
            pltpu.VMEM((Q, D), BF),
            pltpu.VMEM((2, 2, Q, D), F32),
            pltpu.VMEM((8, D), F32),
            pltpu.VMEM((3, 8, D), F32),
            pltpu.VMEM((trees, 8, R), F32),
            pltpu.VMEM((trees - 1, 8, R), F32),
            DMA((3,)),
            DMA((3,)),
            DMA((3, A - 1)),
            DMA((3, A - 1)),
            DMA((8,)),
            DMA((8,)),
            DMA((3,)),
            DMA((3,)),
            DMA((trees - 1,)),
            DMA((trees - 1,)),
            DMA((4,)),
        ],
        compiler_params=pltpu.CompilerParams(
            collective_id=2, has_side_effects=True, vmem_limit_bytes=58 * 2**20
        ),
    )(
        x,
        hidden.reshape(2, 2, Q, D),
        d_hidden,
        xn,
        dq,
        dk,
        dv,
        att,
        db,
        wq,
        wk,
        wv,
        mix.reshape(2, 2, Q, D),
        gain.reshape(1, D),
        gain_second.reshape(1, D),
    )
    block_out, grad_x, g1, g2, gq, gk, gv, go = outs
    return block_out.reshape(T, D), grad_x, g1.reshape(R), g2.reshape(R), gq, gk, gv, go


def local(
    block_input,
    norm_first,
    norm_second,
    w_query,
    w_key,
    w_value,
    w_out,
    w_gate,
    w_up,
    w_down,
    routes,
    gates,
    parents,
    clip_limits,
    cotangent,
):
    count, width = block_input.shape
    head_dim = HEAD_DIM
    query_cols = w_query.shape[1]
    key_cols = w_key.shape[1]
    query_heads = query_cols // head_dim
    kv_heads = key_cols // head_dim
    group = query_heads // kv_heads
    scale_factor = head_dim ** (-0.5)
    segment, position, visible, seg_hot, token_ids = tree_tables(parents[0], count)
    reach = jnp.dot(seg_hot, visible)
    cosine, sine = rotary_tables(position, head_dim)

    def mask_for():
        near = jnp.dot(reach, seg_hot.T) > 0.5
        return near & (
            (segment[:, None] != segment[None, :]) | (token_ids[:, None] >= token_ids[None, :])
        )

    wo_all = lax.all_gather(w_out.astype(jnp.float32), "tensor", tiled=True)
    routed = routes[:, :, None] == jnp.arange(EXPERTS, dtype=jnp.int32)[None, None, :]
    dense_gates = jnp.sum(jnp.where(routed, gates[:, :, None], 0.0), axis=1)
    trees = lax.axis_size("dp")
    own = EXPERTS // trees
    x_float = block_input.astype(jnp.float32)
    inverse_first = lax.rsqrt(jnp.mean(x_float * x_float, axis=-1, keepdims=True) + epsilon)
    normal_first = x_float * inverse_first
    input_first = (normal_first * norm_first).astype(jnp.bfloat16)
    query_pre = jnp.dot(input_first, w_query, preferred_element_type=jnp.float32).reshape(
        count, query_heads, head_dim
    )
    key_pre = jnp.dot(input_first, w_key, preferred_element_type=jnp.float32).reshape(
        count, kv_heads, head_dim
    )
    queries = rotate(query_pre, cosine, sine).astype(jnp.bfloat16).reshape(count, query_cols)
    keys_view = rotate(key_pre, cosine, sine).astype(jnp.bfloat16)
    values_view = (
        jnp.dot(input_first, w_value, preferred_element_type=jnp.float32)
        .astype(jnp.bfloat16)
        .reshape(count, kv_heads, head_dim)
    )

    def scores_for():
        query_block = queries.reshape(count, kv_heads, group, head_dim)
        raw = (
            jnp.einsum("qgrd,kgd->grqk", query_block, keys_view, preferred_element_type=jnp.float32)
            * scale_factor
        )
        return (query_block, jnp.where(mask_for()[None, None], raw, -1e30))

    head_peaks = jnp.full((kv_heads, group), -1e30, jnp.float32)
    query_block, scores = scores_for()
    top = jnp.max(scores, axis=-1, keepdims=True)
    expo = jnp.exp(scores - top)
    totals = jnp.sum(expo, axis=-1, keepdims=True)
    probs = (expo / totals).astype(jnp.bfloat16)
    log_norms = [(top + jnp.log(totals))[..., 0]]
    head_peaks = jnp.maximum(head_peaks, jnp.max(top[..., 0], axis=-1))
    attended_block = jnp.einsum(
        "grqk,kgd->qgrd", probs, values_view, preferred_element_type=jnp.float32
    )
    attended_parts = attended_block.astype(jnp.bfloat16).reshape(count, query_cols)
    peaks_local = head_peaks.reshape(query_heads)
    msgs = jnp.concatenate(
        [
            dense_gates.T.reshape(trees, own, count),
            jnp.zeros((trees, 7 - own, count), jnp.float32),
            jnp.broadcast_to(
                jnp.pad(peaks_local, (0, count - query_heads))[None, None, :], (trees, 1, count)
            ),
        ],
        axis=1,
    )
    hidden, input_second, pair, got = hidden_step(
        attended_parts.astype(jnp.float32), wo_all, block_input, cotangent, norm_second, msgs
    )
    peaks_all = jnp.max(got[:, 7, :query_heads], axis=0)
    order = (lax.axis_index("dp") - jnp.arange(trees)) % trees
    hot = (order[:, None] == jnp.arange(trees)[None, :]).astype(jnp.float32)
    own_gates = jnp.sum(hot[:, :, None, None] * got[:, None, :own, :], axis=0)
    def by_head(rows, heads):
        return rows.reshape(count, heads, head_dim).transpose(1, 0, 2)

    bias = jnp.where(mask_for(), 0.0, -1e30).astype(jnp.bfloat16)
    (
        mixture_part,
        d_hidden,
        grad_gain_second,
        d_branch,
        d_queries,
        d_keys,
        d_values,
        gate_shard,
        up_shard,
        down_shard,
    ) = experts(
        pair,
        input_second,
        cotangent,
        dense_gates,
        own_gates,
        w_gate,
        w_up,
        w_down,
        hidden,
        norm_second,
        by_head(queries, query_heads),
        by_head(keys_view, kv_heads),
        by_head(values_view, kv_heads),
        log_norms[0].reshape(query_heads, count).T,
        bias,
        w_out,
        trees,
    )
    d_queries = d_queries.transpose(1, 0, 2)
    d_keys = d_keys.transpose(1, 0, 2)
    d_values = d_values.transpose(1, 0, 2)
    d_query_pre = (
        rotate_back(d_queries, cosine, sine).astype(jnp.bfloat16).reshape(count, query_cols)
    )
    d_key_pre = rotate_back(d_keys, cosine, sine).astype(jnp.bfloat16).reshape(count, key_cols)
    d_value_low = d_values.astype(jnp.bfloat16).reshape(count, key_cols)
    (
        block_out,
        grad_x,
        first_gain_grad,
        second_shard,
        query_shard,
        key_shard,
        value_shard,
        out_shard,
    ) = finish(
        block_input,
        hidden,
        d_hidden,
        input_first,
        d_query_pre,
        d_key_pre,
        d_value_low,
        attended_parts,
        d_branch,
        w_query,
        w_key,
        w_value,
        mixture_part,
        norm_first,
        grad_gain_second,
        trees,
    )
    factors = clip_limits / jnp.maximum(peaks_all, clip_limits)
    query_scale = jnp.repeat(jnp.sqrt(factors), head_dim)
    key_scale = jnp.repeat(jnp.sqrt(jnp.min(factors.reshape(kv_heads, group), axis=1)), head_dim)
    query_scaled = (w_query.astype(jnp.float32) * query_scale[None, :]).astype(jnp.bfloat16)
    key_scaled = (w_key.astype(jnp.float32) * key_scale[None, :]).astype(jnp.bfloat16)
    return (
        block_out,
        grad_x,
        first_gain_grad,
        second_shard,
        query_shard,
        key_shard,
        value_shard,
        out_shard,
        gate_shard,
        up_shard,
        down_shard,
        factors,
        query_scaled,
        key_scaled,
    )


def solution(mesh):
    placed = (
        P("dp", None),
        P(),
        P(),
        P(None, "tensor"),
        P(None, "tensor"),
        P(None, "tensor"),
        P("tensor", None),
        P(None, None, "tensor"),
        P(None, None, "tensor"),
        P(None, "tensor", None),
        P("dp", None),
        P("dp", None),
        P("dp", None),
        P("tensor"),
        P("dp", None),
    )
    return jax.shard_map(
        local,
        mesh=mesh,
        in_specs=placed,
        out_specs=(
            P("dp", None),
            P(("dp", "tensor"), None),
            P("dp"),
            P("dp"),
            P("dp", "tensor"),
            P("dp", "tensor"),
            P("dp", "tensor"),
            P("dp", "tensor"),
            P("dp", None, "tensor"),
            P("dp", None, "tensor"),
            P("dp", "tensor", None),
            P("tensor"),
            P(None, "tensor"),
            P(None, "tensor"),
        ),
        check_vma=False,
    )
```

```python
import functools

import jax
import jax.numpy as jnp
from jax import lax
from jax.experimental import pallas as pl
from jax.experimental.pallas import tpu as pltpu
from jax.sharding import PartitionSpec as P

HEAD_DIM = 64
EXPERTS = 32
TOPK = 8
TRUNK = 256
SEG = 48
SEGS = 13


epsilon = 1e-06
theta_base = 10000.0
expert_group = 4


def tree_tables(parent_row, count):
    slot_ids = jnp.arange(SEGS, dtype=jnp.int32)
    safe_parent = jnp.maximum(parent_row, 0)
    hot_parent = (safe_parent[:, None] == slot_ids[None, :]).astype(jnp.int32)
    grand_raw = jnp.sum(hot_parent * parent_row[None, :], axis=1)
    grand_parent = jnp.where(parent_row >= 0, grand_raw, -1)
    visible = (
        (slot_ids[:, None] == slot_ids[None, :])
        | (slot_ids[None, :] == parent_row[:, None])
        | (slot_ids[None, :] == grand_parent[:, None])
    )
    depth = (parent_row >= 0).astype(jnp.int32) + (grand_parent >= 0).astype(jnp.int32)
    token_ids = jnp.arange(count, dtype=jnp.int32)
    segment = jnp.where(token_ids < TRUNK, 0, 1 + (token_ids - TRUNK) // SEG)
    local_index = jnp.where(token_ids < TRUNK, token_ids, (token_ids - TRUNK) % SEG)
    seg_match = segment[:, None] == slot_ids[None, :]
    token_depth = jnp.sum(seg_match.astype(jnp.int32) * depth[None, :], axis=1)
    position = jnp.where(segment == 0, token_ids, TRUNK + (token_depth - 1) * SEG + local_index)
    return position, visible


def rotary_tables(position, head_dim):
    half = head_dim // 2
    inverse = theta_base ** (-(jnp.arange(half, dtype=jnp.float32) * 2.0 / head_dim))
    angle = position.astype(jnp.float32)[:, None] * inverse[None, :]
    return (jnp.cos(angle)[:, None, :], jnp.sin(angle)[:, None, :])


def rotate_back(grads, cosine, sine):
    half = grads.shape[-1] // 2
    first = grads[..., :half]
    second = grads[..., half:]
    return jnp.concatenate(
        [first * cosine + second * sine, second * cosine - first * sine], axis=-1
    )


F32 = jnp.float32
BF = jnp.bfloat16
MESH = pl.DeviceIdType.MESH
CHUNK = 64
PART = 8
BOTH = 16
EG = 4
LAG = 4
EARLY = 3


def dot(a, b):
    return jnp.dot(a, b, preferred_element_type=F32)


def dot_t(a, b):
    return lax.dot_general(a, b, (((1,), (1,)), ((), ())), preferred_element_type=F32)


def dot_l(a, b):
    return lax.dot_general(a, b, (((0,), (0,)), ((), ())), preferred_element_type=F32)


def expert_core(x, c, g, wcat, wdcat):
    n = len(g)
    f = wdcat.shape[0]
    both = dot(x, wcat)
    gate = both[:, :f]
    up = both[:, f:]
    d_act = dot_t(c, wdcat)
    wide = jnp.concatenate([jnp.broadcast_to(v, (x.shape[0], f // n)) for v in g], axis=1)
    sigma = jax.nn.sigmoid(gate)
    silu = gate * sigma
    act = ((silu * up).astype(BF).astype(F32) * wide).astype(BF)
    d_act = d_act * wide
    d_gate = (d_act * up * (sigma + silu * (1.0 - sigma))).astype(BF)
    d_up = (d_act * silu).astype(BF)
    return act, jnp.concatenate([d_gate, d_up], axis=1)


VMEM = pl.BlockSpec(memory_space=pltpu.VMEM)
HBM = pl.BlockSpec(memory_space=pl.ANY)
DMA = pltpu.SemaphoreType.DMA


def sync_with(devices):
    barrier = pltpu.get_barrier_semaphore()
    for dev in devices:
        pl.semaphore_signal(barrier, inc=1, device_id=dev, device_id_type=MESH)
    pl.semaphore_wait(barrier, len(devices))


def send(src, dst, out_sem, in_sem, dev):
    return pltpu.make_async_remote_copy(
        src_ref=src,
        dst_ref=dst,
        send_sem=out_sem,
        recv_sem=in_sem,
        device_id=dev,
        device_id_type=MESH,
    )


def cut(ref, index):
    return ref.at[index] if index else ref


def gatherer(src, dst, send_sem, recv_sem, own_sem, first, last):
    A = dst.shape[0]
    p = lax.axis_index("dp")
    t = lax.axis_index("tensor")
    a = p // 2
    b = p % 2
    xq = t // 2
    c = t % 2
    y_dev = (a * 2 + 1 - b, t)
    x_dev = (p, (1 - xq) * 2 + c)
    c_dev = (p, xq * 2 + 1 - c)
    z_devs = [(((a + j) % A) * 2 + b, t) for j in range(1, A)]

    def rows1(k):
        return pl.ds(pl.multiple_of(k * CHUNK + (c * 2 + xq) * PART, 8), PART)

    def rows_pair(k):
        return pl.ds(pl.multiple_of(k * CHUNK + c * 2 * PART, 8), 2 * PART)

    def rows2(k):
        return pl.ds(pl.multiple_of(k * CHUNK + 4 * PART + c * BOTH, 8), BOTH)

    def remote(one, two, stage, k, dev):
        return pltpu.make_async_remote_copy(
            src_ref=one,
            dst_ref=two,
            send_sem=send_sem.at[stage, k - first],
            recv_sem=recv_sem.at[stage, k - first],
            device_id=dev,
            device_id_type=MESH,
        )

    sizes = [
        dst.at[pl.ds(0, A - 1), 0, pl.ds(0, PART + BOTH)],
        dst.at[:, 0, pl.ds(0, PART + BOTH)],
        dst.at[:, :, pl.ds(0, PART)],
        dst.at[:, :, pl.ds(0, 2 * PART + BOTH)],
    ]

    def took(stage, k, sem):
        pltpu.make_async_copy(sizes[stage], sizes[stage], sem.at[stage, k - first]).wait()

    def own(k, i):
        rows = (rows1(k), rows2(k))[i]
        return pltpu.make_async_copy(src.at[rows], dst.at[a, b, rows], own_sem.at[i, k - first])

    def start(k):
        for i, rows in enumerate((rows1(k), rows2(k))):
            for dev in z_devs:
                remote(src.at[rows], dst.at[a, b, rows], 0, k, dev).start()
            own(k, i).start()

    def second(k):
        took(0, k, recv_sem)
        for i, rows in enumerate((rows1(k), rows2(k))):
            own(k, i).wait()
            remote(dst.at[:, b, rows], dst.at[:, b, rows], 1, k, y_dev).start()

    def third(k):
        took(1, k, recv_sem)
        rows = rows1(k)
        remote(dst.at[:, :, rows], dst.at[:, :, rows], 2, k, x_dev).start()

    def fourth(k):
        took(2, k, recv_sem)
        for rows in (rows_pair(k), rows2(k)):
            remote(dst.at[:, :, rows], dst.at[:, :, rows], 3, k, c_dev).start()

    def done(k):
        took(3, k, recv_sem)

    def sent(k):
        for stage in range(4):
            took(stage, k, send_sem)

    def pump(s):
        for back, stage in ((3, fourth), (2, third), (1, second), (-1, start)):
            k = first + s - back
            if isinstance(s, int):
                if first <= k < last:
                    stage(k)
            else:

                @pl.when((k >= first) & (k < last))
                def _(k=k, stage=stage):
                    stage(k)

    return start, pump, done, sent, z_devs + [y_dev, x_dev, c_dev]


def experts_kernel(
    xf_ref,
    cf_ref,
    early_ref,
    x_ref,
    c_ref,
    g_ref,
    og_ref,
    wg_ref,
    wu_ref,
    wd_ref,
    hid_ref,
    gain_ref,
    q_ref,
    k_ref,
    v_ref,
    lse_ref,
    bias_ref,
    wo_ref,
    all_x,
    all_c,
    mix_ref,
    dh_ref,
    g2_ref,
    db_ref,
    dq_ref,
    dk_ref,
    dv_ref,
    gg_ref,
    gu_ref,
    gd_ref,
    wbg,
    wbu,
    wbd,
    wc,
    mixp,
    part,
    half_in,
    quarter_in,
    tot,
    hidq,
    d_att,
    owg,
    owu,
    owd,
    owc,
    acc,
    accd,
    ux,
    uc,
    w_sem,
    ow_sem,
    load_sem,
    out_sem,
    x_send,
    x_recv,
    x_own,
    c_send,
    c_recv,
    c_own,
    mix_sem,
    ssend,
    srecv,
):
    T, D = x_ref.shape
    A = all_x.shape[0]
    E, _, f = wg_ref.shape
    n_own = owg.shape[0]
    chunks = T // CHUNK
    p = lax.axis_index("dp")
    t = lax.axis_index("tensor")
    xq = t // 2
    c = t % 2
    x_dev = (p, (1 - xq) * 2 + c)
    c_dev = (p, xq * 2 + 1 - c)
    x_start, x_pump, x_done, x_sent, partners = gatherer(xf_ref, all_x, x_send, x_recv, x_own, 0, chunks)
    c_start, c_pump, c_done, c_sent, _ = gatherer(cf_ref, all_c, c_send, c_recv, c_own, EARLY, chunks)
    sync_with(partners)

    def pump(s):
        x_pump(s)
        c_pump(s)

    x_start(0)
    c_start(EARLY)

    first_own = p * n_own
    own_loads = [
        pltpu.make_async_copy(src.at[pl.ds(first_own, n_own)], dst, ow_sem.at[i])
        for i, (src, dst) in enumerate(((wg_ref, owg), (wu_ref, owu), (wd_ref, owd)))
    ]
    for copy in own_loads:
        copy.start()

    def w_loads(i, slot):
        return [
            pltpu.make_async_copy(src.at[pl.ds(i * EG, EG)], dst.at[slot], w_sem.at[j, slot])
            for j, (src, dst) in enumerate(((wg_ref, wbg), (wu_ref, wbu), (wd_ref, wbd)))
        ]

    for copy in w_loads(0, 0):
        copy.start()
    part[...] = jnp.zeros_like(part)
    mixp[...] = jnp.zeros_like(mixp)
    groups = E // EG
    rows_at = T // 2
    lanes = g_ref.shape[1]

    def group_step(i, _):
        slot = i % 2

        @pl.when(i + 1 < groups)
        def _():
            for copy in w_loads(i + 1, 1 - slot):
                copy.start()

        @pl.when(i % 2 == 0)
        def _():
            pump(i // 2)

        for copy in w_loads(i, slot):
            copy.wait()
        for j in range(EG):
            wc[:, j * f : (j + 1) * f] = wbg[slot, j]
            wc[:, (EG + j) * f : (EG + j + 1) * f] = wbu[slot, j]
        wd = wbd[slot].reshape(EG * f, D)

        def rows_step(r, _):
            rows = pl.ds(pl.multiple_of(r * rows_at, 16), rows_at)
            turned = pltpu.roll(g_ref[rows, :], lanes - i * EG, 1)
            g = [turned[:, j : j + 1] for j in range(EG)]
            act, dgu = expert_core(x_ref[rows, :], c_ref[rows, :], g, wc[...], wd)
            mixp[rows, :] += dot(act, wd)
            part[r] += dot_t(dgu, wc[...]).reshape(2, rows_at // 2, D)
            return 0

        lax.fori_loop(0, 2, rows_step, 0)
        return 0

    lax.fori_loop(0, groups, group_step, 0)

    for copy in own_loads:
        copy.wait()
    for j in range(n_own):
        owc[:, j * f : (j + 1) * f] = owg[j]
        owc[:, (n_own + j) * f : (n_own + j + 1) * f] = owu[j]
    acc[...] = jnp.zeros_like(acc)
    accd[...] = jnp.zeros_like(accd)

    Q = T // 4
    my_rows = pl.ds(pl.multiple_of(t * Q, 16), Q)
    hid_load = pltpu.make_async_copy(hid_ref.at[my_rows], hidq, ow_sem.at[3])
    hid_load.start()

    def summing(src, dst, i, dev):
        return pltpu.make_async_remote_copy(
            src_ref=src,
            dst_ref=dst,
            send_sem=ssend.at[i],
            recv_sem=srecv.at[i],
            device_id=dev,
            device_id_type=MESH,
        )

    sum_copies = [
        summing(part.at[:, 1 - c], half_in, 0, c_dev),
        summing(part.at[1 - xq, c], quarter_in, 1, x_dev),
        summing(dh_ref, tot.at[xq, c], 2, x_dev),
        summing(tot.at[:, c], tot.at[:, c], 3, c_dev),
    ]
    mix_out = pltpu.make_async_copy(mixp, mix_ref, mix_sem)
    mix_out.start()

    first = groups // 2
    units = A // 4
    group_trees = A // units

    def part_of(ref, k, u):
        rows = pl.ds(pl.multiple_of(k * CHUNK, 8), CHUNK)
        return ref.at[pl.ds(u * group_trees, group_trees), :, rows]

    def load_x(k, u, slot):
        return pltpu.make_async_copy(part_of(all_x, k, u), ux.at[slot], load_sem.at[0, slot])

    def load_c(ref, k, u, slot):
        return pltpu.make_async_copy(part_of(ref, k, u), uc.at[slot], load_sem.at[1, slot])

    def load(k, u, slot):
        load_x(k, u, slot).start()

        @pl.when(k < EARLY)
        def _():
            load_c(early_ref, k, u, slot).start()

        @pl.when(k >= EARLY)
        def _():
            load_c(all_c, k, u, slot).start()

    wdo = owd[...].reshape(n_own * f, D)

    def own_unit(k, u, slot):
        load_x(k, u, slot).wait()
        load_c(all_c, k, u, slot).wait()
        size = group_trees * 2 * CHUNK
        xs = ux[slot].reshape(size, D).astype(BF)
        cs = uc[slot].reshape(size, D).astype(BF)
        turned = og_ref[k, u].T
        g = [turned[:, j : j + 1] for j in range(n_own)]
        act, dgu = expert_core(xs, cs, g, owc[...], wdo)
        acc[...] += dot_l(xs, dgu)
        accd[...] += dot_l(act, cs)

    heads, _, hd = q_ref.shape
    group = heads // k_ref.shape[0]
    scale = hd ** (-0.5)
    dk_ref[...] = jnp.zeros_like(dk_ref)
    dv_ref[...] = jnp.zeros_like(dv_ref)

    def attention_back(h):
        g = h // group

        def block(i, _):
            rows = pl.ds(pl.multiple_of(i * Q, 16), Q)
            q = q_ref[h, rows, :]
            da = d_att[h, rows, :]
            lse = pltpu.roll(lse_ref[rows, :], lse_ref.shape[1] - h, 1)[:, 0:1]
            scores = dot_t(q, k_ref[g]) * scale + bias_ref[rows, :].astype(F32)
            probs = jnp.exp(scores - lse)
            d_probs = dot_t(da, v_ref[g])
            row_dot = jnp.sum(probs * d_probs, axis=-1, keepdims=True)
            d_scores = (probs * (d_probs - row_dot) * scale).astype(BF)
            dq_ref[h, rows, :] = dot(d_scores, k_ref[g])
            dk_ref[g] += dot_l(d_scores, q)
            dv_ref[g] += dot_l(probs.astype(BF), da)
            return 0

        lax.fori_loop(0, 4, block, 0)

    def slot_step(s, _):
        pump(s)

        @pl.when(s == first)
        def _():
            sum_copies[0].start()

        @pl.when(s == first + 1)
        def _():
            sum_copies[0].wait()
            part[:, c] += half_in[...]
            sum_copies[1].start()

        @pl.when(s == first + 3)
        def _():
            sum_copies[1].wait()
            hid_load.wait()
            hidden = hidq[...]
            inverse = lax.rsqrt(jnp.mean(hidden * hidden, axis=-1, keepdims=True) + epsilon)
            normal = hidden * inverse
            d_in = part[xq, c] + quarter_in[...]
            g2_ref[...] = jnp.sum(d_in * normal, axis=0, keepdims=True)
            scaled = d_in * gain_ref[...]
            d_hidden = c_ref[my_rows, :].astype(F32) + inverse * (
                scaled - normal * jnp.mean(scaled * normal, axis=-1, keepdims=True)
            )
            dh_ref[...] = d_hidden
            tot[xq, c] = d_hidden
            sum_copies[2].start()

        @pl.when(s == first + 5)
        def _():
            sum_copies[2].wait()
            sum_copies[3].start()

        @pl.when(s == first + 6)
        def _():
            sum_copies[3].wait()
            db_ref[...] = tot[...].reshape(T, D).astype(BF)
            for h in range(heads):
                w = wo_ref[h * hd : (h + 1) * hd, :]
                d_att[h] = dot_t(db_ref[...], w).astype(BF)

        h = s - (first + 6)

        @pl.when((h >= 0) & (h < heads))
        def _():
            attention_back(h)

        k = s - LAG

        @pl.when((k >= 0) & (k < chunks))
        def _():
            x_done(k)

            @pl.when(k >= EARLY)
            def _():
                c_done(k)

            load(k, 0, 0)
            for u in range(units):
                if u + 1 < units:
                    load(k, u + 1, (u + 1) % 2)
                own_unit(k, u, u % 2)

        return 0

    lax.fori_loop(first, chunks + LAG, slot_step, 0)

    outs = []
    for j in range(n_own):
        outs += [
            pltpu.make_async_copy(acc.at[:, pl.ds(j * f, f)], gg_ref.at[j], out_sem.at[0, j]),
            pltpu.make_async_copy(acc.at[:, pl.ds((n_own + j) * f, f)], gu_ref.at[j], out_sem.at[1, j]),
            pltpu.make_async_copy(accd.at[pl.ds(j * f, f)], gd_ref.at[j], out_sem.at[2, j]),
        ]
    for copy in outs:
        copy.start()

    def sends(k, _):
        x_sent(k)

        @pl.when(k >= EARLY)
        def _():
            c_sent(k)

        return 0

    lax.fori_loop(0, chunks, sends, 0)
    mix_out.wait()
    for copy in outs:
        copy.wait()


def experts(xf, cf, early, x, c, dense_gates, own_gates, wg, wu, wd, hidden, gain, q, k, v, lse, bias, wo, trees):
    T, D = x.shape
    E, _, f = wg.shape
    own = E // trees
    chunks = T // CHUNK
    A = trees // 2
    gates_in = jnp.pad(dense_gates, ((0, 0), (0, 128 - E)))
    units = A // 4
    og = jnp.pad(own_gates, ((0, 0), (0, 8 - own), (0, 0)))
    og = og.reshape(units, trees // units, 8, chunks, CHUNK).transpose(3, 0, 2, 1, 4)
    og = og.reshape(chunks, units, 8, trees // units * CHUNK)
    vmem = pl.BlockSpec(memory_space=pltpu.VMEM)
    hbm = pl.BlockSpec(memory_space=pl.ANY)
    DMA = pltpu.SemaphoreType.DMA
    slots = 2 if A > 4 else 1
    out = pl.pallas_call(
        experts_kernel,
        in_specs=[hbm] * 3 + [vmem] * 4 + [hbm] * 4 + [vmem] * 7,
        out_specs=[hbm] * 3 + [vmem] * 6 + [hbm] * 3,
        out_shape=[
            jax.ShapeDtypeStruct((A, 2, T, D), F32),
            jax.ShapeDtypeStruct((A, 2, T, D), F32),
            jax.ShapeDtypeStruct((T, D), F32),
            jax.ShapeDtypeStruct((T // 4, D), F32),
            jax.ShapeDtypeStruct((1, D), F32),
            jax.ShapeDtypeStruct((T, D), BF),
            jax.ShapeDtypeStruct(q.shape, F32),
            jax.ShapeDtypeStruct(k.shape, F32),
            jax.ShapeDtypeStruct(v.shape, F32),
            jax.ShapeDtypeStruct((own, D, f), F32),
            jax.ShapeDtypeStruct((own, D, f), F32),
            jax.ShapeDtypeStruct((own, f, D), F32),
        ],
        scratch_shapes=[
            pltpu.VMEM((2, EG, D, f), BF),
            pltpu.VMEM((2, EG, D, f), BF),
            pltpu.VMEM((2, EG, f, D), BF),
            pltpu.VMEM((D, 2 * EG * f), BF),
            pltpu.VMEM((T, D), F32),
            pltpu.VMEM((2, 2, T // 4, D), F32),
            pltpu.VMEM((2, T // 4, D), F32),
            pltpu.VMEM((T // 4, D), F32),
            pltpu.VMEM((2, 2, T // 4, D), F32),
            pltpu.VMEM((T // 4, D), F32),
            pltpu.VMEM(q.shape, BF),
            pltpu.VMEM((own, D, f), BF),
            pltpu.VMEM((own, D, f), BF),
            pltpu.VMEM((own, f, D), BF),
            pltpu.VMEM((D, 2 * own * f), BF),
            pltpu.VMEM((D, 2 * own * f), F32),
            pltpu.VMEM((own * f, D), F32),
            pltpu.VMEM((slots, 4, 2, CHUNK, D), F32),
            pltpu.VMEM((slots, 4, 2, CHUNK, D), F32),
            DMA((3, 2)),
            DMA((4,)),
            DMA((2, 2)),
            DMA((3, own)),
            DMA((4, chunks)),
            DMA((4, chunks)),
            DMA((2, chunks)),
            DMA((4, chunks - EARLY)),
            DMA((4, chunks - EARLY)),
            DMA((2, chunks - EARLY)),
            DMA(()),
            DMA((4,)),
            DMA((4,)),
        ],
        compiler_params=pltpu.CompilerParams(
            collective_id=0, has_side_effects=True, vmem_limit_bytes=60 * 2**20
        ),
    )(xf, cf, early, x, c, gates_in, og, wg, wu, wd, hidden, gain.reshape(1, D), q, k, v, lse, bias, wo)
    return out[2:]


def front_kernel(
    x_ref,
    c_ref,
    gain1_ref,
    gain2_ref,
    wq_ref,
    wk_ref,
    wv_ref,
    wo_ref,
    visible_ref,
    cos_ref,
    sin_ref,
    gates_ref,
    early_ref,
    hidden_ref,
    xb_ref,
    xf_ref,
    cf_ref,
    xn_ref,
    att_out,
    q_ref,
    k_ref,
    v_ref,
    lse_ref,
    bias_ref,
    got_ref,
    att,
    others,
    wof,
    wr,
    hot,
    msg,
    peaks,
    ssem,
    rsem,
    wsend,
    wrecv,
    msend,
    mrecv,
    msem,
    c_send,
    c_recv,
    c_own,
):
    T, D = x_ref.shape
    trees = got_ref.shape[0]
    heads, _, hd = q_ref.shape
    kvs = k_ref.shape[0]
    group = heads // kvs
    width = heads * hd
    kwidth = kvs * hd
    scale = hd ** (-0.5)
    half = T // 2
    Q = T // 4
    p = lax.axis_index("dp")
    t = lax.axis_index("tensor")
    xq = t // 2
    c = t % 2
    x_dev = (p, (1 - xq) * 2 + c)
    c_dev = (p, xq * 2 + 1 - c)
    peers = [((p + j) % trees, t) for j in range(1, trees)]
    c_start, pump, c_done, c_sent, _ = gatherer(cf_ref, early_ref, c_send, c_recv, c_own, 0, EARLY)
    sync_with(peers + [x_dev, c_dev])
    cf_ref[...] = c_ref[...].astype(F32)
    c_start(0)
    wof[t] = wo_ref[...].astype(F32)
    w_x = send(wof.at[t], wof.at[t], wsend.at[0], wrecv.at[0], x_dev)
    w_c = send(wof.at[t], wof.at[t], wsend.at[1], wrecv.at[1], c_dev)
    far = (1 - xq) * 2 + c
    w_on = send(wof.at[far], wof.at[far], wsend.at[2], wrecv.at[2], c_dev)
    w_x.start()
    w_c.start()
    pump(0)

    row = lax.broadcasted_iota(jnp.int32, (width, width), 0)
    col = lax.broadcasted_iota(jnp.int32, (width, width), 1)
    low = (col % hd) < hd // 2
    turn = jnp.where(low & (row == col + hd // 2), -1.0, jnp.where(~low & (row == col - hd // 2), 1.0, 0.0))
    turn = turn.astype(BF)
    wr[:, :width] = dot(wq_ref[...], turn).astype(BF)
    wr[:, width:] = dot(wk_ref[...], turn[:kwidth, :kwidth]).astype(BF)

    token = lax.broadcasted_iota(jnp.int32, (T, 128), 0)
    seg = lax.broadcasted_iota(jnp.int32, (T, 128), 1)
    begin = jnp.where(seg == 0, 0, TRUNK + (seg - 1) * SEG)
    end = TRUNK + seg * SEG
    hot[...] = ((token >= begin) & (token < end)).astype(F32).astype(BF)

    def project(i, _):
        rows = pl.ds(pl.multiple_of(i * Q, 16), Q)
        x32 = x_ref[rows, :].astype(F32)
        inverse = lax.rsqrt(jnp.mean(x32 * x32, axis=-1, keepdims=True) + epsilon)
        xn = (x32 * inverse * gain1_ref[...]).astype(BF)
        xn_ref[rows, :] = xn
        cosine = cos_ref[rows, :]
        sine = sin_ref[rows, :]
        turned = dot(xn, wr[...])
        query = dot(xn, wq_ref[...])
        query = query * jnp.concatenate([cosine] * (width // 128), axis=1) + turned[:, :width] * jnp.concatenate(
            [sine] * (width // 128), axis=1
        )
        key = dot(xn, wk_ref[...]) * cosine + turned[:, width:] * sine
        value = dot(xn, wv_ref[...])
        for h in range(heads):
            q_ref[h, rows, :] = query[:, h * hd : (h + 1) * hd].astype(BF)
        for g in range(kvs):
            k_ref[g, rows, :] = key[:, g * hd : (g + 1) * hd].astype(BF)
            v_ref[g, rows, :] = value[:, g * hd : (g + 1) * hd].astype(BF)
        mine = hot[rows, :]
        reach = dot(mine, visible_ref[...]).astype(BF)
        near = dot_t(reach, hot[...]) > 0.5
        same = dot_t(mine, hot[...]) > 0.5
        qi = lax.broadcasted_iota(jnp.int32, (Q, T), 0) + i * Q
        kj = lax.broadcasted_iota(jnp.int32, (Q, T), 1)
        seen = near & (~same | (kj <= qi))
        bias_ref[rows, :] = jnp.where(seen, 0.0, -1e30).astype(BF)
        return 0

    lax.fori_loop(0, 4, project, 0)
    pump(1)
    peaks[...] = jnp.full_like(peaks, -1e30)
    lane = lax.broadcasted_iota(jnp.int32, (1, 128), 1)

    def attend(i, _):
        rows = pl.ds(pl.multiple_of(i * Q, 16), Q)
        bias = bias_ref[rows, :].astype(F32)
        for h in range(heads):
            g = h // group
            scores = dot_t(q_ref[h, rows, :], k_ref[g]) * scale + bias
            top = jnp.max(scores, axis=-1, keepdims=True)
            expo = jnp.exp(scores - top)
            total = jnp.sum(expo, axis=-1, keepdims=True)
            probs = (expo / total).astype(BF)
            out = dot(probs, v_ref[g]).astype(BF)
            att_out[rows, h * hd : (h + 1) * hd] = out
            att[rows, h * hd : (h + 1) * hd] = out.astype(F32)
            lse_ref[rows, h : h + 1] = top + jnp.log(total)
            peak = jnp.max(top, axis=0, keepdims=True)
            peaks[0:1, :] = jnp.maximum(peaks[0:1, :], jnp.where(lane == h, peak, -1e30))
        return 0

    rows = [pl.ds(i * half, half) for i in range(2)]
    to_x = [send(att.at[r], others.at[1, r], ssem.at[0, i], rsem.at[0, i], x_dev) for i, r in enumerate(rows)]
    to_c = [send(att.at[r], others.at[0, r], ssem.at[1, i], rsem.at[1, i], c_dev) for i, r in enumerate(rows)]
    on = [send(others.at[1, r], others.at[2, r], ssem.at[2, i], rsem.at[2, i], c_dev) for i, r in enumerate(rows)]
    lax.fori_loop(0, 2, attend, 0)
    to_x[0].start()
    to_c[0].start()
    pump(2)
    lax.fori_loop(2, 4, attend, 0)
    to_x[1].start()
    to_c[1].start()
    pump(3)
    msg[...] = gates_ref[...]
    msg[:, 7:8, 0:128] = jnp.broadcast_to(peaks[0:1, :][None], (trees, 1, 128))
    messages = [
        send(msg.at[dev[0]], got_ref.at[j], msend.at[j], mrecv.at[j], dev) for j, dev in enumerate(peers, 1)
    ]
    for copy in messages:
        copy.start()
    mine = pltpu.make_async_copy(msg.at[p], got_ref.at[0], msem)
    mine.start()
    w_x.wait()
    w_on.start()
    w_c.wait()

    def proj(block, owner):
        return dot(block.astype(BF), wof[owner].astype(BF))

    for i, r in enumerate(rows):
        hidden_ref[r, :] = x_ref[r, :].astype(F32) + proj(att[r, :], t)
    for i, r in enumerate(rows):
        to_c[i].wait()
        hidden_ref[r, :] += proj(others[0, r, :], xq * 2 + 1 - c)
    for i, r in enumerate(rows):
        to_x[i].wait()
        on[i].start()
        hidden_ref[r, :] += proj(others[1, r, :], far)
        pump(4 + i)
    w_on.wait()
    for i, r in enumerate(rows):
        on[i].wait()
        hidden = hidden_ref[r, :] + proj(others[2, r, :], (1 - xq) * 2 + 1 - c)
        hidden_ref[r, :] = hidden
        inverse = lax.rsqrt(jnp.mean(hidden * hidden, axis=-1, keepdims=True) + epsilon)
        low_x = (hidden * inverse * gain2_ref[...]).astype(BF)
        xb_ref[r, :] = low_x
        xf_ref[r, :] = low_x.astype(F32)
    for copy in messages:
        copy.wait()
    mine.wait()
    for s in range(6, EARLY + 3):
        pump(s)
    for k in range(EARLY):
        c_done(k)
        c_sent(k)


def front(x, c, gain1, gain2, wq, wk, wv, wo, visible, cosine, sine, gates_out):
    T, D = x.shape
    trees = gates_out.shape[0]
    A = trees // 2
    heads = wq.shape[1] // HEAD_DIM
    kvs = wk.shape[1] // HEAD_DIM
    width = wq.shape[1]
    S = jax.ShapeDtypeStruct
    V = pltpu.VMEM
    return pl.pallas_call(
        front_kernel,
        in_specs=[VMEM] * 12,
        out_specs=[HBM] + [VMEM] * 12,
        out_shape=[
            S((A, 2, T, D), F32),
            S((T, D), F32),
            S((T, D), BF),
            S((T, D), F32),
            S((T, D), F32),
            S((T, D), BF),
            S((T, width), BF),
            S((heads, T, HEAD_DIM), BF),
            S((kvs, T, HEAD_DIM), BF),
            S((kvs, T, HEAD_DIM), BF),
            S((T, 128), F32),
            S((T, T), BF),
            S(gates_out.shape, F32),
        ],
        scratch_shapes=[
            V((T, width), F32),
            V((3, T, width), F32),
            V((4, width, D), F32),
            V((D, width + wk.shape[1]), BF),
            V((T, 128), BF),
            V(gates_out.shape, F32),
            V((8, 128), F32),
            DMA((3, 2)),
            DMA((3, 2)),
            DMA((3,)),
            DMA((3,)),
            DMA((trees,)),
            DMA((trees,)),
            DMA(()),
            DMA((4, EARLY)),
            DMA((4, EARLY)),
            DMA((2, EARLY)),
        ],
        compiler_params=pltpu.CompilerParams(
            collective_id=1, has_side_effects=True, vmem_limit_bytes=58 * 2**20
        ),
    )(x, c, gain1.reshape(1, D), gain2.reshape(1, D), wq, wk, wv, wo, visible, cosine, sine, gates_out)


def finish_kernel(
    x_ref,
    hid_ref,
    dhrows,
    xn_ref,
    dq_ref,
    dk_ref,
    dv_ref,
    att_ref,
    db_ref,
    wq_ref,
    wk_ref,
    wv_ref,
    mix_ref,
    gain_ref,
    gs_ref,
    out_ref,
    gx_ref,
    g1_ref,
    g2_ref,
    gq_ref,
    gk_ref,
    gv_ref,
    go_ref,
    grads,
    ybuf,
    zbuf,
    first,
    mixp,
    tot,
    half_in,
    mhalf_in,
    quarter_in,
    mquarter_in,
    xrows,
    hid,
    gvec,
    gvec_in,
    msg,
    msg_in,
    ysem,
    yrsem,
    zsem,
    zrsem,
    tsem,
    trsem,
    vsem,
    vrsem,
    msem,
    mrsem,
    lsem,
):
    trees, R = msg.shape[0], msg.shape[2]
    A = grads.shape[1]
    T, D = xn_ref.shape
    Q = T // 4
    p = lax.axis_index("dp")
    t = lax.axis_index("tensor")
    a = p // 2
    b = p % 2
    xq = t // 2
    c = t % 2
    y_dev = (a * 2 + 1 - b, t)
    x_dev = (p, (1 - xq) * 2 + c)
    c_dev = (p, xq * 2 + 1 - c)
    f_dev = (p, (1 - xq) * 2 + 1 - c)
    peers = [((p + j) % trees, t) for j in range(1, trees)]
    sync_with(peers + [x_dev, c_dev, f_dev])
    my_rows = pl.ds(pl.multiple_of(t * Q, 16), Q)
    loads = [
        pltpu.make_async_copy(x_ref.at[my_rows], xrows, lsem.at[0]),
        pltpu.make_async_copy(hid_ref, hid, lsem.at[2]),
        pltpu.make_async_copy(mix_ref, mixp, lsem.at[3]),
    ]
    for copy in reversed(loads):
        copy.start()

    W = grads.shape[4]
    to_y = [send(grads.at[i, :, 1 - b], ybuf.at[i], ysem.at[i], yrsem.at[i], y_dev) for i in range(3)]

    def z_sends(i):
        return [
            send(
                grads.at[i, (a + j) % A, b],
                zbuf.at[i, j - 1],
                zsem.at[i, j - 1],
                zrsem.at[i, j - 1],
                (((a + j) % A) * 2 + b, t),
            )
            for j in range(1, A)
        ]

    dqkv = jnp.concatenate([dq_ref[...], dk_ref[...], dv_ref[...]], axis=1)
    out_grad = dot_l(db_ref[...], att_ref[...])
    grads[0] = out_grad.reshape(A, 2, R, W)
    to_y[0].start()
    loads[2].wait()
    core_mix = send(mixp.at[:, 1 - c], mhalf_in, tsem.at[4], trsem.at[4], c_dev)
    core_mix.start()
    grads[1] = dot_l(xn_ref[...], dq_ref[...]).reshape(A, 2, R, W)
    to_y[1].start()
    first_all = dot_t(dq_ref[...], wq_ref[...])
    first_all += dot_t(dk_ref[...], wk_ref[...])
    first_all += dot_t(dv_ref[...], wv_ref[...])
    first[...] = first_all.reshape(2, 2, Q, D)
    core_first = send(first.at[:, 1 - c], half_in, tsem.at[0], trsem.at[0], c_dev)
    core_first.start()
    grads[2] = dot_l(xn_ref[...], dqkv[:, W:]).reshape(A, 2, R, W)
    to_y[2].start()
    core_first.wait()
    first[:, c] += half_in[...]
    x_first = send(first.at[1 - xq, c], quarter_in, tsem.at[1], trsem.at[1], x_dev)
    x_first.start()
    core_mix.wait()
    mixp[:, c] += mhalf_in[...]
    x_mix = send(mixp.at[1 - xq, c], mquarter_in, tsem.at[5], trsem.at[5], x_dev)
    x_mix.start()

    def y_done(i):
        to_y[i].wait()
        grads[i, :, b] += ybuf[i]
        copies = z_sends(i)
        for copy in copies:
            copy.start()
        return copies

    pending = [y_done(0)]
    loads[0].wait()
    x_first.wait()
    d_first = first[xq, c] + quarter_in[...]
    x32 = xrows[...].astype(F32)
    inverse = lax.rsqrt(jnp.mean(x32 * x32, axis=-1, keepdims=True) + epsilon)
    normal = x32 * inverse
    scaled = d_first * gain_ref[...]
    gx_ref[...] = dhrows[...] + inverse * (
        scaled - normal * jnp.mean(scaled * normal, axis=-1, keepdims=True)
    )
    gvec[1:2, :] = gs_ref[...]
    gvec[0:1, :] = jnp.sum(d_first * normal, axis=0, keepdims=True)
    v_sends = [
        send(gvec, gvec_in.at[j], vsem.at[j], vrsem.at[j], dev) for j, dev in enumerate((x_dev, c_dev, f_dev))
    ]
    for copy in v_sends:
        copy.start()
    pending.append(y_done(1))
    x_mix.wait()
    tot[xq, c] = mixp[xq, c] + mquarter_in[...]
    back_x = send(tot.at[xq, c], tot.at[xq, c], tsem.at[6], trsem.at[6], x_dev)
    back_x.start()
    for copy in v_sends:
        copy.wait()
    total = gvec[0:2, :] + gvec_in[0, 0:2, :] + gvec_in[1, 0:2, :] + gvec_in[2, 0:2, :]
    for i in range(trees):
        msg[i, 0:2, :] = total[:, i * R : (i + 1) * R]
    m_sends = [
        send(msg.at[dev[0]], msg_in.at[j], msem.at[j], mrsem.at[j], dev) for j, dev in enumerate(peers)
    ]
    for copy in m_sends:
        copy.start()
    pending.append(y_done(2))

    def z_done(i):
        for copy in pending[i]:
            copy.wait()
        whole = grads[i, a, b]
        for j in range(A - 1):
            whole += zbuf[i, j]
        return whole

    go_ref[...] = z_done(0)
    gq_ref[...] = z_done(1)
    back_x.wait()
    back_c = send(tot.at[:, c], tot.at[:, c], tsem.at[7], trsem.at[7], c_dev)
    back_c.start()
    loads[1].wait()
    for copy in m_sends:
        copy.wait()
    mine = msg[p]
    for j in range(trees - 1):
        mine += msg_in[j]
    g1_ref[...] = mine[0:1]
    g2_ref[...] = mine[1:2]
    back_c.wait()
    out_ref[...] = (hid[...] + tot[...]).astype(BF)
    kv = z_done(2)
    gk_ref[...] = kv[:, : W // 2]
    gv_ref[...] = kv[:, W // 2 :]


def finish(x, hidden, d_hidden, xn, dq, dk, dv, att, db, wq, wk, wv, mix, gain, gain_second, trees):
    T, D = x.shape
    W = wq.shape[1]
    A = trees // 2
    R = D // trees
    Q = T // 4
    S = jax.ShapeDtypeStruct
    outs = pl.pallas_call(
        finish_kernel,
        in_specs=[HBM] * 2 + [VMEM] * 10 + [HBM] + [VMEM] * 2,
        out_specs=[VMEM] * 8,
        out_shape=[
            S((2, 2, Q, D), BF),
            S((Q, D), F32),
            S((1, R), F32),
            S((1, R), F32),
            S((R, W), F32),
            S((R, W // 2), F32),
            S((R, W // 2), F32),
            S((R, W), F32),
        ],
        scratch_shapes=[
            pltpu.VMEM((3, A, 2, R, W), F32),
            pltpu.VMEM((3, A, R, W), F32),
            pltpu.VMEM((3, A - 1, R, W), F32),
            pltpu.VMEM((2, 2, Q, D), F32),
            pltpu.VMEM((2, 2, Q, D), F32),
            pltpu.VMEM((2, 2, Q, D), F32),
            pltpu.VMEM((2, Q, D), F32),
            pltpu.VMEM((2, Q, D), F32),
            pltpu.VMEM((Q, D), F32),
            pltpu.VMEM((Q, D), F32),
            pltpu.VMEM((Q, D), BF),
            pltpu.VMEM((2, 2, Q, D), F32),
            pltpu.VMEM((8, D), F32),
            pltpu.VMEM((3, 8, D), F32),
            pltpu.VMEM((trees, 8, R), F32),
            pltpu.VMEM((trees - 1, 8, R), F32),
            DMA((3,)),
            DMA((3,)),
            DMA((3, A - 1)),
            DMA((3, A - 1)),
            DMA((8,)),
            DMA((8,)),
            DMA((3,)),
            DMA((3,)),
            DMA((trees - 1,)),
            DMA((trees - 1,)),
            DMA((4,)),
        ],
        compiler_params=pltpu.CompilerParams(
            collective_id=2, has_side_effects=True, vmem_limit_bytes=58 * 2**20
        ),
    )(
        x,
        hidden.reshape(2, 2, Q, D),
        d_hidden,
        xn,
        dq,
        dk,
        dv,
        att,
        db,
        wq,
        wk,
        wv,
        mix.reshape(2, 2, Q, D),
        gain.reshape(1, D),
        gain_second.reshape(1, D),
    )
    block_out, grad_x, g1, g2, gq, gk, gv, go = outs
    return block_out.reshape(T, D), grad_x, g1.reshape(R), g2.reshape(R), gq, gk, gv, go


def local(
    block_input,
    norm_first,
    norm_second,
    w_query,
    w_key,
    w_value,
    w_out,
    w_gate,
    w_up,
    w_down,
    routes,
    gates,
    parents,
    clip_limits,
    cotangent,
):
    count, width = block_input.shape
    head_dim = HEAD_DIM
    query_cols = w_query.shape[1]
    key_cols = w_key.shape[1]
    query_heads = query_cols // head_dim
    kv_heads = key_cols // head_dim
    group = query_heads // kv_heads
    trees = lax.axis_size("dp")
    own = EXPERTS // trees
    position, visible = tree_tables(parents[0], count)
    visible = jnp.pad(visible.astype(jnp.bfloat16), ((0, 128 - SEGS), (0, 128 - SEGS)))
    cosine, sine = rotary_tables(position, head_dim)
    wide_cosine = jnp.tile(cosine[:, 0], (1, 128 * 2 // head_dim))
    wide_sine = jnp.tile(sine[:, 0], (1, 128 * 2 // head_dim))
    routed = routes[:, :, None] == jnp.arange(EXPERTS, dtype=jnp.int32)[None, None, :]
    dense_gates = jnp.sum(jnp.where(routed, gates[:, :, None], 0.0), axis=1)
    gates_out = jnp.pad(dense_gates.T.reshape(trees, own, count), ((0, 0), (0, 8 - own), (0, 0)))
    (
        early,
        hidden,
        input_second,
        x_wide,
        c_wide,
        input_first,
        attended_parts,
        queries,
        keys,
        values,
        log_norms,
        bias,
        got,
    ) = front(
        block_input,
        cotangent,
        norm_first,
        norm_second,
        w_query,
        w_key,
        w_value,
        w_out,
        visible,
        wide_cosine,
        wide_sine,
        gates_out,
    )
    peaks_all = jnp.max(got[:, 7, :query_heads], axis=0)
    order = (lax.axis_index("dp") - jnp.arange(trees)) % trees
    hot = (order[:, None] == jnp.arange(trees)[None, :]).astype(jnp.float32)
    own_gates = jnp.sum(hot[:, :, None, None] * got[:, None, :own, :], axis=0)
    (
        mixture_part,
        d_hidden,
        grad_gain_second,
        d_branch,
        d_queries,
        d_keys,
        d_values,
        gate_shard,
        up_shard,
        down_shard,
    ) = experts(
        x_wide,
        c_wide,
        early,
        input_second,
        cotangent,
        dense_gates,
        own_gates,
        w_gate,
        w_up,
        w_down,
        hidden,
        norm_second,
        queries,
        keys,
        values,
        log_norms,
        bias,
        w_out,
        trees,
    )
    d_queries = d_queries.transpose(1, 0, 2)
    d_keys = d_keys.transpose(1, 0, 2)
    d_values = d_values.transpose(1, 0, 2)
    d_query_pre = (
        rotate_back(d_queries, cosine, sine).astype(jnp.bfloat16).reshape(count, query_cols)
    )
    d_key_pre = rotate_back(d_keys, cosine, sine).astype(jnp.bfloat16).reshape(count, key_cols)
    d_value_low = d_values.astype(jnp.bfloat16).reshape(count, key_cols)
    (
        block_out,
        grad_x,
        first_gain_grad,
        second_shard,
        query_shard,
        key_shard,
        value_shard,
        out_shard,
    ) = finish(
        block_input,
        hidden,
        d_hidden,
        input_first,
        d_query_pre,
        d_key_pre,
        d_value_low,
        attended_parts,
        d_branch,
        w_query,
        w_key,
        w_value,
        mixture_part,
        norm_first,
        grad_gain_second,
        trees,
    )
    factors = clip_limits / jnp.maximum(peaks_all, clip_limits)
    query_scale = jnp.repeat(jnp.sqrt(factors), head_dim)
    key_scale = jnp.repeat(jnp.sqrt(jnp.min(factors.reshape(kv_heads, group), axis=1)), head_dim)
    query_scaled = (w_query.astype(jnp.float32) * query_scale[None, :]).astype(jnp.bfloat16)
    key_scaled = (w_key.astype(jnp.float32) * key_scale[None, :]).astype(jnp.bfloat16)
    return (
        block_out,
        grad_x,
        first_gain_grad,
        second_shard,
        query_shard,
        key_shard,
        value_shard,
        out_shard,
        gate_shard,
        up_shard,
        down_shard,
        factors,
        query_scaled,
        key_scaled,
    )


def solution(mesh):
    placed = (
        P("dp", None),
        P(),
        P(),
        P(None, "tensor"),
        P(None, "tensor"),
        P(None, "tensor"),
        P("tensor", None),
        P(None, None, "tensor"),
        P(None, None, "tensor"),
        P(None, "tensor", None),
        P("dp", None),
        P("dp", None),
        P("dp", None),
        P("tensor"),
        P("dp", None),
    )
    return jax.shard_map(
        local,
        mesh=mesh,
        in_specs=placed,
        out_specs=(
            P("dp", None),
            P(("dp", "tensor"), None),
            P("dp"),
            P("dp"),
            P("dp", "tensor"),
            P("dp", "tensor"),
            P("dp", "tensor"),
            P("dp", "tensor"),
            P("dp", None, "tensor"),
            P("dp", None, "tensor"),
            P("dp", "tensor", None),
            P("tensor"),
            P(None, "tensor"),
            P(None, "tensor"),
        ),
        check_vma=False,
    )
```

```python
import functools

import jax
import jax.numpy as jnp
from jax import lax
from jax.experimental import pallas as pl
from jax.experimental.pallas import tpu as pltpu
from jax.sharding import PartitionSpec as P

HEAD_DIM = 64
EXPERTS = 32
TOPK = 8
TRUNK = 256
SEG = 48
SEGS = 13


epsilon = 1e-06
theta_base = 10000.0
expert_group = 4


def tree_tables(parent_row, count):
    slot_ids = jnp.arange(SEGS, dtype=jnp.int32)
    safe_parent = jnp.maximum(parent_row, 0)
    hot_parent = (safe_parent[:, None] == slot_ids[None, :]).astype(jnp.int32)
    grand_raw = jnp.sum(hot_parent * parent_row[None, :], axis=1)
    grand_parent = jnp.where(parent_row >= 0, grand_raw, -1)
    visible = (
        (slot_ids[:, None] == slot_ids[None, :])
        | (slot_ids[None, :] == parent_row[:, None])
        | (slot_ids[None, :] == grand_parent[:, None])
    )
    depth = (parent_row >= 0).astype(jnp.int32) + (grand_parent >= 0).astype(jnp.int32)
    token_ids = jnp.arange(count, dtype=jnp.int32)
    segment = jnp.where(token_ids < TRUNK, 0, 1 + (token_ids - TRUNK) // SEG)
    local_index = jnp.where(token_ids < TRUNK, token_ids, (token_ids - TRUNK) % SEG)
    seg_match = segment[:, None] == slot_ids[None, :]
    token_depth = jnp.sum(seg_match.astype(jnp.int32) * depth[None, :], axis=1)
    position = jnp.where(segment == 0, token_ids, TRUNK + (token_depth - 1) * SEG + local_index)
    return position, visible


def rotary_tables(position, head_dim):
    half = head_dim // 2
    inverse = theta_base ** (-(jnp.arange(half, dtype=jnp.float32) * 2.0 / head_dim))
    angle = position.astype(jnp.float32)[:, None] * inverse[None, :]
    return (jnp.cos(angle)[:, None, :], jnp.sin(angle)[:, None, :])


F32 = jnp.float32
BF = jnp.bfloat16
MESH = pl.DeviceIdType.MESH
CHUNK = 64
PART = 8
BOTH = 16
EG = 4
LAG = 4
EARLY = 3


def dot(a, b):
    return jnp.dot(a, b, preferred_element_type=F32)


def dot_t(a, b):
    return lax.dot_general(a, b, (((1,), (1,)), ((), ())), preferred_element_type=F32)


def dot_l(a, b):
    return lax.dot_general(a, b, (((0,), (0,)), ((), ())), preferred_element_type=F32)


def expert_core(x, c, g, wcat, wdcat):
    n = len(g)
    f = wdcat.shape[0]
    both = dot(x, wcat)
    gate = both[:, :f]
    up = both[:, f:]
    d_act = dot_t(c, wdcat)
    wide = jnp.concatenate([jnp.broadcast_to(v, (x.shape[0], f // n)) for v in g], axis=1)
    sigma = jax.nn.sigmoid(gate)
    silu = gate * sigma
    act = ((silu * up).astype(BF).astype(F32) * wide).astype(BF)
    d_act = d_act * wide
    d_gate = (d_act * up * (sigma + silu * (1.0 - sigma))).astype(BF)
    d_up = (d_act * silu).astype(BF)
    return act, jnp.concatenate([d_gate, d_up], axis=1)


VMEM = pl.BlockSpec(memory_space=pltpu.VMEM)
HBM = pl.BlockSpec(memory_space=pl.ANY)
DMA = pltpu.SemaphoreType.DMA


def sync_with(devices):
    barrier = pltpu.get_barrier_semaphore()
    for dev in devices:
        pl.semaphore_signal(barrier, inc=1, device_id=dev, device_id_type=MESH)
    pl.semaphore_wait(barrier, len(devices))


def send(src, dst, out_sem, in_sem, dev):
    return pltpu.make_async_remote_copy(
        src_ref=src,
        dst_ref=dst,
        send_sem=out_sem,
        recv_sem=in_sem,
        device_id=dev,
        device_id_type=MESH,
    )


def gatherer(src, dst, send_sem, recv_sem, own_sem, first, last, part, both):
    A = dst.shape[0]
    p = lax.axis_index("dp")
    t = lax.axis_index("tensor")
    a = p // 2
    b = p % 2
    xq = t // 2
    c = t % 2
    y_dev = (a * 2 + 1 - b, t)
    x_dev = (p, (1 - xq) * 2 + c)
    c_dev = (p, xq * 2 + 1 - c)
    z_devs = [(((a + j) % A) * 2 + b, t) for j in range(1, A)]

    def rows1(k):
        return pl.ds(pl.multiple_of(k * CHUNK + (c * 2 + xq) * part, 8), part)

    def rows_pair(k):
        return pl.ds(pl.multiple_of(k * CHUNK + c * 2 * part, 8), 2 * part)

    def rows2(k):
        return pl.ds(pl.multiple_of(k * CHUNK + 4 * part + c * both, 8), both)

    def mine(k):
        return [rows1(k), rows2(k)] if part and both else [rows1(k)] if part else [rows2(k)]

    def of_core(k):
        return [rows_pair(k), rows2(k)] if part and both else [rows_pair(k)] if part else [rows2(k)]

    def remote(one, two, stage, k, dev):
        return pltpu.make_async_remote_copy(
            src_ref=one,
            dst_ref=two,
            send_sem=send_sem.at[stage, k - first],
            recv_sem=recv_sem.at[stage, k - first],
            device_id=dev,
            device_id_type=MESH,
        )

    sizes = [
        dst.at[pl.ds(0, A - 1), 0, pl.ds(0, part + both)],
        dst.at[:, 0, pl.ds(0, part + both)],
        dst.at[:, :, pl.ds(0, max(part, 8))],
        dst.at[:, :, pl.ds(0, 2 * part + both)],
    ]

    def took(stage, k, sem):
        pltpu.make_async_copy(sizes[stage], sizes[stage], sem.at[stage, k - first]).wait()

    def own(k, i):
        rows = mine(k)[i]
        return pltpu.make_async_copy(src.at[rows], dst.at[a, b, rows], own_sem.at[i, k - first])

    def start(k):
        for i, rows in enumerate(mine(k)):
            for dev in z_devs:
                remote(src.at[rows], dst.at[a, b, rows], 0, k, dev).start()
            own(k, i).start()

    def second(k):
        took(0, k, recv_sem)
        for i, rows in enumerate(mine(k)):
            own(k, i).wait()
            remote(dst.at[:, b, rows], dst.at[:, b, rows], 1, k, y_dev).start()

    def to_core(k):
        for rows in of_core(k):
            remote(dst.at[:, :, rows], dst.at[:, :, rows], 3, k, c_dev).start()

    def third(k):
        took(1, k, recv_sem)
        if not part:
            to_core(k)
            return
        rows = rows1(k)
        remote(dst.at[:, :, rows], dst.at[:, :, rows], 2, k, x_dev).start()

    def fourth(k):
        took(2, k, recv_sem)
        to_core(k)

    def done(k):
        took(3, k, recv_sem)

    def sent(k):
        for stage in (0, 1, 2, 3) if part else (0, 1, 3):
            took(stage, k, send_sem)

    def pump(s):
        steps = ((3, fourth), (2, third), (1, second), (-1, start))
        for back, stage in steps if part else steps[1:]:
            k = first + s - back
            if isinstance(s, int):
                if first <= k < last:
                    stage(k)
            else:

                @pl.when((k >= first) & (k < last))
                def _(k=k, stage=stage):
                    stage(k)

    return start, second, third, done, sent, pump, z_devs + [y_dev, x_dev, c_dev]


def experts_kernel(
    xf_ref,
    cf_ref,
    early_ref,
    xb_ref,
    c_ref,
    g_ref,
    og_ref,
    wg_ref,
    wu_ref,
    wd_ref,
    hid_ref,
    xin_ref,
    xn_ref,
    gain1_ref,
    gain_ref,
    q_ref,
    k_ref,
    v_ref,
    lse_ref,
    bias_ref,
    wo_ref,
    att_ref,
    wq_ref,
    wk_ref,
    wv_ref,
    cos_ref,
    sin_ref,
    all_x,
    all_c,
    mix_ref,
    gx_ref,
    gg_ref,
    gu_ref,
    gd_ref,
    g1_ref,
    g2_ref,
    go_ref,
    gq_ref,
    gk_ref,
    gv_ref,
    x_ref,
    wc,
    wbd,
    mixp,
    part,
    half_in,
    quarter_in,
    tot,
    mhalf_in,
    mquarter_in,
    grads,
    ybuf,
    zbuf,
    hidq,
    d_att,
    dq_ref,
    dk_ref,
    dv_ref,
    dqkv,
    xrows,
    gvec,
    gvec_in,
    msg,
    msg_in,
    acc,
    accd,
    ux,
    uc,
    w_sem,
    in_sem,
    load_sem,
    out_sem,
    x_send,
    x_recv,
    x_own,
    c_send,
    c_recv,
    c_own,
    mix_sem,
    ysem,
    yrsem,
    zsem,
    zrsem,
    vsem,
    vrsem,
    msem,
    mrsem,
    ssend,
    srecv,
):
    T, D = x_ref.shape
    A = all_x.shape[0]
    E, _, f = wg_ref.shape
    n_own = gg_ref.shape[0]
    chunks = T // CHUNK
    p = lax.axis_index("dp")
    t = lax.axis_index("tensor")
    xq = t // 2
    c = t % 2
    x_dev = (p, (1 - xq) * 2 + c)
    c_dev = (p, xq * 2 + 1 - c)
    f_dev = (p, (1 - xq) * 2 + 1 - c)
    trees = msg.shape[0]
    peers = [((p + j) % trees, t) for j in range(1, trees)]
    x_start, _, _, x_done, x_sent, x_pump, _ = gatherer(
        xf_ref, all_x, x_send, x_recv, x_own, 0, chunks, PART, BOTH
    )
    c_start, _, _, c_done, c_sent, c_pump, _ = gatherer(
        cf_ref, all_c, c_send, c_recv, c_own, EARLY, chunks, PART, BOTH
    )
    xb_load = pltpu.make_async_copy(xb_ref, x_ref, in_sem.at[0])
    xb_load.start()
    sync_with(peers + [x_dev, c_dev, f_dev])

    def pump(s):
        x_pump(s)
        c_pump(s)

    x_start(0)
    c_start(EARLY)

    first_own = p * n_own
    own_loads = [pltpu.make_async_copy(wd_ref.at[pl.ds(first_own, n_own)], wbd.at[0, pl.ds(0, n_own)], w_sem.at[0, 0])]
    for i in range(n_own):
        for h, src in enumerate((wg_ref, wu_ref)):
            dst = wc.at[0, :, pl.ds((h * n_own + i) * f, f)]
            own_loads.append(pltpu.make_async_copy(src.at[first_own + i], dst, w_sem.at[1 + 2 * i + h, 0]))

    def w_loads(i, slot):
        loads = [pltpu.make_async_copy(wd_ref.at[pl.ds(i * EG, EG)], wbd.at[slot], w_sem.at[0, slot])]
        for j in range(EG):
            for h, src in enumerate((wg_ref, wu_ref)):
                dst = wc.at[slot, :, pl.ds((h * EG + j) * f, f)]
                loads.append(pltpu.make_async_copy(src.at[i * EG + j], dst, w_sem.at[1 + 2 * j + h, slot]))
        return loads

    for copy in w_loads(0, 0):
        copy.start()
    part[...] = jnp.zeros_like(part)
    xb_load.wait()
    mixp[...] = jnp.zeros_like(mixp)
    groups = E // EG
    rows_at = T // 2
    lanes = g_ref.shape[1]

    def group_step(i, _):
        slot = i % 2

        @pl.when(i + 1 < groups)
        def _():
            for copy in w_loads(i + 1, 1 - slot):
                copy.start()

        @pl.when(i + 1 == groups)
        def _():
            for copy in own_loads:
                copy.start()

        @pl.when(i % 2 == 0)
        def _():
            pump(i // 2)

        for copy in w_loads(i, slot):
            copy.wait()
        wd = wbd[slot].reshape(EG * f, D)

        def rows_step(r, _):
            rows = pl.ds(pl.multiple_of(r * rows_at, 16), rows_at)
            turned = pltpu.roll(g_ref[rows, :], lanes - i * EG, 1)
            g = [turned[:, j : j + 1] for j in range(EG)]
            act, dgu = expert_core(x_ref[rows, :], c_ref[rows, :], g, wc[slot], wd)
            mixp[r] += dot(act, wd).reshape(2, rows_at // 2, D)
            part[r] += dot_t(dgu, wc[slot]).reshape(2, rows_at // 2, D)
            return 0

        lax.fori_loop(0, 2, rows_step, 0)
        return 0

    lax.fori_loop(0, groups, group_step, 0)

    acc[...] = jnp.zeros_like(acc)
    accd[...] = jnp.zeros_like(accd)

    Q = T // 4
    my_rows = pl.ds(pl.multiple_of(t * Q, 16), Q)
    hid_load = pltpu.make_async_copy(hid_ref.at[my_rows], hidq, in_sem.at[1])
    hid_load.start()
    xrows_load = pltpu.make_async_copy(xin_ref.at[my_rows], xrows, in_sem.at[2])
    xrows_load.start()
    xn_load = pltpu.make_async_copy(xn_ref, x_ref, in_sem.at[3])

    def summing(src, dst, i, dev):
        return pltpu.make_async_remote_copy(
            src_ref=src,
            dst_ref=dst,
            send_sem=ssend.at[i],
            recv_sem=srecv.at[i],
            device_id=dev,
            device_id_type=MESH,
        )

    sum_copies = [
        summing(part.at[:, 1 - c], half_in, 0, c_dev),
        summing(part.at[1 - xq, c], quarter_in, 1, x_dev),
        summing(tot.at[xq, c], tot.at[xq, c], 2, x_dev),
        summing(tot.at[:, c], tot.at[:, c], 3, c_dev),
    ]
    mix_copies = [
        summing(mixp.at[:, 1 - c], mhalf_in, 4, c_dev),
        summing(mixp.at[1 - xq, c], mquarter_in, 5, x_dev),
        summing(mixp.at[xq, c], mix_ref.at[xq, c], 6, x_dev),
        summing(mix_ref.at[:, c], mix_ref.at[:, c], 7, c_dev),
    ]
    mix_own = pltpu.make_async_copy(mixp.at[xq, c], mix_ref.at[xq, c], mix_sem)
    core_first = summing(part.at[:, 1 - c], half_in, 8, c_dev)
    x_first = summing(part.at[1 - xq, c], quarter_in, 9, x_dev)
    gx_out = pltpu.make_async_copy(hidq, gx_ref, in_sem.at[4])

    a = p // 2
    b = p % 2
    pieces, _, _, R, W = grads.shape
    y_dev = (a * 2 + 1 - b, t)

    def to_y(i):
        return send(grads.at[i, :, 1 - b], ybuf.at[i], ysem.at[i], yrsem.at[i], y_dev)

    def to_z(i):
        return [
            send(
                grads.at[i, (a + j) % A, b],
                zbuf.at[i, j - 1],
                zsem.at[i, j - 1],
                zrsem.at[i, j - 1],
                (((a + j) % A) * 2 + b, t),
            )
            for j in range(1, A)
        ]

    def y_done(i):
        to_y(i).wait()
        grads[i, :, b] += ybuf[i]
        for copy in to_z(i):
            copy.start()

    def z_done(i):
        for copy in to_z(i):
            copy.wait()
        whole = grads[i, a, b]
        for j in range(A - 1):
            whole += zbuf[i, j]
        return whole

    v_sends = [
        send(gvec, gvec_in.at[j], vsem.at[j], vrsem.at[j], dev) for j, dev in enumerate((x_dev, c_dev, f_dev))
    ]
    m_sends = [
        send(msg.at[dev[0]], msg_in.at[j], msem.at[j], mrsem.at[j], dev) for j, dev in enumerate(peers)
    ]

    first = groups // 2
    units = A // 4
    group_trees = A // units

    def part_of(ref, k, u):
        rows = pl.ds(pl.multiple_of(k * CHUNK, 8), CHUNK)
        return ref.at[pl.ds(u * group_trees, group_trees), :, rows]

    def load_x(k, u, slot):
        return pltpu.make_async_copy(part_of(all_x, k, u), ux.at[slot], load_sem.at[0, slot])

    def load_c(ref, k, u, slot):
        return pltpu.make_async_copy(part_of(ref, k, u), uc.at[slot], load_sem.at[1, slot])

    def load(k, u, slot):
        load_x(k, u, slot).start()

        @pl.when(k < EARLY)
        def _():
            load_c(early_ref, k, u, slot).start()

        @pl.when(k >= EARLY)
        def _():
            load_c(all_c, k, u, slot).start()

    for copy in own_loads:
        copy.wait()
    wdo = wbd[0, 0:n_own].reshape(n_own * f, D)

    def own_unit(k, u, slot):
        load_x(k, u, slot).wait()
        load_c(all_c, k, u, slot).wait()
        size = group_trees * 2 * CHUNK
        xs = ux[slot].reshape(size, D).astype(BF)
        cs = uc[slot].reshape(size, D).astype(BF)
        turned = og_ref[k, u].T
        g = [turned[:, j : j + 1] for j in range(n_own)]
        act, dgu = expert_core(xs, cs, g, wc[0, :, 0 : 2 * n_own * f], wdo)
        acc[...] += dot_l(xs, dgu)
        accd[...] += dot_l(act, cs)

    heads, _, hd = q_ref.shape
    group = heads // k_ref.shape[0]
    scale = hd ** (-0.5)
    dk_ref[...] = jnp.zeros_like(dk_ref)
    dv_ref[...] = jnp.zeros_like(dv_ref)

    def attention_back(h):
        g = h // group

        def block(i, _):
            rows = pl.ds(pl.multiple_of(i * Q, 16), Q)
            q = q_ref[h, rows, :]
            da = d_att[h, rows, :]
            lse = pltpu.roll(lse_ref[rows, :], lse_ref.shape[1] - h, 1)[:, 0:1]
            scores = dot_t(q, k_ref[g]) * scale + bias_ref[rows, :].astype(F32)
            probs = jnp.exp(scores - lse)
            d_probs = dot_t(da, v_ref[g])
            row_dot = jnp.sum(probs * d_probs, axis=-1, keepdims=True)
            d_scores = (probs * (d_probs - row_dot) * scale).astype(BF)
            dq_ref[h, rows, :] = dot(d_scores, k_ref[g])
            dk_ref[g] += dot_l(d_scores, q)
            dv_ref[g] += dot_l(probs.astype(BF), da)
            return 0

        lax.fori_loop(0, 4, block, 0)

    width = heads * hd
    kwidth = k_ref.shape[0] * hd

    def finish_start():
        lane = lax.broadcasted_iota(jnp.int32, (T, hd), 1)
        cosine = cos_ref[:, 0:hd]
        sine = jnp.where(lane < hd // 2, sin_ref[:, 0:hd], -sin_ref[:, 0:hd])

        def turned_back(d):
            swapped = jnp.concatenate([d[:, hd // 2 :], d[:, : hd // 2]], axis=1)
            return (d * cosine + swapped * sine).astype(BF)

        for h in range(heads):
            dqkv[:, h * hd : (h + 1) * hd] = turned_back(dq_ref[h])
        for g in range(k_ref.shape[0]):
            at = width + g * hd
            dqkv[:, at : at + hd] = turned_back(dk_ref[g])
            at = width + kwidth + g * hd
            dqkv[:, at : at + hd] = dv_ref[g].astype(BF)
        xn_load.wait()
        for i in range(width // W, pieces):
            at = (i - width // W) * W
            grads[i] = dot_l(x_ref[...], dqkv[:, at : at + W]).reshape(A, 2, R, W)
            to_y(i).start()
        for r in range(2):
            rows = pl.ds(r * 2 * Q, 2 * Q)
            total = dot_t(dqkv[rows, 0:width], wq_ref[...])
            total += dot_t(dqkv[rows, width : width + kwidth], wk_ref[...])
            total += dot_t(dqkv[rows, width + kwidth :], wv_ref[...])
            part[r] = total.reshape(2, Q, D)
        core_first.start()

    def slot_step(s, _):
        pump(s)

        @pl.when(s == first)
        def _():
            sum_copies[0].start()

        @pl.when(s == first + 1)
        def _():
            sum_copies[0].wait()
            part[:, c] += half_in[...]
            sum_copies[1].start()

        @pl.when(s == first + 3)
        def _():
            sum_copies[1].wait()
            hid_load.wait()
            hidden = hidq[...]
            inverse = lax.rsqrt(jnp.mean(hidden * hidden, axis=-1, keepdims=True) + epsilon)
            normal = hidden * inverse
            d_in = part[xq, c] + quarter_in[...]
            gvec[1:2, :] = jnp.sum(d_in * normal, axis=0, keepdims=True)
            scaled = d_in * gain_ref[...]
            tot[xq, c] = c_ref[my_rows, :].astype(F32) + inverse * (
                scaled - normal * jnp.mean(scaled * normal, axis=-1, keepdims=True)
            )
            sum_copies[2].start()

        @pl.when(s == first + 5)
        def _():
            sum_copies[2].wait()
            sum_copies[3].start()
            mix_copies[0].start()

        @pl.when(s == first + 6)
        def _():
            sum_copies[3].wait()
            x_ref[...] = tot[...].reshape(T, D).astype(BF)
            for h in range(heads):
                w = wo_ref[h * hd : (h + 1) * hd, :]
                d_att[h] = dot_t(x_ref[...], w).astype(BF)
            for i in range(width // W):
                out_grad = dot_l(x_ref[...], att_ref[:, i * W : (i + 1) * W])
                grads[i] = out_grad.reshape(A, 2, R, W)
                to_y(i).start()
            xn_load.start()
            mix_copies[0].wait()
            mixp[:, c] += mhalf_in[...]
            mix_copies[1].start()

        @pl.when(s == first + 7)
        def _():
            for i in range(width // W):
                y_done(i)

        @pl.when(s == first + 8)
        def _():
            finish_start()
            mix_copies[1].wait()
            mixp[xq, c] += mquarter_in[...]
            mix_own.start()
            mix_copies[2].start()

        @pl.when(s == first + 9)
        def _():
            core_first.wait()
            part[:, c] += half_in[...]
            x_first.start()
            for i in range(width // W, 2 * (width // W)):
                y_done(i)

        @pl.when(s == first + 10)
        def _():
            for i in range(2 * (width // W), pieces):
                y_done(i)
            xrows_load.wait()
            x32 = xrows[...].astype(F32)
            inverse = lax.rsqrt(jnp.mean(x32 * x32, axis=-1, keepdims=True) + epsilon)
            normal = x32 * inverse
            x_first.wait()
            d_first = part[xq, c] + quarter_in[...]
            gvec[0:1, :] = jnp.sum(d_first * normal, axis=0, keepdims=True)
            for copy in v_sends:
                copy.start()
            scaled = d_first * gain1_ref[...]
            hidq[...] = tot[xq, c] + inverse * (
                scaled - normal * jnp.mean(scaled * normal, axis=-1, keepdims=True)
            )
            gx_out.start()

        @pl.when(s == first + 11)
        def _():
            mix_own.wait()
            mix_copies[2].wait()
            mix_copies[3].start()
            for copy in v_sends:
                copy.wait()
            total = gvec[0:2, :] + gvec_in[0, 0:2, :] + gvec_in[1, 0:2, :] + gvec_in[2, 0:2, :]
            for i in range(trees):
                msg[i, 0:2, :] = total[:, i * R : (i + 1) * R]
            for copy in m_sends:
                copy.start()

        @pl.when((s == first + 6) | (s == first + 7))
        def _():
            attention_back((s - first - 6) * 2)
            attention_back((s - first - 6) * 2 + 1)

        k = s - LAG

        @pl.when((k >= 0) & (k < chunks))
        def _():
            x_done(k)

            @pl.when(k >= EARLY)
            def _():
                c_done(k)

            load(k, 0, 0)
            for u in range(units):
                if u + 1 < units:
                    load(k, u + 1, (u + 1) % 2)
                own_unit(k, u, u % 2)

        return 0

    lax.fori_loop(first, chunks + LAG, slot_step, 0)

    outs = []
    for j in range(n_own):
        outs += [
            pltpu.make_async_copy(acc.at[:, pl.ds(j * f, f)], gg_ref.at[j], out_sem.at[0, j]),
            pltpu.make_async_copy(acc.at[:, pl.ds((n_own + j) * f, f)], gu_ref.at[j], out_sem.at[1, j]),
            pltpu.make_async_copy(accd.at[pl.ds(j * f, f)], gd_ref.at[j], out_sem.at[2, j]),
        ]
    for copy in outs:
        copy.start()
    per = width // W
    for i in range(per):
        go_ref[:, i * W : (i + 1) * W] = z_done(i)
        gq_ref[:, i * W : (i + 1) * W] = z_done(per + i)
    gk_ref[...] = z_done(2 * per)
    gv_ref[...] = z_done(2 * per + 1)
    for copy in m_sends:
        copy.wait()
    mine = msg[p]
    for j in range(trees - 1):
        mine += msg_in[j]
    g1_ref[...] = mine[0:1]
    g2_ref[...] = mine[1:2]
    gx_out.wait()
    mix_copies[3].wait()

    def sends(k, _):
        x_sent(k)

        @pl.when(k >= EARLY)
        def _():
            c_sent(k)

        return 0

    lax.fori_loop(0, chunks, sends, 0)
    for copy in outs:
        copy.wait()


def experts(
    xf, cf, early, xb, c, dense_gates, own_gates, wg, wu, wd, hidden, x, xn, gain1, gain2, q, k, v, lse, bias,
    wo, att, wq, wk, wv, cosine, sine, trees,
):
    T, D = c.shape
    E, _, f = wg.shape
    own = E // trees
    chunks = T // CHUNK
    A = trees // 2
    Q = T // 4
    R = D // trees
    W = wk.shape[1]
    pieces = 2 * (wq.shape[1] // W) + 2
    gates_in = jnp.pad(dense_gates, ((0, 0), (0, 128 - E)))
    units = A // 4
    og = own_gates.reshape(units, trees // units, 8, chunks, CHUNK).transpose(3, 0, 2, 1, 4)
    og = og.reshape(chunks, units, 8, trees // units * CHUNK)
    slots = 2 if A > 4 else 1
    S = jax.ShapeDtypeStruct
    V = pltpu.VMEM
    out = pl.pallas_call(
        experts_kernel,
        in_specs=[HBM] * 4 + [VMEM] * 3 + [HBM] * 6 + [VMEM] * 14,
        out_specs=[HBM] * 7 + [VMEM] * 6,
        out_shape=[
            S((A, 2, T, D), F32),
            S((A, 2, T, D), F32),
            S((2, 2, Q, D), F32),
            S((Q, D), F32),
            S((own, D, f), F32),
            S((own, D, f), F32),
            S((own, f, D), F32),
            S((1, R), F32),
            S((1, R), F32),
            S((R, wq.shape[1]), F32),
            S((R, wq.shape[1]), F32),
            S((R, W), F32),
            S((R, W), F32),
        ],
        scratch_shapes=[
            V((T, D), BF),
            V((2, D, 2 * EG * f), BF),
            V((2, EG, f, D), BF),
            V((2, 2, Q, D), F32),
            V((2, 2, Q, D), F32),
            V((2, Q, D), F32),
            V((Q, D), F32),
            V((2, 2, Q, D), F32),
            V((2, Q, D), F32),
            V((Q, D), F32),
            V((pieces, A, 2, R, W), F32),
            V((pieces, A, R, W), F32),
            V((pieces, A - 1, R, W), F32),
            V((Q, D), F32),
            V(q.shape, BF),
            V(q.shape, F32),
            V(k.shape, F32),
            V(v.shape, F32),
            V((T, wq.shape[1] + 2 * W), BF),
            V((Q, D), BF),
            V((8, D), F32),
            V((3, 8, D), F32),
            V((trees, 8, R), F32),
            V((trees - 1, 8, R), F32),
            V((D, 2 * own * f), F32),
            V((own * f, D), F32),
            V((slots, 4, 2, CHUNK, D), F32),
            V((slots, 4, 2, CHUNK, D), F32),
            DMA((1 + 2 * EG, 2)),
            DMA((5,)),
            DMA((2, 2)),
            DMA((3, own)),
            DMA((4, chunks)),
            DMA((4, chunks)),
            DMA((2, chunks)),
            DMA((4, chunks - EARLY)),
            DMA((4, chunks - EARLY)),
            DMA((2, chunks - EARLY)),
            DMA(()),
            DMA((pieces,)),
            DMA((pieces,)),
            DMA((pieces, A - 1)),
            DMA((pieces, A - 1)),
            DMA((3,)),
            DMA((3,)),
            DMA((trees - 1,)),
            DMA((trees - 1,)),
            DMA((10,)),
            DMA((10,)),
        ],
        compiler_params=pltpu.CompilerParams(
            collective_id=0, has_side_effects=True, vmem_limit_bytes=62 * 2**20
        ),
    )(
        xf, cf, early, xb, c, gates_in, og, wg, wu, wd, hidden, x, xn, gain1.reshape(1, D), gain2.reshape(1, D),
        q, k, v, lse, bias, wo, att, wq, wk, wv, cosine, sine,
    )
    return out[2:]


def front_kernel(
    x_ref,
    c_ref,
    gain1_ref,
    gain2_ref,
    wq_ref,
    wk_ref,
    wv_ref,
    wo_ref,
    visible_ref,
    cos_ref,
    sin_ref,
    gates_ref,
    early_ref,
    hidden_ref,
    xb_ref,
    xf_ref,
    cf_ref,
    xn_ref,
    att_out,
    q_ref,
    k_ref,
    v_ref,
    lse_ref,
    bias_ref,
    got_ref,
    att,
    others,
    wof,
    wr,
    hot,
    msg,
    peaks,
    ssem,
    rsem,
    wsend,
    wrecv,
    msend,
    mrecv,
    msem,
    c_send,
    c_recv,
    c_own,
):
    T, D = x_ref.shape
    trees = got_ref.shape[0]
    heads, _, hd = q_ref.shape
    kvs = k_ref.shape[0]
    group = heads // kvs
    width = heads * hd
    kwidth = kvs * hd
    scale = hd ** (-0.5)
    half = T // 2
    Q = T // 4
    p = lax.axis_index("dp")
    t = lax.axis_index("tensor")
    xq = t // 2
    c = t % 2
    x_dev = (p, (1 - xq) * 2 + c)
    c_dev = (p, xq * 2 + 1 - c)
    peers = [((p + j) % trees, t) for j in range(1, trees)]
    c_start, c_second, c_third, c_done, c_sent = gatherer(
        cf_ref, early_ref, c_send, c_recv, c_own, 0, EARLY, 0, CHUNK // 2
    )[:5]
    sync_with(peers + [x_dev, c_dev])
    cf_ref[...] = c_ref[...].astype(F32)
    c_start(0)
    wof[t] = wo_ref[...].astype(F32)
    w_x = send(wof.at[t], wof.at[t], wsend.at[0], wrecv.at[0], x_dev)
    w_c = send(wof.at[t], wof.at[t], wsend.at[1], wrecv.at[1], c_dev)
    far = (1 - xq) * 2 + c
    w_on = send(wof.at[far], wof.at[far], wsend.at[2], wrecv.at[2], c_dev)
    w_x.start()
    w_c.start()

    row = lax.broadcasted_iota(jnp.int32, (width, width), 0)
    col = lax.broadcasted_iota(jnp.int32, (width, width), 1)
    low = (col % hd) < hd // 2
    turn = jnp.where(low & (row == col + hd // 2), -1.0, jnp.where(~low & (row == col - hd // 2), 1.0, 0.0))
    turn = turn.astype(BF)
    wr[:, :width] = dot(wq_ref[...], turn).astype(BF)
    wr[:, width:] = dot(wk_ref[...], turn[:kwidth, :kwidth]).astype(BF)

    token = lax.broadcasted_iota(jnp.int32, (T, 128), 0)
    seg = lax.broadcasted_iota(jnp.int32, (T, 128), 1)
    begin = jnp.where(seg == 0, 0, TRUNK + (seg - 1) * SEG)
    end = TRUNK + seg * SEG
    hot[...] = ((token >= begin) & (token < end)).astype(F32).astype(BF)

    def project(i, _):
        rows = pl.ds(pl.multiple_of(i * Q, 16), Q)
        x32 = x_ref[rows, :].astype(F32)
        inverse = lax.rsqrt(jnp.mean(x32 * x32, axis=-1, keepdims=True) + epsilon)
        xn = (x32 * inverse * gain1_ref[...]).astype(BF)
        xn_ref[rows, :] = xn
        cosine = cos_ref[rows, :]
        sine = sin_ref[rows, :]
        turned = dot(xn, wr[...])
        query = dot(xn, wq_ref[...])
        query = query * jnp.concatenate([cosine] * (width // 128), axis=1) + turned[:, :width] * jnp.concatenate(
            [sine] * (width // 128), axis=1
        )
        key = dot(xn, wk_ref[...]) * cosine + turned[:, width:] * sine
        value = dot(xn, wv_ref[...])
        for h in range(heads):
            q_ref[h, rows, :] = query[:, h * hd : (h + 1) * hd].astype(BF)
        for g in range(kvs):
            k_ref[g, rows, :] = key[:, g * hd : (g + 1) * hd].astype(BF)
            v_ref[g, rows, :] = value[:, g * hd : (g + 1) * hd].astype(BF)
        mine = hot[rows, :]
        reach = dot(mine, visible_ref[...]).astype(BF)
        near = dot_t(reach, hot[...]) > 0.5
        same = dot_t(mine, hot[...]) > 0.5
        qi = lax.broadcasted_iota(jnp.int32, (Q, T), 0) + i * Q
        kj = lax.broadcasted_iota(jnp.int32, (Q, T), 1)
        seen = near & (~same | (kj <= qi))
        bias_ref[rows, :] = jnp.where(seen, 0.0, -1e30).astype(BF)
        return 0

    lax.fori_loop(0, 4, project, 0)
    c_start(1)
    peaks[...] = jnp.full_like(peaks, -1e30)
    lane = lax.broadcasted_iota(jnp.int32, (1, 128), 1)

    def attend(i, _):
        rows = pl.ds(pl.multiple_of(i * Q, 16), Q)
        bias = bias_ref[rows, :].astype(F32)
        for h in range(heads):
            g = h // group
            scores = dot_t(q_ref[h, rows, :], k_ref[g]) * scale + bias
            top = jnp.max(scores, axis=-1, keepdims=True)
            expo = jnp.exp(scores - top)
            total = jnp.sum(expo, axis=-1, keepdims=True)
            probs = (expo / total).astype(BF)
            out = dot(probs, v_ref[g]).astype(BF)
            att_out[rows, h * hd : (h + 1) * hd] = out
            att[rows, h * hd : (h + 1) * hd] = out.astype(F32)
            lse_ref[rows, h : h + 1] = top + jnp.log(total)
            peak = jnp.max(top, axis=0, keepdims=True)
            peaks[0:1, :] = jnp.maximum(peaks[0:1, :], jnp.where(lane == h, peak, -1e30))
        return 0

    rows = [pl.ds(i * half, half) for i in range(2)]
    to_x = [send(att.at[r], others.at[1, r], ssem.at[0, i], rsem.at[0, i], x_dev) for i, r in enumerate(rows)]
    to_c = [send(att.at[r], others.at[0, r], ssem.at[1, i], rsem.at[1, i], c_dev) for i, r in enumerate(rows)]
    on = [send(others.at[1, r], others.at[2, r], ssem.at[2, i], rsem.at[2, i], c_dev) for i, r in enumerate(rows)]
    lax.fori_loop(0, 2, attend, 0)
    to_x[0].start()
    to_c[0].start()
    c_second(0)
    c_start(2)
    lax.fori_loop(2, 4, attend, 0)
    to_x[1].start()
    to_c[1].start()
    c_second(1)
    c_third(0)
    msg[...] = gates_ref[...]
    msg[:, 7:8, 0:128] = jnp.broadcast_to(peaks[0:1, :][None], (trees, 1, 128))
    messages = [
        send(msg.at[dev[0]], got_ref.at[j], msend.at[j], mrecv.at[j], dev) for j, dev in enumerate(peers, 1)
    ]
    for copy in messages:
        copy.start()
    mine = pltpu.make_async_copy(msg.at[p], got_ref.at[0], msem)
    mine.start()
    w_x.wait()
    w_on.start()
    w_c.wait()

    def proj(block, owner):
        return dot(block.astype(BF), wof[owner].astype(BF))

    for i, r in enumerate(rows):
        hidden_ref[r, :] = x_ref[r, :].astype(F32) + proj(att[r, :], t)
    for i, r in enumerate(rows):
        to_c[i].wait()
        hidden_ref[r, :] += proj(others[0, r, :], xq * 2 + 1 - c)
    for i, r in enumerate(rows):
        to_x[i].wait()
        on[i].start()
        hidden_ref[r, :] += proj(others[1, r, :], far)
    c_second(2)
    c_third(1)
    w_on.wait()
    for i, r in enumerate(rows):
        on[i].wait()
        hidden = hidden_ref[r, :] + proj(others[2, r, :], (1 - xq) * 2 + 1 - c)
        hidden_ref[r, :] = hidden
        inverse = lax.rsqrt(jnp.mean(hidden * hidden, axis=-1, keepdims=True) + epsilon)
        low_x = (hidden * inverse * gain2_ref[...]).astype(BF)
        xb_ref[r, :] = low_x
        xf_ref[r, :] = low_x.astype(F32)
    for copy in messages:
        copy.wait()
    mine.wait()
    c_third(2)
    for k in range(EARLY):
        c_done(k)
        c_sent(k)


def front(x, c, gain1, gain2, wq, wk, wv, wo, visible, cosine, sine, gates_out):
    T, D = x.shape
    trees = gates_out.shape[0]
    A = trees // 2
    heads = wq.shape[1] // HEAD_DIM
    kvs = wk.shape[1] // HEAD_DIM
    width = wq.shape[1]
    S = jax.ShapeDtypeStruct
    V = pltpu.VMEM
    return pl.pallas_call(
        front_kernel,
        in_specs=[VMEM] * 12,
        out_specs=[HBM] + [VMEM] * 12,
        out_shape=[
            S((A, 2, T, D), F32),
            S((T, D), F32),
            S((T, D), BF),
            S((T, D), F32),
            S((T, D), F32),
            S((T, D), BF),
            S((T, width), BF),
            S((heads, T, HEAD_DIM), BF),
            S((kvs, T, HEAD_DIM), BF),
            S((kvs, T, HEAD_DIM), BF),
            S((T, 128), F32),
            S((T, T), BF),
            S(gates_out.shape, F32),
        ],
        scratch_shapes=[
            V((T, width), F32),
            V((3, T, width), F32),
            V((4, width, D), F32),
            V((D, width + wk.shape[1]), BF),
            V((T, 128), BF),
            V(gates_out.shape, F32),
            V((8, 128), F32),
            DMA((3, 2)),
            DMA((3, 2)),
            DMA((3,)),
            DMA((3,)),
            DMA((trees,)),
            DMA((trees,)),
            DMA(()),
            DMA((4, EARLY)),
            DMA((4, EARLY)),
            DMA((2, EARLY)),
        ],
        compiler_params=pltpu.CompilerParams(
            collective_id=1, has_side_effects=True, vmem_limit_bytes=58 * 2**20
        ),
    )(x, c, gain1.reshape(1, D), gain2.reshape(1, D), wq, wk, wv, wo, visible, cosine, sine, gates_out)


def local(
    block_input,
    norm_first,
    norm_second,
    w_query,
    w_key,
    w_value,
    w_out,
    w_gate,
    w_up,
    w_down,
    routes,
    gates,
    parents,
    clip_limits,
    cotangent,
):
    count, width = block_input.shape
    head_dim = HEAD_DIM
    query_cols = w_query.shape[1]
    key_cols = w_key.shape[1]
    query_heads = query_cols // head_dim
    kv_heads = key_cols // head_dim
    group = query_heads // kv_heads
    trees = lax.axis_size("dp")
    own = EXPERTS // trees
    position, visible = tree_tables(parents[0], count)
    visible = jnp.pad(visible.astype(jnp.bfloat16), ((0, 128 - SEGS), (0, 128 - SEGS)))
    cosine, sine = rotary_tables(position, head_dim)
    wide_cosine = jnp.tile(cosine[:, 0], (1, 128 * 2 // head_dim))
    wide_sine = jnp.tile(sine[:, 0], (1, 128 * 2 // head_dim))
    routed = routes[:, :, None] == jnp.arange(EXPERTS, dtype=jnp.int32)[None, None, :]
    dense_gates = jnp.sum(jnp.where(routed, gates[:, :, None], 0.0), axis=1)
    gates_out = jnp.pad(dense_gates.T.reshape(trees, own, count), ((0, 0), (0, 8 - own), (0, 0)))
    (
        early,
        hidden,
        input_second,
        x_wide,
        c_wide,
        input_first,
        attended_parts,
        queries,
        keys,
        values,
        log_norms,
        bias,
        got,
    ) = front(
        block_input,
        cotangent,
        norm_first,
        norm_second,
        w_query,
        w_key,
        w_value,
        w_out,
        visible,
        wide_cosine,
        wide_sine,
        gates_out,
    )
    peaks_all = jnp.max(got[:, 7, :query_heads], axis=0)
    order = (lax.axis_index("dp") - jnp.arange(trees)) % trees
    hot = (order[:, None] == jnp.arange(trees)[None, :]).astype(jnp.float32)
    own_gates = jnp.sum(hot[:, :, None, None] * got[:, None], axis=0)
    (
        mixture,
        grad_x,
        gate_shard,
        up_shard,
        down_shard,
        first_gain_grad,
        second_shard,
        out_shard,
        query_shard,
        key_shard,
        value_shard,
    ) = experts(
        x_wide,
        c_wide,
        early,
        input_second,
        cotangent,
        dense_gates,
        own_gates,
        w_gate,
        w_up,
        w_down,
        hidden,
        block_input,
        input_first,
        norm_first,
        norm_second,
        queries,
        keys,
        values,
        log_norms,
        bias,
        w_out,
        attended_parts,
        w_query,
        w_key,
        w_value,
        wide_cosine,
        wide_sine,
        trees,
    )
    first_gain_grad = first_gain_grad.reshape(width // trees)
    second_shard = second_shard.reshape(width // trees)
    block_out = (hidden + mixture.reshape(count, width)).astype(jnp.bfloat16)
    factors = clip_limits / jnp.maximum(peaks_all, clip_limits)
    query_scale = jnp.repeat(jnp.sqrt(factors), head_dim)
    key_scale = jnp.repeat(jnp.sqrt(jnp.min(factors.reshape(kv_heads, group), axis=1)), head_dim)
    query_scaled = (w_query.astype(jnp.float32) * query_scale[None, :]).astype(jnp.bfloat16)
    key_scaled = (w_key.astype(jnp.float32) * key_scale[None, :]).astype(jnp.bfloat16)
    return (
        block_out,
        grad_x,
        first_gain_grad,
        second_shard,
        query_shard,
        key_shard,
        value_shard,
        out_shard,
        gate_shard,
        up_shard,
        down_shard,
        factors,
        query_scaled,
        key_scaled,
    )


def solution(mesh):
    placed = (
        P("dp", None),
        P(),
        P(),
        P(None, "tensor"),
        P(None, "tensor"),
        P(None, "tensor"),
        P("tensor", None),
        P(None, None, "tensor"),
        P(None, None, "tensor"),
        P(None, "tensor", None),
        P("dp", None),
        P("dp", None),
        P("dp", None),
        P("tensor"),
        P("dp", None),
    )
    return jax.shard_map(
        local,
        mesh=mesh,
        in_specs=placed,
        out_specs=(
            P("dp", None),
            P(("dp", "tensor"), None),
            P("dp"),
            P("dp"),
            P("dp", "tensor"),
            P("dp", "tensor"),
            P("dp", "tensor"),
            P("dp", "tensor"),
            P("dp", None, "tensor"),
            P("dp", None, "tensor"),
            P("dp", "tensor", None),
            P("tensor"),
            P(None, "tensor"),
            P(None, "tensor"),
        ),
        check_vma=False,
    )
```

```python
import functools

import jax
import jax.numpy as jnp
from jax import lax
from jax.experimental import pallas as pl
from jax.experimental.pallas import tpu as pltpu
from jax.sharding import PartitionSpec as P

HEAD_DIM = 64
EXPERTS = 32
TOPK = 8
TRUNK = 256
SEG = 48
SEGS = 13


epsilon = 1e-06
theta_base = 10000.0
expert_group = 4


def tree_tables(parent_row, count):
    slot_ids = jnp.arange(SEGS, dtype=jnp.int32)
    safe_parent = jnp.maximum(parent_row, 0)
    hot_parent = (safe_parent[:, None] == slot_ids[None, :]).astype(jnp.int32)
    grand_raw = jnp.sum(hot_parent * parent_row[None, :], axis=1)
    grand_parent = jnp.where(parent_row >= 0, grand_raw, -1)
    visible = (
        (slot_ids[:, None] == slot_ids[None, :])
        | (slot_ids[None, :] == parent_row[:, None])
        | (slot_ids[None, :] == grand_parent[:, None])
    )
    depth = (parent_row >= 0).astype(jnp.int32) + (grand_parent >= 0).astype(jnp.int32)
    token_ids = jnp.arange(count, dtype=jnp.int32)
    segment = jnp.where(token_ids < TRUNK, 0, 1 + (token_ids - TRUNK) // SEG)
    local_index = jnp.where(token_ids < TRUNK, token_ids, (token_ids - TRUNK) % SEG)
    seg_match = segment[:, None] == slot_ids[None, :]
    token_depth = jnp.sum(seg_match.astype(jnp.int32) * depth[None, :], axis=1)
    position = jnp.where(segment == 0, token_ids, TRUNK + (token_depth - 1) * SEG + local_index)
    return position, visible


def rotary_tables(position, head_dim):
    half = head_dim // 2
    inverse = theta_base ** (-(jnp.arange(half, dtype=jnp.float32) * 2.0 / head_dim))
    angle = position.astype(jnp.float32)[:, None] * inverse[None, :]
    return (jnp.cos(angle)[:, None, :], jnp.sin(angle)[:, None, :])


F32 = jnp.float32
BF = jnp.bfloat16
MESH = pl.DeviceIdType.MESH
CHUNK = 64
PART = 8
BOTH = 16
EG = 4
LAG = 4
EARLY = 2
EARLY_ROWS = (0, 32)


def dot(a, b):
    return jnp.dot(a, b, preferred_element_type=F32)


def dot_t(a, b):
    return lax.dot_general(a, b, (((1,), (1,)), ((), ())), preferred_element_type=F32)


def dot_l(a, b):
    return lax.dot_general(a, b, (((0,), (0,)), ((), ())), preferred_element_type=F32)


def expert_core(x, c, g, wcat, wdcat):
    n = len(g)
    f = wdcat.shape[0]
    both = dot(x, wcat)
    gate = both[:, :f]
    up = both[:, f:]
    d_act = dot_t(c, wdcat)
    wide = jnp.concatenate([jnp.broadcast_to(v, (x.shape[0], f // n)) for v in g], axis=1)
    sigma = jax.nn.sigmoid(gate)
    silu = gate * sigma
    act = ((silu * up).astype(BF).astype(F32) * wide).astype(BF)
    d_act = d_act * wide
    d_gate = (d_act * up * (sigma + silu * (1.0 - sigma))).astype(BF)
    d_up = (d_act * silu).astype(BF)
    return act, jnp.concatenate([d_gate, d_up], axis=1)


VMEM = pl.BlockSpec(memory_space=pltpu.VMEM)
HBM = pl.BlockSpec(memory_space=pl.ANY)
DMA = pltpu.SemaphoreType.DMA


def sync_with(devices):
    barrier = pltpu.get_barrier_semaphore()
    for dev in devices:
        pl.semaphore_signal(barrier, inc=1, device_id=dev, device_id_type=MESH)
    pl.semaphore_wait(barrier, len(devices))


def send(src, dst, out_sem, in_sem, dev):
    return pltpu.make_async_remote_copy(
        src_ref=src,
        dst_ref=dst,
        send_sem=out_sem,
        recv_sem=in_sem,
        device_id=dev,
        device_id_type=MESH,
    )


def gatherer(src, dst, send_sem, recv_sem, own_sem, first, last, part, both):
    A = dst.shape[0]
    p = lax.axis_index("dp")
    t = lax.axis_index("tensor")
    a = p // 2
    b = p % 2
    xq = t // 2
    c = t % 2
    y_dev = (a * 2 + 1 - b, t)
    x_dev = (p, (1 - xq) * 2 + c)
    c_dev = (p, xq * 2 + 1 - c)
    z_devs = [(((a + j) % A) * 2 + b, t) for j in range(1, A)]

    def rows1(k):
        return pl.ds(pl.multiple_of(k * CHUNK + (c * 2 + xq) * part, 8), part)

    def rows_pair(k):
        return pl.ds(pl.multiple_of(k * CHUNK + c * 2 * part, 8), 2 * part)

    def rows2(k):
        return pl.ds(pl.multiple_of(k * CHUNK + 4 * part + c * both, 8), both)

    def mine(k):
        return [rows1(k), rows2(k)] if part and both else [rows1(k)] if part else [rows2(k)]

    def of_core(k):
        return [rows_pair(k), rows2(k)] if part and both else [rows_pair(k)] if part else [rows2(k)]

    def remote(one, two, stage, k, dev):
        return pltpu.make_async_remote_copy(
            src_ref=one,
            dst_ref=two,
            send_sem=send_sem.at[stage, k - first],
            recv_sem=recv_sem.at[stage, k - first],
            device_id=dev,
            device_id_type=MESH,
        )

    sizes = [
        dst.at[pl.ds(0, A - 1), 0, pl.ds(0, part + both)],
        dst.at[:, 0, pl.ds(0, part + both)],
        dst.at[:, :, pl.ds(0, max(part, 8))],
        dst.at[:, :, pl.ds(0, 2 * part + both)],
    ]

    def took(stage, k, sem):
        pltpu.make_async_copy(sizes[stage], sizes[stage], sem.at[stage, k - first]).wait()

    def own(k, i):
        rows = mine(k)[i]
        return pltpu.make_async_copy(src.at[rows], dst.at[a, b, rows], own_sem.at[i, k - first])

    def start(k):
        for i, rows in enumerate(mine(k)):
            for dev in z_devs:
                remote(src.at[rows], dst.at[a, b, rows], 0, k, dev).start()
            own(k, i).start()

    def second(k):
        took(0, k, recv_sem)
        for i, rows in enumerate(mine(k)):
            own(k, i).wait()
            remote(dst.at[:, b, rows], dst.at[:, b, rows], 1, k, y_dev).start()

    def to_core(k):
        for rows in of_core(k):
            remote(dst.at[:, :, rows], dst.at[:, :, rows], 3, k, c_dev).start()

    def third(k):
        took(1, k, recv_sem)
        if not part:
            to_core(k)
            return
        rows = rows1(k)
        remote(dst.at[:, :, rows], dst.at[:, :, rows], 2, k, x_dev).start()

    def fourth(k):
        took(2, k, recv_sem)
        to_core(k)

    def done(k):
        took(3, k, recv_sem)

    def sent(k):
        for stage in (0, 1, 2, 3) if part else (0, 1, 3):
            took(stage, k, send_sem)

    def pump(s):
        steps = ((3, fourth), (2, third), (1, second), (-1, start))
        for back, stage in steps if part else steps[1:]:
            k = first + s - back
            if isinstance(s, int):
                if first <= k < last:
                    stage(k)
            else:

                @pl.when((k >= first) & (k < last))
                def _(k=k, stage=stage):
                    stage(k)

    return start, second, third, done, sent, pump, z_devs + [y_dev, x_dev, c_dev]


def experts_kernel(
    xf_ref,
    cf_ref,
    early_ref,
    xb_ref,
    c_ref,
    g_ref,
    og_ref,
    wg_ref,
    wu_ref,
    wd_ref,
    hid_ref,
    xin_ref,
    xn_ref,
    gain1_ref,
    gain_ref,
    q_ref,
    k_ref,
    v_ref,
    lse_ref,
    bias_ref,
    wo_ref,
    att_ref,
    wq_ref,
    wk_ref,
    wv_ref,
    cos_ref,
    sin_ref,
    all_x,
    all_c,
    mix_ref,
    gx_ref,
    gg_ref,
    gu_ref,
    gd_ref,
    g1_ref,
    g2_ref,
    go_ref,
    gq_ref,
    gk_ref,
    gv_ref,
    x_ref,
    wc,
    wbd,
    mixp,
    part,
    half_in,
    quarter_in,
    tot,
    mhalf_in,
    mquarter_in,
    grads,
    ybuf,
    zbuf,
    hidq,
    d_att,
    dq_ref,
    dk_ref,
    dv_ref,
    dqkv,
    xrows,
    gvec,
    gvec_in,
    msg,
    msg_in,
    acc,
    accd,
    ux,
    uc,
    w_sem,
    in_sem,
    load_sem,
    out_sem,
    x_send,
    x_recv,
    x_own,
    c_send,
    c_recv,
    c_own,
    mix_sem,
    ysem,
    yrsem,
    zsem,
    zrsem,
    vsem,
    vrsem,
    msem,
    mrsem,
    ssend,
    srecv,
):
    T, D = x_ref.shape
    A = all_x.shape[0]
    E, _, f = wg_ref.shape
    n_own = gg_ref.shape[0]
    chunks = T // CHUNK
    p = lax.axis_index("dp")
    t = lax.axis_index("tensor")
    xq = t // 2
    c = t % 2
    x_dev = (p, (1 - xq) * 2 + c)
    c_dev = (p, xq * 2 + 1 - c)
    f_dev = (p, (1 - xq) * 2 + 1 - c)
    trees = msg.shape[0]
    peers = [((p + j) % trees, t) for j in range(1, trees)]
    x_start, _, _, x_done, x_sent, x_pump, _ = gatherer(
        xf_ref, all_x, x_send, x_recv, x_own, 0, chunks, PART, BOTH
    )
    c_start, _, _, c_done, c_sent, c_pump, _ = gatherer(
        cf_ref, all_c, c_send, c_recv, c_own, EARLY, chunks, PART, BOTH
    )
    xb_load = pltpu.make_async_copy(xb_ref, x_ref, in_sem.at[0])
    xb_load.start()
    sync_with(peers + [x_dev, c_dev, f_dev])

    def pump(s):
        x_pump(s)
        c_pump(s)

    x_start(0)
    c_start(EARLY)

    first_own = p * n_own
    own_loads = [pltpu.make_async_copy(wd_ref.at[pl.ds(first_own, n_own)], wbd.at[0, pl.ds(0, n_own)], w_sem.at[0, 0])]
    for i in range(n_own):
        for h, src in enumerate((wg_ref, wu_ref)):
            dst = wc.at[0, :, pl.ds((h * n_own + i) * f, f)]
            own_loads.append(pltpu.make_async_copy(src.at[first_own + i], dst, w_sem.at[1 + 2 * i + h, 0]))

    def w_loads(i, slot):
        loads = [pltpu.make_async_copy(wd_ref.at[pl.ds(i * EG, EG)], wbd.at[slot], w_sem.at[0, slot])]
        for j in range(EG):
            for h, src in enumerate((wg_ref, wu_ref)):
                dst = wc.at[slot, :, pl.ds((h * EG + j) * f, f)]
                loads.append(pltpu.make_async_copy(src.at[i * EG + j], dst, w_sem.at[1 + 2 * j + h, slot]))
        return loads

    for copy in w_loads(0, 0):
        copy.start()
    part[...] = jnp.zeros_like(part)
    xb_load.wait()
    mixp[...] = jnp.zeros_like(mixp)
    groups = E // EG
    rows_at = T // 2
    lanes = g_ref.shape[1]

    def group_step(i, _):
        slot = i % 2

        @pl.when(i + 1 < groups)
        def _():
            for copy in w_loads(i + 1, 1 - slot):
                copy.start()

        @pl.when(i + 1 == groups)
        def _():
            for copy in own_loads:
                copy.start()

        @pl.when(i % 2 == 0)
        def _():
            pump(i // 2)

        for copy in w_loads(i, slot):
            copy.wait()
        wd = wbd[slot].reshape(EG * f, D)

        def rows_step(r, _):
            rows = pl.ds(pl.multiple_of(r * rows_at, 16), rows_at)
            turned = pltpu.roll(g_ref[rows, :], lanes - i * EG, 1)
            g = [turned[:, j : j + 1] for j in range(EG)]
            act, dgu = expert_core(x_ref[rows, :], c_ref[rows, :], g, wc[slot], wd)
            mixp[r] += dot(act, wd).reshape(2, rows_at // 2, D)
            part[r] += dot_t(dgu, wc[slot]).reshape(2, rows_at // 2, D)
            return 0

        lax.fori_loop(0, 2, rows_step, 0)
        return 0

    lax.fori_loop(0, groups, group_step, 0)

    acc[...] = jnp.zeros_like(acc)
    accd[...] = jnp.zeros_like(accd)

    Q = T // 4
    my_rows = pl.ds(pl.multiple_of(t * Q, 16), Q)
    hid_load = pltpu.make_async_copy(hid_ref.at[my_rows], hidq, in_sem.at[1])
    hid_load.start()
    xrows_load = pltpu.make_async_copy(xin_ref.at[my_rows], xrows, in_sem.at[2])
    xrows_load.start()
    xn_load = pltpu.make_async_copy(xn_ref, x_ref, in_sem.at[3])

    def summing(src, dst, i, dev):
        return pltpu.make_async_remote_copy(
            src_ref=src,
            dst_ref=dst,
            send_sem=ssend.at[i],
            recv_sem=srecv.at[i],
            device_id=dev,
            device_id_type=MESH,
        )

    sum_copies = [
        summing(part.at[:, 1 - c], half_in, 0, c_dev),
        summing(part.at[1 - xq, c], quarter_in, 1, x_dev),
        summing(tot.at[xq, c], tot.at[xq, c], 2, x_dev),
        summing(tot.at[:, c], tot.at[:, c], 3, c_dev),
    ]
    mix_copies = [
        summing(mixp.at[:, 1 - c], mhalf_in, 4, c_dev),
        summing(mixp.at[1 - xq, c], mquarter_in, 5, x_dev),
        summing(mixp.at[xq, c], mix_ref.at[xq, c], 6, x_dev),
        summing(mix_ref.at[:, c], mix_ref.at[:, c], 7, c_dev),
    ]
    mix_own = pltpu.make_async_copy(mixp.at[xq, c], mix_ref.at[xq, c], mix_sem)
    core_first = summing(part.at[:, 1 - c], half_in, 8, c_dev)
    x_first = summing(part.at[1 - xq, c], quarter_in, 9, x_dev)
    gx_out = pltpu.make_async_copy(hidq, gx_ref, in_sem.at[4])

    a = p // 2
    b = p % 2
    pieces, _, _, R, W = grads.shape
    y_dev = (a * 2 + 1 - b, t)

    def to_y(i):
        return send(grads.at[i, :, 1 - b], ybuf.at[i], ysem.at[i], yrsem.at[i], y_dev)

    def to_z(i):
        return [
            send(
                grads.at[i, (a + j) % A, b],
                zbuf.at[i, j - 1],
                zsem.at[i, j - 1],
                zrsem.at[i, j - 1],
                (((a + j) % A) * 2 + b, t),
            )
            for j in range(1, A)
        ]

    def y_done(i):
        to_y(i).wait()
        grads[i, :, b] += ybuf[i]
        for copy in to_z(i):
            copy.start()

    def z_done(i):
        for copy in to_z(i):
            copy.wait()
        whole = grads[i, a, b]
        for j in range(A - 1):
            whole += zbuf[i, j]
        return whole

    v_sends = [
        send(gvec, gvec_in.at[j], vsem.at[j], vrsem.at[j], dev) for j, dev in enumerate((x_dev, c_dev, f_dev))
    ]
    m_sends = [
        send(msg.at[dev[0]], msg_in.at[j], msem.at[j], mrsem.at[j], dev) for j, dev in enumerate(peers)
    ]

    first = groups // 2
    units = A // 4
    group_trees = A // units

    def part_of(ref, k, u):
        rows = pl.ds(pl.multiple_of(k * CHUNK, 8), CHUNK)
        return ref.at[pl.ds(u * group_trees, group_trees), :, rows]

    def load_x(k, u, slot):
        return pltpu.make_async_copy(part_of(all_x, k, u), ux.at[slot], load_sem.at[0, slot])

    def load_c(ref, k, u, slot):
        return pltpu.make_async_copy(part_of(ref, k, u), uc.at[slot], load_sem.at[1, slot])

    def load(k, u, slot):
        load_x(k, u, slot).start()

        @pl.when(k < EARLY)
        def _():
            load_c(early_ref, k, u, slot).start()

        @pl.when(k >= EARLY)
        def _():
            load_c(all_c, k, u, slot).start()

    for copy in own_loads:
        copy.wait()
    wdo = wbd[0, 0:n_own].reshape(n_own * f, D)

    def own_unit(k, u, slot):
        load_x(k, u, slot).wait()
        load_c(all_c, k, u, slot).wait()
        size = group_trees * 2 * CHUNK
        xs = ux[slot].reshape(size, D).astype(BF)
        cs = uc[slot].reshape(size, D).astype(BF)
        turned = og_ref[k, u].T
        g = [turned[:, j : j + 1] for j in range(n_own)]
        act, dgu = expert_core(xs, cs, g, wc[0, :, 0 : 2 * n_own * f], wdo)
        acc[...] += dot_l(xs, dgu)
        accd[...] += dot_l(act, cs)

    heads, _, hd = q_ref.shape
    group = heads // k_ref.shape[0]
    scale = hd ** (-0.5)
    dk_ref[...] = jnp.zeros_like(dk_ref)
    dv_ref[...] = jnp.zeros_like(dv_ref)

    def attention_back(h):
        g = h // group

        def block(i, _):
            rows = pl.ds(pl.multiple_of(i * Q, 16), Q)
            q = q_ref[h, rows, :]
            da = d_att[h, rows, :]
            lse = pltpu.roll(lse_ref[rows, :], lse_ref.shape[1] - h, 1)[:, 0:1]
            scores = dot_t(q, k_ref[g]) * scale + bias_ref[rows, :].astype(F32)
            probs = jnp.exp(scores - lse)
            d_probs = dot_t(da, v_ref[g])
            row_dot = jnp.sum(probs * d_probs, axis=-1, keepdims=True)
            d_scores = (probs * (d_probs - row_dot) * scale).astype(BF)
            dq_ref[h, rows, :] = dot(d_scores, k_ref[g])
            dk_ref[g] += dot_l(d_scores, q)
            dv_ref[g] += dot_l(probs.astype(BF), da)
            return 0

        lax.fori_loop(0, 4, block, 0)

    width = heads * hd
    kwidth = k_ref.shape[0] * hd

    def finish_start():
        lane = lax.broadcasted_iota(jnp.int32, (T, hd), 1)
        cosine = cos_ref[:, 0:hd]
        sine = jnp.where(lane < hd // 2, sin_ref[:, 0:hd], -sin_ref[:, 0:hd])

        def turned_back(d):
            swapped = jnp.concatenate([d[:, hd // 2 :], d[:, : hd // 2]], axis=1)
            return (d * cosine + swapped * sine).astype(BF)

        for h in range(heads):
            dqkv[:, h * hd : (h + 1) * hd] = turned_back(dq_ref[h])
        for g in range(k_ref.shape[0]):
            at = width + g * hd
            dqkv[:, at : at + hd] = turned_back(dk_ref[g])
            at = width + kwidth + g * hd
            dqkv[:, at : at + hd] = dv_ref[g].astype(BF)
        xn_load.wait()
        for i in range(width // W, pieces):
            at = (i - width // W) * W
            grads[i] = dot_l(x_ref[...], dqkv[:, at : at + W]).reshape(A, 2, R, W)
            to_y(i).start()
        for r in range(2):
            rows = pl.ds(r * 2 * Q, 2 * Q)
            total = dot_t(dqkv[rows, 0:width], wq_ref[...])
            total += dot_t(dqkv[rows, width : width + kwidth], wk_ref[...])
            total += dot_t(dqkv[rows, width + kwidth :], wv_ref[...])
            part[r] = total.reshape(2, Q, D)
        core_first.start()

    def slot_step(s, _):
        pump(s)

        @pl.when(s == first)
        def _():
            sum_copies[0].start()

        @pl.when(s == first + 1)
        def _():
            sum_copies[0].wait()
            part[:, c] += half_in[...]
            sum_copies[1].start()

        @pl.when(s == first + 3)
        def _():
            sum_copies[1].wait()
            hid_load.wait()
            hidden = hidq[...]
            inverse = lax.rsqrt(jnp.mean(hidden * hidden, axis=-1, keepdims=True) + epsilon)
            normal = hidden * inverse
            d_in = part[xq, c] + quarter_in[...]
            gvec[1:2, :] = jnp.sum(d_in * normal, axis=0, keepdims=True)
            scaled = d_in * gain_ref[...]
            tot[xq, c] = c_ref[my_rows, :].astype(F32) + inverse * (
                scaled - normal * jnp.mean(scaled * normal, axis=-1, keepdims=True)
            )
            sum_copies[2].start()

        @pl.when(s == first + 5)
        def _():
            sum_copies[2].wait()
            sum_copies[3].start()
            mix_copies[0].start()

        @pl.when(s == first + 6)
        def _():
            sum_copies[3].wait()
            x_ref[...] = tot[...].reshape(T, D).astype(BF)
            for h in range(heads):
                w = wo_ref[h * hd : (h + 1) * hd, :]
                d_att[h] = dot_t(x_ref[...], w).astype(BF)
            for i in range(width // W):
                out_grad = dot_l(x_ref[...], att_ref[:, i * W : (i + 1) * W])
                grads[i] = out_grad.reshape(A, 2, R, W)
                to_y(i).start()
            xn_load.start()
            mix_copies[0].wait()
            mixp[:, c] += mhalf_in[...]
            mix_copies[1].start()

        @pl.when(s == first + 7)
        def _():
            for i in range(width // W):
                y_done(i)

        @pl.when(s == first + 8)
        def _():
            finish_start()
            mix_copies[1].wait()
            mixp[xq, c] += mquarter_in[...]
            mix_own.start()
            mix_copies[2].start()

        @pl.when(s == first + 9)
        def _():
            core_first.wait()
            part[:, c] += half_in[...]
            x_first.start()
            for i in range(width // W, 2 * (width // W)):
                y_done(i)

        @pl.when(s == first + 10)
        def _():
            for i in range(2 * (width // W), pieces):
                y_done(i)
            xrows_load.wait()
            x32 = xrows[...].astype(F32)
            inverse = lax.rsqrt(jnp.mean(x32 * x32, axis=-1, keepdims=True) + epsilon)
            normal = x32 * inverse
            x_first.wait()
            d_first = part[xq, c] + quarter_in[...]
            gvec[0:1, :] = jnp.sum(d_first * normal, axis=0, keepdims=True)
            for copy in v_sends:
                copy.start()
            scaled = d_first * gain1_ref[...]
            hidq[...] = tot[xq, c] + inverse * (
                scaled - normal * jnp.mean(scaled * normal, axis=-1, keepdims=True)
            )
            gx_out.start()

        @pl.when(s == first + 11)
        def _():
            mix_own.wait()
            mix_copies[2].wait()
            mix_copies[3].start()
            for copy in v_sends:
                copy.wait()
            total = gvec[0:2, :] + gvec_in[0, 0:2, :] + gvec_in[1, 0:2, :] + gvec_in[2, 0:2, :]
            for i in range(trees):
                msg[i, 0:2, :] = total[:, i * R : (i + 1) * R]
            for copy in m_sends:
                copy.start()

        @pl.when((s == first + 6) | (s == first + 7))
        def _():
            attention_back((s - first - 6) * 2)
            attention_back((s - first - 6) * 2 + 1)

        k = s - LAG

        @pl.when((k >= 0) & (k < chunks))
        def _():
            x_done(k)

            @pl.when(k >= EARLY)
            def _():
                c_done(k)

            load(k, 0, 0)
            for u in range(units):
                if u + 1 < units:
                    load(k, u + 1, (u + 1) % 2)
                own_unit(k, u, u % 2)

        return 0

    lax.fori_loop(first, chunks + LAG, slot_step, 0)

    outs = []
    for j in range(n_own):
        outs += [
            pltpu.make_async_copy(acc.at[:, pl.ds(j * f, f)], gg_ref.at[j], out_sem.at[0, j]),
            pltpu.make_async_copy(acc.at[:, pl.ds((n_own + j) * f, f)], gu_ref.at[j], out_sem.at[1, j]),
            pltpu.make_async_copy(accd.at[pl.ds(j * f, f)], gd_ref.at[j], out_sem.at[2, j]),
        ]
    for copy in outs:
        copy.start()
    per = width // W
    for i in range(per):
        go_ref[:, i * W : (i + 1) * W] = z_done(i)
        gq_ref[:, i * W : (i + 1) * W] = z_done(per + i)
    gk_ref[...] = z_done(2 * per)
    gv_ref[...] = z_done(2 * per + 1)
    for copy in m_sends:
        copy.wait()
    mine = msg[p]
    for j in range(trees - 1):
        mine += msg_in[j]
    g1_ref[...] = mine[0:1]
    g2_ref[...] = mine[1:2]
    gx_out.wait()
    mix_copies[3].wait()

    def sends(k, _):
        x_sent(k)

        @pl.when(k >= EARLY)
        def _():
            c_sent(k)

        return 0

    lax.fori_loop(0, chunks, sends, 0)
    for copy in outs:
        copy.wait()


def experts(
    xf, cf, early, xb, c, dense_gates, own_gates, wg, wu, wd, hidden, x, xn, gain1, gain2, q, k, v, lse, bias,
    wo, att, wq, wk, wv, cosine, sine, trees,
):
    T, D = c.shape
    E, _, f = wg.shape
    own = E // trees
    chunks = T // CHUNK
    A = trees // 2
    Q = T // 4
    R = D // trees
    W = wk.shape[1]
    pieces = 2 * (wq.shape[1] // W) + 2
    gates_in = jnp.pad(dense_gates, ((0, 0), (0, 128 - E)))
    units = A // 4
    og = own_gates.reshape(units, trees // units, 8, chunks, CHUNK).transpose(3, 0, 2, 1, 4)
    og = og.reshape(chunks, units, 8, trees // units * CHUNK)
    slots = 2 if A > 4 else 1
    S = jax.ShapeDtypeStruct
    V = pltpu.VMEM
    out = pl.pallas_call(
        experts_kernel,
        in_specs=[HBM] * 4 + [VMEM] * 3 + [HBM] * 6 + [VMEM] * 14,
        out_specs=[HBM] * 7 + [VMEM] * 6,
        out_shape=[
            S((A, 2, T, D), F32),
            S((A, 2, T, D), F32),
            S((2, 2, Q, D), F32),
            S((Q, D), F32),
            S((own, D, f), F32),
            S((own, D, f), F32),
            S((own, f, D), F32),
            S((1, R), F32),
            S((1, R), F32),
            S((R, wq.shape[1]), F32),
            S((R, wq.shape[1]), F32),
            S((R, W), F32),
            S((R, W), F32),
        ],
        scratch_shapes=[
            V((T, D), BF),
            V((2, D, 2 * EG * f), BF),
            V((2, EG, f, D), BF),
            V((2, 2, Q, D), F32),
            V((2, 2, Q, D), F32),
            V((2, Q, D), F32),
            V((Q, D), F32),
            V((2, 2, Q, D), F32),
            V((2, Q, D), F32),
            V((Q, D), F32),
            V((pieces, A, 2, R, W), F32),
            V((pieces, A, R, W), F32),
            V((pieces, A - 1, R, W), F32),
            V((Q, D), F32),
            V(q.shape, BF),
            V(q.shape, F32),
            V(k.shape, F32),
            V(v.shape, F32),
            V((T, wq.shape[1] + 2 * W), BF),
            V((Q, D), BF),
            V((8, D), F32),
            V((3, 8, D), F32),
            V((trees, 8, R), F32),
            V((trees - 1, 8, R), F32),
            V((D, 2 * own * f), F32),
            V((own * f, D), F32),
            V((slots, 4, 2, CHUNK, D), F32),
            V((slots, 4, 2, CHUNK, D), F32),
            DMA((1 + 2 * EG, 2)),
            DMA((5,)),
            DMA((2, 2)),
            DMA((3, own)),
            DMA((4, chunks)),
            DMA((4, chunks)),
            DMA((2, chunks)),
            DMA((4, chunks - EARLY)),
            DMA((4, chunks - EARLY)),
            DMA((2, chunks - EARLY)),
            DMA(()),
            DMA((pieces,)),
            DMA((pieces,)),
            DMA((pieces, A - 1)),
            DMA((pieces, A - 1)),
            DMA((3,)),
            DMA((3,)),
            DMA((trees - 1,)),
            DMA((trees - 1,)),
            DMA((10,)),
            DMA((10,)),
        ],
        compiler_params=pltpu.CompilerParams(
            collective_id=0, has_side_effects=True, vmem_limit_bytes=62 * 2**20
        ),
    )(
        xf, cf, early, xb, c, gates_in, og, wg, wu, wd, hidden, x, xn, gain1.reshape(1, D), gain2.reshape(1, D),
        q, k, v, lse, bias, wo, att, wq, wk, wv, cosine, sine,
    )
    return out[2:]


def front_kernel(
    x_ref,
    c_ref,
    gain1_ref,
    gain2_ref,
    wq_ref,
    wk_ref,
    wv_ref,
    wo_ref,
    visible_ref,
    cos_ref,
    sin_ref,
    gates_ref,
    early_ref,
    hidden_ref,
    xb_ref,
    xf_ref,
    cf_ref,
    xn_ref,
    att_out,
    q_ref,
    k_ref,
    v_ref,
    lse_ref,
    bias_ref,
    got_ref,
    att,
    others,
    wof,
    wr,
    hot,
    msg,
    peaks,
    ssem,
    rsem,
    wsend,
    wrecv,
    msend,
    mrecv,
    msem,
    c_send,
    c_recv,
    c_own,
):
    T, D = x_ref.shape
    trees = got_ref.shape[0]
    heads, _, hd = q_ref.shape
    kvs = k_ref.shape[0]
    group = heads // kvs
    width = heads * hd
    kwidth = kvs * hd
    scale = hd ** (-0.5)
    half = T // 2
    Q = T // 4
    p = lax.axis_index("dp")
    t = lax.axis_index("tensor")
    xq = t // 2
    c = t % 2
    x_dev = (p, (1 - xq) * 2 + c)
    c_dev = (p, xq * 2 + 1 - c)
    peers = [((p + j) % trees, t) for j in range(1, trees)]
    c_start, _, _, c_done, c_sent, pump, _ = gatherer(
        cf_ref, early_ref, c_send, c_recv, c_own, 0, EARLY, *EARLY_ROWS
    )
    sync_with(peers + [x_dev, c_dev])
    cf_ref[...] = c_ref[...].astype(F32)
    c_start(0)
    wof[t] = wo_ref[...].astype(F32)
    w_x = send(wof.at[t], wof.at[t], wsend.at[0], wrecv.at[0], x_dev)
    w_c = send(wof.at[t], wof.at[t], wsend.at[1], wrecv.at[1], c_dev)
    far = (1 - xq) * 2 + c
    w_on = send(wof.at[far], wof.at[far], wsend.at[2], wrecv.at[2], c_dev)
    w_x.start()
    w_c.start()

    row = lax.broadcasted_iota(jnp.int32, (width, width), 0)
    col = lax.broadcasted_iota(jnp.int32, (width, width), 1)
    low = (col % hd) < hd // 2
    turn = jnp.where(low & (row == col + hd // 2), -1.0, jnp.where(~low & (row == col - hd // 2), 1.0, 0.0))
    turn = turn.astype(BF)
    wr[:, :width] = dot(wq_ref[...], turn).astype(BF)
    wr[:, width:] = dot(wk_ref[...], turn[:kwidth, :kwidth]).astype(BF)

    token = lax.broadcasted_iota(jnp.int32, (T, 128), 0)
    seg = lax.broadcasted_iota(jnp.int32, (T, 128), 1)
    begin = jnp.where(seg == 0, 0, TRUNK + (seg - 1) * SEG)
    end = TRUNK + seg * SEG
    hot[...] = ((token >= begin) & (token < end)).astype(F32).astype(BF)

    def project(i, _):
        rows = pl.ds(pl.multiple_of(i * Q, 16), Q)
        x32 = x_ref[rows, :].astype(F32)
        inverse = lax.rsqrt(jnp.mean(x32 * x32, axis=-1, keepdims=True) + epsilon)
        xn = (x32 * inverse * gain1_ref[...]).astype(BF)
        xn_ref[rows, :] = xn
        cosine = cos_ref[rows, :]
        sine = sin_ref[rows, :]
        turned = dot(xn, wr[...])
        query = dot(xn, wq_ref[...])
        query = query * jnp.concatenate([cosine] * (width // 128), axis=1) + turned[:, :width] * jnp.concatenate(
            [sine] * (width // 128), axis=1
        )
        key = dot(xn, wk_ref[...]) * cosine + turned[:, width:] * sine
        value = dot(xn, wv_ref[...])
        for h in range(heads):
            q_ref[h, rows, :] = query[:, h * hd : (h + 1) * hd].astype(BF)
        for g in range(kvs):
            k_ref[g, rows, :] = key[:, g * hd : (g + 1) * hd].astype(BF)
            v_ref[g, rows, :] = value[:, g * hd : (g + 1) * hd].astype(BF)
        mine = hot[rows, :]
        reach = dot(mine, visible_ref[...]).astype(BF)
        near = dot_t(reach, hot[...]) > 0.5
        same = dot_t(mine, hot[...]) > 0.5
        qi = lax.broadcasted_iota(jnp.int32, (Q, T), 0) + i * Q
        kj = lax.broadcasted_iota(jnp.int32, (Q, T), 1)
        seen = near & (~same | (kj <= qi))
        bias_ref[rows, :] = jnp.where(seen, 0.0, -1e30).astype(BF)
        return 0

    lax.fori_loop(0, 4, project, 0)
    pump(0)
    peaks[...] = jnp.full_like(peaks, -1e30)
    lane = lax.broadcasted_iota(jnp.int32, (1, 128), 1)

    def attend(i, _):
        rows = pl.ds(pl.multiple_of(i * Q, 16), Q)
        bias = bias_ref[rows, :].astype(F32)
        for h in range(heads):
            g = h // group
            scores = dot_t(q_ref[h, rows, :], k_ref[g]) * scale + bias
            top = jnp.max(scores, axis=-1, keepdims=True)
            expo = jnp.exp(scores - top)
            total = jnp.sum(expo, axis=-1, keepdims=True)
            probs = (expo / total).astype(BF)
            out = dot(probs, v_ref[g]).astype(BF)
            att_out[rows, h * hd : (h + 1) * hd] = out
            att[rows, h * hd : (h + 1) * hd] = out.astype(F32)
            lse_ref[rows, h : h + 1] = top + jnp.log(total)
            peak = jnp.max(top, axis=0, keepdims=True)
            peaks[0:1, :] = jnp.maximum(peaks[0:1, :], jnp.where(lane == h, peak, -1e30))
        return 0

    rows = [pl.ds(i * half, half) for i in range(2)]
    to_x = [send(att.at[r], others.at[1, r], ssem.at[0, i], rsem.at[0, i], x_dev) for i, r in enumerate(rows)]
    to_c = [send(att.at[r], others.at[0, r], ssem.at[1, i], rsem.at[1, i], c_dev) for i, r in enumerate(rows)]
    on = [send(others.at[1, r], others.at[2, r], ssem.at[2, i], rsem.at[2, i], c_dev) for i, r in enumerate(rows)]
    lax.fori_loop(0, 2, attend, 0)
    to_x[0].start()
    to_c[0].start()
    pump(1)
    lax.fori_loop(2, 4, attend, 0)
    to_x[1].start()
    to_c[1].start()
    pump(2)
    msg[...] = gates_ref[...]
    msg[:, 7:8, 0:128] = jnp.broadcast_to(peaks[0:1, :][None], (trees, 1, 128))
    messages = [
        send(msg.at[dev[0]], got_ref.at[j], msend.at[j], mrecv.at[j], dev) for j, dev in enumerate(peers, 1)
    ]
    for copy in messages:
        copy.start()
    mine = pltpu.make_async_copy(msg.at[p], got_ref.at[0], msem)
    mine.start()
    w_x.wait()
    w_on.start()
    w_c.wait()

    def proj(block, owner):
        return dot(block.astype(BF), wof[owner].astype(BF))

    for i, r in enumerate(rows):
        hidden_ref[r, :] = x_ref[r, :].astype(F32) + proj(att[r, :], t)
    for i, r in enumerate(rows):
        to_c[i].wait()
        hidden_ref[r, :] += proj(others[0, r, :], xq * 2 + 1 - c)
    pump(3)
    for i, r in enumerate(rows):
        to_x[i].wait()
        on[i].start()
        hidden_ref[r, :] += proj(others[1, r, :], far)
    pump(4)
    w_on.wait()
    for i, r in enumerate(rows):
        on[i].wait()
        hidden = hidden_ref[r, :] + proj(others[2, r, :], (1 - xq) * 2 + 1 - c)
        hidden_ref[r, :] = hidden
        inverse = lax.rsqrt(jnp.mean(hidden * hidden, axis=-1, keepdims=True) + epsilon)
        low_x = (hidden * inverse * gain2_ref[...]).astype(BF)
        xb_ref[r, :] = low_x
        xf_ref[r, :] = low_x.astype(F32)
    for copy in messages:
        copy.wait()
    mine.wait()
    for s in range(5, EARLY + 3):
        pump(s)
    for k in range(EARLY):
        c_done(k)
        c_sent(k)


def front(x, c, gain1, gain2, wq, wk, wv, wo, visible, cosine, sine, gates_out):
    T, D = x.shape
    trees = gates_out.shape[0]
    A = trees // 2
    heads = wq.shape[1] // HEAD_DIM
    kvs = wk.shape[1] // HEAD_DIM
    width = wq.shape[1]
    S = jax.ShapeDtypeStruct
    V = pltpu.VMEM
    return pl.pallas_call(
        front_kernel,
        in_specs=[VMEM] * 12,
        out_specs=[HBM] + [VMEM] * 12,
        out_shape=[
            S((A, 2, T, D), F32),
            S((T, D), F32),
            S((T, D), BF),
            S((T, D), F32),
            S((T, D), F32),
            S((T, D), BF),
            S((T, width), BF),
            S((heads, T, HEAD_DIM), BF),
            S((kvs, T, HEAD_DIM), BF),
            S((kvs, T, HEAD_DIM), BF),
            S((T, 128), F32),
            S((T, T), BF),
            S(gates_out.shape, F32),
        ],
        scratch_shapes=[
            V((T, width), F32),
            V((3, T, width), F32),
            V((4, width, D), F32),
            V((D, width + wk.shape[1]), BF),
            V((T, 128), BF),
            V(gates_out.shape, F32),
            V((8, 128), F32),
            DMA((3, 2)),
            DMA((3, 2)),
            DMA((3,)),
            DMA((3,)),
            DMA((trees,)),
            DMA((trees,)),
            DMA(()),
            DMA((4, EARLY)),
            DMA((4, EARLY)),
            DMA((2, EARLY)),
        ],
        compiler_params=pltpu.CompilerParams(
            collective_id=1, has_side_effects=True, vmem_limit_bytes=58 * 2**20
        ),
    )(x, c, gain1.reshape(1, D), gain2.reshape(1, D), wq, wk, wv, wo, visible, cosine, sine, gates_out)


def last_kernel(hid_ref, mix_ref, got_ref, limit_ref, wq_ref, wk_ref, *refs):
    n = (len(refs) - 9) // 3
    out_ref, factor_ref, qs_ref, ks_ref = refs[n : n + 4]
    hid, mix, held = refs[2 * n + 4], refs[2 * n + 5], refs[2 * n + 6 : 3 * n + 6]
    in_sem, sem, big_sem = refs[3 * n + 6 :]
    big = [pltpu.make_async_copy(hid_ref, hid, big_sem.at[0]), pltpu.make_async_copy(mix_ref, mix, big_sem.at[1])]
    ins = [pltpu.make_async_copy(refs[i], held[i], in_sem.at[i]) for i in range(n)]
    outs = [pltpu.make_async_copy(held[i], refs[n + 4 + i], sem.at[i]) for i in range(n)]
    for copy in big + ins:
        copy.start()
    heads = limit_ref.shape[1]
    limits = limit_ref[...]
    peaks = jnp.max(got_ref[:, 7, 0:128], axis=0, keepdims=True)[:, 0:heads]
    factors = limits / jnp.maximum(peaks, limits)
    factor_ref[...] = factors
    group = wq_ref.shape[1] // wk_ref.shape[1]
    roots = [jnp.sqrt(factors[:, h : h + 1]) for h in range(heads)]
    least = [
        jnp.sqrt(jnp.min(factors[:, g * group : (g + 1) * group], axis=1, keepdims=True)) for g in range(heads // group)
    ]

    def scaled(w_ref, values):
        head = lax.broadcasted_iota(jnp.int32, (1, w_ref.shape[1]), 1) // HEAD_DIM
        row = jnp.zeros((1, w_ref.shape[1]), F32)
        for h, value in enumerate(values):
            row = jnp.where(head == h, value, row)
        return (w_ref[...].astype(F32) * row).astype(BF)

    qs_ref[...] = scaled(wq_ref, roots)
    ks_ref[...] = scaled(wk_ref, least)
    for copy in big:
        copy.wait()
    out_ref[...] = (hid[...] + mix[...]).astype(BF)
    for i in range(n):
        ins[i].wait()
        outs[i].start()
    for copy in outs:
        copy.wait()


def last(hidden, mixture, got, limits, wq, wk, *rest):
    T, D = hidden.shape
    S = jax.ShapeDtypeStruct
    n = len(rest)
    return pl.pallas_call(
        last_kernel,
        in_specs=[HBM] * 2 + [VMEM] * 4 + [HBM] * n,
        out_specs=[VMEM] * 4 + [HBM] * n,
        out_shape=[
            S((T, D), BF),
            S((1, limits.shape[0]), F32),
            S(wq.shape, BF),
            S(wk.shape, BF),
        ]
        + [S(r.shape, r.dtype) for r in rest],
        scratch_shapes=[pltpu.VMEM((T, D), F32)] * 2
        + [pltpu.VMEM(r.shape, r.dtype) for r in rest]
        + [DMA((n,)), DMA((n,)), DMA((2,))],
        compiler_params=pltpu.CompilerParams(vmem_limit_bytes=62 * 2**20),
    )(hidden, mixture.reshape(T, D), got, limits.reshape(1, -1), wq, wk, *rest)


def local(
    block_input,
    norm_first,
    norm_second,
    w_query,
    w_key,
    w_value,
    w_out,
    w_gate,
    w_up,
    w_down,
    routes,
    gates,
    parents,
    clip_limits,
    cotangent,
):
    count, width = block_input.shape
    head_dim = HEAD_DIM
    query_cols = w_query.shape[1]
    key_cols = w_key.shape[1]
    query_heads = query_cols // head_dim
    kv_heads = key_cols // head_dim
    trees = lax.axis_size("dp")
    own = EXPERTS // trees
    position, visible = tree_tables(parents[0], count)
    visible = jnp.pad(visible.astype(jnp.bfloat16), ((0, 128 - SEGS), (0, 128 - SEGS)))
    cosine, sine = rotary_tables(position, head_dim)
    wide_cosine = jnp.tile(cosine[:, 0], (1, 128 * 2 // head_dim))
    wide_sine = jnp.tile(sine[:, 0], (1, 128 * 2 // head_dim))
    routed = routes[:, :, None] == jnp.arange(EXPERTS, dtype=jnp.int32)[None, None, :]
    dense_gates = jnp.sum(jnp.where(routed, gates[:, :, None], 0.0), axis=1)
    gates_out = jnp.pad(dense_gates.T.reshape(trees, own, count), ((0, 0), (0, 8 - own), (0, 0)))
    (
        early,
        hidden,
        input_second,
        x_wide,
        c_wide,
        input_first,
        attended_parts,
        queries,
        keys,
        values,
        log_norms,
        bias,
        got,
    ) = front(
        block_input,
        cotangent,
        norm_first,
        norm_second,
        w_query,
        w_key,
        w_value,
        w_out,
        visible,
        wide_cosine,
        wide_sine,
        gates_out,
    )
    order = (lax.axis_index("dp") - jnp.arange(trees)) % trees
    hot = (order[:, None] == jnp.arange(trees)[None, :]).astype(jnp.float32)
    own_gates = jnp.sum(hot[:, :, None, None] * got[:, None], axis=0)
    (
        mixture,
        grad_x,
        gate_shard,
        up_shard,
        down_shard,
        first_gain_grad,
        second_shard,
        out_shard,
        query_shard,
        key_shard,
        value_shard,
    ) = experts(
        x_wide,
        c_wide,
        early,
        input_second,
        cotangent,
        dense_gates,
        own_gates,
        w_gate,
        w_up,
        w_down,
        hidden,
        block_input,
        input_first,
        norm_first,
        norm_second,
        queries,
        keys,
        values,
        log_norms,
        bias,
        w_out,
        attended_parts,
        w_query,
        w_key,
        w_value,
        wide_cosine,
        wide_sine,
        trees,
    )
    block_out, factors, query_scaled, key_scaled, *rest = last(
        hidden,
        mixture,
        got,
        clip_limits,
        w_query,
        w_key,
        grad_x,
        first_gain_grad,
        second_shard,
        query_shard,
        key_shard,
        value_shard,
        out_shard,
        gate_shard,
        up_shard,
        down_shard,
    )
    grad_x, first_gain_grad, second_shard = rest[:3]
    return (
        block_out,
        grad_x,
        first_gain_grad.reshape(width // trees),
        second_shard.reshape(width // trees),
        *rest[3:],
        factors.reshape(query_heads),
        query_scaled,
        key_scaled,
    )


def solution(mesh):
    placed = (
        P("dp", None),
        P(),
        P(),
        P(None, "tensor"),
        P(None, "tensor"),
        P(None, "tensor"),
        P("tensor", None),
        P(None, None, "tensor"),
        P(None, None, "tensor"),
        P(None, "tensor", None),
        P("dp", None),
        P("dp", None),
        P("dp", None),
        P("tensor"),
        P("dp", None),
    )
    return jax.shard_map(
        local,
        mesh=mesh,
        in_specs=placed,
        out_specs=(
            P("dp", None),
            P(("dp", "tensor"), None),
            P("dp"),
            P("dp"),
            P("dp", "tensor"),
            P("dp", "tensor"),
            P("dp", "tensor"),
            P("dp", "tensor"),
            P("dp", None, "tensor"),
            P("dp", None, "tensor"),
            P("dp", "tensor", None),
            P("tensor"),
            P(None, "tensor"),
            P(None, "tensor"),
        ),
        check_vma=False,
    )
```

```python
import functools

import jax
import jax.numpy as jnp
from jax import lax
from jax.experimental import pallas as pl
from jax.experimental.pallas import tpu as pltpu
from jax.sharding import PartitionSpec as P

HEAD_DIM = 64
EXPERTS = 32
TOPK = 8
TRUNK = 256
SEG = 48
SEGS = 13


epsilon = 1e-06
theta_base = 10000.0
expert_group = 4


def tree_tables(parent_row, count):
    slot_ids = jnp.arange(SEGS, dtype=jnp.int32)
    safe_parent = jnp.maximum(parent_row, 0)
    hot_parent = (safe_parent[:, None] == slot_ids[None, :]).astype(jnp.int32)
    grand_raw = jnp.sum(hot_parent * parent_row[None, :], axis=1)
    grand_parent = jnp.where(parent_row >= 0, grand_raw, -1)
    visible = (
        (slot_ids[:, None] == slot_ids[None, :])
        | (slot_ids[None, :] == parent_row[:, None])
        | (slot_ids[None, :] == grand_parent[:, None])
    )
    depth = (parent_row >= 0).astype(jnp.int32) + (grand_parent >= 0).astype(jnp.int32)
    token_ids = jnp.arange(count, dtype=jnp.int32)
    segment = jnp.where(token_ids < TRUNK, 0, 1 + (token_ids - TRUNK) // SEG)
    local_index = jnp.where(token_ids < TRUNK, token_ids, (token_ids - TRUNK) % SEG)
    seg_match = segment[:, None] == slot_ids[None, :]
    token_depth = jnp.sum(seg_match.astype(jnp.int32) * depth[None, :], axis=1)
    position = jnp.where(segment == 0, token_ids, TRUNK + (token_depth - 1) * SEG + local_index)
    return position, visible


def rotary_tables(position, head_dim):
    half = head_dim // 2
    inverse = theta_base ** (-(jnp.arange(half, dtype=jnp.float32) * 2.0 / head_dim))
    angle = position.astype(jnp.float32)[:, None] * inverse[None, :]
    return (jnp.cos(angle)[:, None, :], jnp.sin(angle)[:, None, :])


F32 = jnp.float32
BF = jnp.bfloat16
MESH = pl.DeviceIdType.MESH
CHUNK = 64
PART = 8
BOTH = 16
EG = 4
LAG = 4
EARLY = 2
QUARTER_AT = 3
SHARED_AT = 6
MIX_AT = 6
EARLY_ROWS = (0, 32)


def dot(a, b):
    return jnp.dot(a, b, preferred_element_type=F32)


def dot_t(a, b):
    return lax.dot_general(a, b, (((1,), (1,)), ((), ())), preferred_element_type=F32)


def dot_l(a, b):
    return lax.dot_general(a, b, (((0,), (0,)), ((), ())), preferred_element_type=F32)


def expert_core(x, c, g, wcat, wdcat):
    n = len(g)
    f = wdcat.shape[0]
    both = dot(x, wcat)
    gate = both[:, :f]
    up = both[:, f:]
    d_act = dot_t(c, wdcat)
    wide = jnp.concatenate([jnp.broadcast_to(v, (x.shape[0], f // n)) for v in g], axis=1)
    sigma = jax.nn.sigmoid(gate)
    silu = gate * sigma
    act = ((silu * up).astype(BF).astype(F32) * wide).astype(BF)
    d_act = d_act * wide
    d_gate = (d_act * up * (sigma + silu * (1.0 - sigma))).astype(BF)
    d_up = (d_act * silu).astype(BF)
    return act, jnp.concatenate([d_gate, d_up], axis=1)


VMEM = pl.BlockSpec(memory_space=pltpu.VMEM)
HBM = pl.BlockSpec(memory_space=pl.ANY)
DMA = pltpu.SemaphoreType.DMA


def sync_with(devices):
    barrier = pltpu.get_barrier_semaphore()
    for dev in devices:
        pl.semaphore_signal(barrier, inc=1, device_id=dev, device_id_type=MESH)
    pl.semaphore_wait(barrier, len(devices))


def send(src, dst, out_sem, in_sem, dev):
    return pltpu.make_async_remote_copy(
        src_ref=src,
        dst_ref=dst,
        send_sem=out_sem,
        recv_sem=in_sem,
        device_id=dev,
        device_id_type=MESH,
    )


def gatherer(src, dst, send_sem, recv_sem, own_sem, first, last, part, both):
    A = dst.shape[0]
    p = lax.axis_index("dp")
    t = lax.axis_index("tensor")
    a = p // 2
    b = p % 2
    xq = t // 2
    c = t % 2
    y_dev = (a * 2 + 1 - b, t)
    x_dev = (p, (1 - xq) * 2 + c)
    c_dev = (p, xq * 2 + 1 - c)
    z_devs = [(((a + j) % A) * 2 + b, t) for j in range(1, A)]

    def rows1(k):
        return pl.ds(pl.multiple_of(k * CHUNK + (c * 2 + xq) * part, 8), part)

    def rows_pair(k):
        return pl.ds(pl.multiple_of(k * CHUNK + c * 2 * part, 8), 2 * part)

    def rows2(k):
        return pl.ds(pl.multiple_of(k * CHUNK + 4 * part + c * both, 8), both)

    def mine(k):
        return [rows1(k), rows2(k)] if part and both else [rows1(k)] if part else [rows2(k)]

    def of_core(k):
        return [rows_pair(k), rows2(k)] if part and both else [rows_pair(k)] if part else [rows2(k)]

    def remote(one, two, stage, k, dev):
        return pltpu.make_async_remote_copy(
            src_ref=one,
            dst_ref=two,
            send_sem=send_sem.at[stage, k - first],
            recv_sem=recv_sem.at[stage, k - first],
            device_id=dev,
            device_id_type=MESH,
        )

    sizes = [
        dst.at[pl.ds(0, A - 1), 0, pl.ds(0, part + both)],
        dst.at[:, 0, pl.ds(0, part + both)],
        dst.at[:, :, pl.ds(0, max(part, 8))],
        dst.at[:, :, pl.ds(0, 2 * part + both)],
    ]

    def took(stage, k, sem):
        pltpu.make_async_copy(sizes[stage], sizes[stage], sem.at[stage, k - first]).wait()

    def own(k, i):
        rows = mine(k)[i]
        return pltpu.make_async_copy(src.at[rows], dst.at[a, b, rows], own_sem.at[i, k - first])

    def start(k):
        for i, rows in enumerate(mine(k)):
            for dev in z_devs:
                remote(src.at[rows], dst.at[a, b, rows], 0, k, dev).start()
            own(k, i).start()

    def second(k):
        took(0, k, recv_sem)
        for i, rows in enumerate(mine(k)):
            own(k, i).wait()
            remote(dst.at[:, b, rows], dst.at[:, b, rows], 1, k, y_dev).start()

    def to_core(k):
        for rows in of_core(k):
            remote(dst.at[:, :, rows], dst.at[:, :, rows], 3, k, c_dev).start()

    def third(k):
        took(1, k, recv_sem)
        if not part:
            to_core(k)
            return
        rows = rows1(k)
        remote(dst.at[:, :, rows], dst.at[:, :, rows], 2, k, x_dev).start()

    def fourth(k):
        took(2, k, recv_sem)
        to_core(k)

    def done(k):
        took(3, k, recv_sem)

    def sent(k):
        for stage in (0, 1, 2, 3) if part else (0, 1, 3):
            took(stage, k, send_sem)

    def pump(s):
        steps = ((3, fourth), (2, third), (1, second), (-1, start))
        for back, stage in steps if part else steps[1:]:
            k = first + s - back
            if isinstance(s, int):
                if first <= k < last:
                    stage(k)
            else:

                @pl.when((k >= first) & (k < last))
                def _(k=k, stage=stage):
                    stage(k)

    return start, second, third, done, sent, pump, z_devs + [y_dev, x_dev, c_dev]


def experts_kernel(
    xf_ref,
    cf_ref,
    early_ref,
    xb_ref,
    c_ref,
    g_ref,
    og_ref,
    wg_ref,
    wu_ref,
    wd_ref,
    hid_ref,
    xin_ref,
    xn_ref,
    gain1_ref,
    gain_ref,
    q_ref,
    k_ref,
    v_ref,
    lse_ref,
    bias_ref,
    wo_ref,
    att_ref,
    wq_ref,
    wk_ref,
    wv_ref,
    cos_ref,
    sin_ref,
    all_x,
    all_c,
    mix_ref,
    gx_ref,
    gg_ref,
    gu_ref,
    gd_ref,
    g1_ref,
    g2_ref,
    go_ref,
    gq_ref,
    gk_ref,
    gv_ref,
    x_ref,
    wc,
    wbd,
    mixp,
    part,
    half_in,
    quarter_in,
    tot,
    mhalf_in,
    mquarter_in,
    grads,
    ybuf,
    zbuf,
    hidq,
    d_att,
    dq_ref,
    dk_ref,
    dv_ref,
    dqkv,
    xrows,
    gvec,
    gvec_in,
    msg,
    msg_in,
    acc,
    accd,
    ux,
    uc,
    w_sem,
    in_sem,
    load_sem,
    out_sem,
    x_send,
    x_recv,
    x_own,
    c_send,
    c_recv,
    c_own,
    mix_sem,
    ysem,
    yrsem,
    zsem,
    zrsem,
    vsem,
    vrsem,
    msem,
    mrsem,
    ssend,
    srecv,
):
    T, D = x_ref.shape
    A = all_x.shape[0]
    E, _, f = wg_ref.shape
    n_own = gg_ref.shape[0]
    chunks = T // CHUNK
    p = lax.axis_index("dp")
    t = lax.axis_index("tensor")
    xq = t // 2
    c = t % 2
    x_dev = (p, (1 - xq) * 2 + c)
    c_dev = (p, xq * 2 + 1 - c)
    f_dev = (p, (1 - xq) * 2 + 1 - c)
    trees = msg.shape[0]
    peers = [((p + j) % trees, t) for j in range(1, trees)]
    x_start, _, _, x_done, x_sent, x_pump, _ = gatherer(
        xf_ref, all_x, x_send, x_recv, x_own, 0, chunks, PART, BOTH
    )
    c_start, _, _, c_done, c_sent, c_pump, _ = gatherer(
        cf_ref, all_c, c_send, c_recv, c_own, EARLY, chunks, PART, BOTH
    )
    xb_load = pltpu.make_async_copy(xb_ref, x_ref, in_sem.at[0])
    xb_load.start()
    sync_with(peers + [x_dev, c_dev, f_dev])

    def pump(s):
        c_pump(s)
        x_pump(s)

    x_start(0)
    c_start(EARLY)

    first_own = p * n_own
    own_loads = [pltpu.make_async_copy(wd_ref.at[pl.ds(first_own, n_own)], wbd.at[0, pl.ds(0, n_own)], w_sem.at[0, 0])]
    for i in range(n_own):
        for h, src in enumerate((wg_ref, wu_ref)):
            dst = wc.at[0, :, pl.ds((h * n_own + i) * f, f)]
            own_loads.append(pltpu.make_async_copy(src.at[first_own + i], dst, w_sem.at[1 + 2 * i + h, 0]))

    def w_loads(i, slot):
        loads = [pltpu.make_async_copy(wd_ref.at[pl.ds(i * EG, EG)], wbd.at[slot], w_sem.at[0, slot])]
        for j in range(EG):
            for h, src in enumerate((wg_ref, wu_ref)):
                dst = wc.at[slot, :, pl.ds((h * EG + j) * f, f)]
                loads.append(pltpu.make_async_copy(src.at[i * EG + j], dst, w_sem.at[1 + 2 * j + h, slot]))
        return loads

    for copy in w_loads(0, 0):
        copy.start()
    part[...] = jnp.zeros_like(part)
    xb_load.wait()
    mixp[...] = jnp.zeros_like(mixp)
    groups = E // EG
    rows_at = T // 2
    lanes = g_ref.shape[1]

    def group_step(i, _):
        slot = i % 2

        @pl.when(i + 1 < groups)
        def _():
            for copy in w_loads(i + 1, 1 - slot):
                copy.start()

        @pl.when(i + 1 == groups)
        def _():
            for copy in own_loads:
                copy.start()

        @pl.when(i % 2 == 0)
        def _():
            pump(i // 2)

        for copy in w_loads(i, slot):
            copy.wait()
        wd = wbd[slot].reshape(EG * f, D)

        def rows_step(r, _):
            rows = pl.ds(pl.multiple_of(r * rows_at, 16), rows_at)
            turned = pltpu.roll(g_ref[rows, :], lanes - i * EG, 1)
            g = [turned[:, j : j + 1] for j in range(EG)]
            act, dgu = expert_core(x_ref[rows, :], c_ref[rows, :], g, wc[slot], wd)
            mixp[r] += dot(act, wd).reshape(2, rows_at // 2, D)
            part[r] += dot_t(dgu, wc[slot]).reshape(2, rows_at // 2, D)
            return 0

        lax.fori_loop(0, 2, rows_step, 0)
        return 0

    lax.fori_loop(0, groups, group_step, 0)

    acc[...] = jnp.zeros_like(acc)
    accd[...] = jnp.zeros_like(accd)

    Q = T // 4
    my_rows = pl.ds(pl.multiple_of(t * Q, 16), Q)
    hid_load = pltpu.make_async_copy(hid_ref.at[my_rows], hidq, in_sem.at[1])
    hid_load.start()
    xrows_load = pltpu.make_async_copy(xin_ref.at[my_rows], xrows, in_sem.at[2])
    xrows_load.start()
    xn_load = pltpu.make_async_copy(xn_ref, x_ref, in_sem.at[3])

    def summing(src, dst, i, dev):
        return pltpu.make_async_remote_copy(
            src_ref=src,
            dst_ref=dst,
            send_sem=ssend.at[i],
            recv_sem=srecv.at[i],
            device_id=dev,
            device_id_type=MESH,
        )

    sum_copies = [
        summing(part.at[:, 1 - c], half_in, 0, c_dev),
        summing(part.at[1 - xq, c], quarter_in, 1, x_dev),
        summing(tot.at[xq, c], tot.at[xq, c], 2, x_dev),
        summing(tot.at[:, c], tot.at[:, c], 3, c_dev),
    ]
    mix_copies = [
        summing(mixp.at[:, 1 - c], mhalf_in, 4, c_dev),
        summing(mixp.at[1 - xq, c], mquarter_in, 5, x_dev),
        summing(mixp.at[xq, c], mix_ref.at[xq, c], 6, x_dev),
        summing(mix_ref.at[:, c], mix_ref.at[:, c], 7, c_dev),
    ]
    mix_own = pltpu.make_async_copy(mixp.at[xq, c], mix_ref.at[xq, c], mix_sem)
    core_first = summing(part.at[:, 1 - c], half_in, 8, c_dev)
    x_first = summing(part.at[1 - xq, c], quarter_in, 9, x_dev)
    gx_out = pltpu.make_async_copy(hidq, gx_ref, in_sem.at[4])

    a = p // 2
    b = p % 2
    pieces, _, _, R, W = grads.shape
    y_dev = (a * 2 + 1 - b, t)

    def to_y(i):
        return send(grads.at[i, :, 1 - b], ybuf.at[i], ysem.at[i], yrsem.at[i], y_dev)

    def to_z(i):
        return [
            send(
                grads.at[i, (a + j) % A, b],
                zbuf.at[i, j - 1],
                zsem.at[i, j - 1],
                zrsem.at[i, j - 1],
                (((a + j) % A) * 2 + b, t),
            )
            for j in range(1, A)
        ]

    def y_done(i):
        to_y(i).wait()
        grads[i, :, b] += ybuf[i]
        for copy in to_z(i):
            copy.start()

    def z_done(i):
        for copy in to_z(i):
            copy.wait()
        whole = grads[i, a, b]
        for j in range(A - 1):
            whole += zbuf[i, j]
        return whole

    v_sends = [
        send(gvec, gvec_in.at[j], vsem.at[j], vrsem.at[j], dev) for j, dev in enumerate((x_dev, c_dev, f_dev))
    ]
    m_sends = [
        send(msg.at[dev[0]], msg_in.at[j], msem.at[j], mrsem.at[j], dev) for j, dev in enumerate(peers)
    ]

    first = groups // 2
    units = A // 4
    group_trees = A // units

    def part_of(ref, k, u):
        rows = pl.ds(pl.multiple_of(k * CHUNK, 8), CHUNK)
        return ref.at[pl.ds(u * group_trees, group_trees), :, rows]

    def load_x(k, u, slot):
        return pltpu.make_async_copy(part_of(all_x, k, u), ux.at[slot], load_sem.at[0, slot])

    def load_c(ref, k, u, slot):
        return pltpu.make_async_copy(part_of(ref, k, u), uc.at[slot], load_sem.at[1, slot])

    def load(k, u, slot):
        load_x(k, u, slot).start()

        @pl.when(k < EARLY)
        def _():
            load_c(early_ref, k, u, slot).start()

        @pl.when(k >= EARLY)
        def _():
            load_c(all_c, k, u, slot).start()

    for copy in own_loads:
        copy.wait()
    wdo = wbd[0, 0:n_own].reshape(n_own * f, D)

    def own_unit(k, u, slot):
        load_x(k, u, slot).wait()
        load_c(all_c, k, u, slot).wait()
        size = group_trees * 2 * CHUNK
        xs = ux[slot].reshape(size, D).astype(BF)
        cs = uc[slot].reshape(size, D).astype(BF)
        turned = og_ref[k, u].T
        g = [turned[:, j : j + 1] for j in range(n_own)]
        act, dgu = expert_core(xs, cs, g, wc[0, :, 0 : 2 * n_own * f], wdo)
        acc[...] += dot_l(xs, dgu)
        accd[...] += dot_l(act, cs)

    heads, _, hd = q_ref.shape
    group = heads // k_ref.shape[0]
    scale = hd ** (-0.5)
    dk_ref[...] = jnp.zeros_like(dk_ref)
    dv_ref[...] = jnp.zeros_like(dv_ref)

    def attention_back(h):
        g = h // group

        def block(i, _):
            rows = pl.ds(pl.multiple_of(i * Q, 16), Q)
            q = q_ref[h, rows, :]
            da = d_att[h, rows, :]
            lse = pltpu.roll(lse_ref[rows, :], lse_ref.shape[1] - h, 1)[:, 0:1]
            scores = dot_t(q, k_ref[g]) * scale + bias_ref[rows, :].astype(F32)
            probs = jnp.exp(scores - lse)
            d_probs = dot_t(da, v_ref[g])
            row_dot = jnp.sum(probs * d_probs, axis=-1, keepdims=True)
            d_scores = (probs * (d_probs - row_dot) * scale).astype(BF)
            dq_ref[h, rows, :] = dot(d_scores, k_ref[g])
            dk_ref[g] += dot_l(d_scores, q)
            dv_ref[g] += dot_l(probs.astype(BF), da)
            return 0

        lax.fori_loop(0, 4, block, 0)

    width = heads * hd
    kwidth = k_ref.shape[0] * hd

    def finish_start():
        lane = lax.broadcasted_iota(jnp.int32, (T, hd), 1)
        cosine = cos_ref[:, 0:hd]
        sine = jnp.where(lane < hd // 2, sin_ref[:, 0:hd], -sin_ref[:, 0:hd])

        def turned_back(d):
            swapped = jnp.concatenate([d[:, hd // 2 :], d[:, : hd // 2]], axis=1)
            return (d * cosine + swapped * sine).astype(BF)

        for h in range(heads):
            dqkv[:, h * hd : (h + 1) * hd] = turned_back(dq_ref[h])
        for g in range(k_ref.shape[0]):
            at = width + g * hd
            dqkv[:, at : at + hd] = turned_back(dk_ref[g])
            at = width + kwidth + g * hd
            dqkv[:, at : at + hd] = dv_ref[g].astype(BF)
        xn_load.wait()
        for i in range(width // W, pieces):
            at = (i - width // W) * W
            grads[i] = dot_l(x_ref[...], dqkv[:, at : at + W]).reshape(A, 2, R, W)
            to_y(i).start()
        for r in range(2):
            rows = pl.ds(r * 2 * Q, 2 * Q)
            total = dot_t(dqkv[rows, 0:width], wq_ref[...])
            total += dot_t(dqkv[rows, width : width + kwidth], wk_ref[...])
            total += dot_t(dqkv[rows, width + kwidth :], wv_ref[...])
            part[r] = total.reshape(2, Q, D)
        core_first.start()

    def slot_step(s, _):
        pump(s)

        @pl.when(s == first)
        def _():
            sum_copies[0].start()
            sum_copies[0].wait()
            part[:, c] += half_in[...]
            sum_copies[1].start()

        @pl.when(s == first + QUARTER_AT)
        def _():
            sum_copies[1].wait()
            hid_load.wait()
            hidden = hidq[...]
            inverse = lax.rsqrt(jnp.mean(hidden * hidden, axis=-1, keepdims=True) + epsilon)
            normal = hidden * inverse
            d_in = part[xq, c] + quarter_in[...]
            gvec[1:2, :] = jnp.sum(d_in * normal, axis=0, keepdims=True)
            scaled = d_in * gain_ref[...]
            tot[xq, c] = c_ref[my_rows, :].astype(F32) + inverse * (
                scaled - normal * jnp.mean(scaled * normal, axis=-1, keepdims=True)
            )
            sum_copies[2].start()

        @pl.when(s == first + SHARED_AT)
        def _():
            mix_copies[0].start()
            sum_copies[2].wait()
            sum_copies[3].start()
            sum_copies[3].wait()
            x_ref[...] = tot[...].reshape(T, D).astype(BF)
            for h in range(heads):
                w = wo_ref[h * hd : (h + 1) * hd, :]
                d_att[h] = dot_t(x_ref[...], w).astype(BF)
            for i in range(width // W):
                out_grad = dot_l(x_ref[...], att_ref[:, i * W : (i + 1) * W])
                grads[i] = out_grad.reshape(A, 2, R, W)
                to_y(i).start()
            xn_load.start()
            mix_copies[0].wait()
            mixp[:, c] += mhalf_in[...]

        @pl.when(s == first + SHARED_AT + 1)
        def _():
            for i in range(width // W):
                y_done(i)

        @pl.when(s == first + SHARED_AT + 2)
        def _():
            finish_start()
            core_first.wait()
            part[:, c] += half_in[...]
            x_first.start()

        @pl.when(s == first + SHARED_AT + 3)
        def _():
            for i in range(width // W, pieces):
                y_done(i)

        @pl.when(s == first + SHARED_AT + 4)
        def _():
            xrows_load.wait()
            x32 = xrows[...].astype(F32)
            inverse = lax.rsqrt(jnp.mean(x32 * x32, axis=-1, keepdims=True) + epsilon)
            normal = x32 * inverse
            x_first.wait()
            d_first = part[xq, c] + quarter_in[...]
            gvec[0:1, :] = jnp.sum(d_first * normal, axis=0, keepdims=True)
            for copy in v_sends:
                copy.start()
            scaled = d_first * gain1_ref[...]
            hidq[...] = tot[xq, c] + inverse * (
                scaled - normal * jnp.mean(scaled * normal, axis=-1, keepdims=True)
            )
            gx_out.start()

        @pl.when(s == first + MIX_AT)
        def _():
            mix_copies[1].start()

        @pl.when(s == first + MIX_AT + 2)
        def _():
            mix_copies[1].wait()
            mixp[xq, c] += mquarter_in[...]

        @pl.when(s == first + MIX_AT + 3)
        def _():
            mix_own.start()
            mix_copies[2].start()

        @pl.when(s == first + MIX_AT + 5)
        def _():
            mix_own.wait()
            mix_copies[2].wait()
            mix_copies[3].start()

        @pl.when(s == first + SHARED_AT + 5)
        def _():
            for copy in v_sends:
                copy.wait()
            total = gvec[0:2, :] + gvec_in[0, 0:2, :] + gvec_in[1, 0:2, :] + gvec_in[2, 0:2, :]
            for i in range(trees):
                msg[i, 0:2, :] = total[:, i * R : (i + 1) * R]
            for copy in m_sends:
                copy.start()

        @pl.when((s == first + SHARED_AT) | (s == first + SHARED_AT + 1))
        def _():
            attention_back((s - first - SHARED_AT) * 2)
            attention_back((s - first - SHARED_AT) * 2 + 1)

        k = s - LAG

        @pl.when((k >= 0) & (k < chunks))
        def _():
            x_done(k)

            @pl.when(k >= EARLY)
            def _():
                c_done(k)

            load(k, 0, 0)
            for u in range(units):
                if u + 1 < units:
                    load(k, u + 1, (u + 1) % 2)
                own_unit(k, u, u % 2)

        return 0

    lax.fori_loop(first, chunks + LAG, slot_step, 0)

    outs = []
    for j in range(n_own):
        outs += [
            pltpu.make_async_copy(acc.at[:, pl.ds(j * f, f)], gg_ref.at[j], out_sem.at[0, j]),
            pltpu.make_async_copy(acc.at[:, pl.ds((n_own + j) * f, f)], gu_ref.at[j], out_sem.at[1, j]),
            pltpu.make_async_copy(accd.at[pl.ds(j * f, f)], gd_ref.at[j], out_sem.at[2, j]),
        ]
    for copy in outs:
        copy.start()
    per = width // W
    for i in range(per):
        go_ref[:, i * W : (i + 1) * W] = z_done(i)
        gq_ref[:, i * W : (i + 1) * W] = z_done(per + i)
    gk_ref[...] = z_done(2 * per)
    gv_ref[...] = z_done(2 * per + 1)
    for copy in m_sends:
        copy.wait()
    mine = msg[p]
    for j in range(trees - 1):
        mine += msg_in[j]
    g1_ref[...] = mine[0:1]
    g2_ref[...] = mine[1:2]
    gx_out.wait()
    mix_copies[3].wait()

    def sends(k, _):
        x_sent(k)

        @pl.when(k >= EARLY)
        def _():
            c_sent(k)

        return 0

    lax.fori_loop(0, chunks, sends, 0)
    for copy in outs:
        copy.wait()


def experts(
    xf, cf, early, xb, c, dense_gates, own_gates, wg, wu, wd, hidden, x, xn, gain1, gain2, q, k, v, lse, bias,
    wo, att, wq, wk, wv, cosine, sine, trees,
):
    T, D = c.shape
    E, _, f = wg.shape
    own = E // trees
    chunks = T // CHUNK
    A = trees // 2
    Q = T // 4
    R = D // trees
    W = wk.shape[1]
    pieces = 2 * (wq.shape[1] // W) + 2
    gates_in = jnp.pad(dense_gates, ((0, 0), (0, 128 - E)))
    units = A // 4
    og = own_gates.reshape(units, trees // units, 8, chunks, CHUNK).transpose(3, 0, 2, 1, 4)
    og = og.reshape(chunks, units, 8, trees // units * CHUNK)
    slots = 2 if A > 4 else 1
    S = jax.ShapeDtypeStruct
    V = pltpu.VMEM
    out = pl.pallas_call(
        experts_kernel,
        in_specs=[HBM] * 4 + [VMEM] * 3 + [HBM] * 6 + [VMEM] * 14,
        out_specs=[HBM] * 7 + [VMEM] * 6,
        out_shape=[
            S((A, 2, T, D), F32),
            S((A, 2, T, D), F32),
            S((2, 2, Q, D), F32),
            S((Q, D), F32),
            S((own, D, f), F32),
            S((own, D, f), F32),
            S((own, f, D), F32),
            S((1, R), F32),
            S((1, R), F32),
            S((R, wq.shape[1]), F32),
            S((R, wq.shape[1]), F32),
            S((R, W), F32),
            S((R, W), F32),
        ],
        scratch_shapes=[
            V((T, D), BF),
            V((2, D, 2 * EG * f), BF),
            V((2, EG, f, D), BF),
            V((2, 2, Q, D), F32),
            V((2, 2, Q, D), F32),
            V((2, Q, D), F32),
            V((Q, D), F32),
            V((2, 2, Q, D), F32),
            V((2, Q, D), F32),
            V((Q, D), F32),
            V((pieces, A, 2, R, W), F32),
            V((pieces, A, R, W), F32),
            V((pieces, A - 1, R, W), F32),
            V((Q, D), F32),
            V(q.shape, BF),
            V(q.shape, F32),
            V(k.shape, F32),
            V(v.shape, F32),
            V((T, wq.shape[1] + 2 * W), BF),
            V((Q, D), BF),
            V((8, D), F32),
            V((3, 8, D), F32),
            V((trees, 8, R), F32),
            V((trees - 1, 8, R), F32),
            V((D, 2 * own * f), F32),
            V((own * f, D), F32),
            V((slots, 4, 2, CHUNK, D), F32),
            V((slots, 4, 2, CHUNK, D), F32),
            DMA((1 + 2 * EG, 2)),
            DMA((5,)),
            DMA((2, 2)),
            DMA((3, own)),
            DMA((4, chunks)),
            DMA((4, chunks)),
            DMA((2, chunks)),
            DMA((4, chunks - EARLY)),
            DMA((4, chunks - EARLY)),
            DMA((2, chunks - EARLY)),
            DMA(()),
            DMA((pieces,)),
            DMA((pieces,)),
            DMA((pieces, A - 1)),
            DMA((pieces, A - 1)),
            DMA((3,)),
            DMA((3,)),
            DMA((trees - 1,)),
            DMA((trees - 1,)),
            DMA((10,)),
            DMA((10,)),
        ],
        compiler_params=pltpu.CompilerParams(
            collective_id=0, has_side_effects=True, vmem_limit_bytes=62 * 2**20
        ),
    )(
        xf, cf, early, xb, c, gates_in, og, wg, wu, wd, hidden, x, xn, gain1.reshape(1, D), gain2.reshape(1, D),
        q, k, v, lse, bias, wo, att, wq, wk, wv, cosine, sine,
    )
    return out[2:]


def front_kernel(
    x_ref,
    c_ref,
    gain1_ref,
    gain2_ref,
    wq_ref,
    wk_ref,
    wv_ref,
    wo_ref,
    visible_ref,
    cos_ref,
    sin_ref,
    gates_ref,
    early_ref,
    cf_out,
    xn_out,
    bias_out,
    hidden_ref,
    xb_ref,
    xf_ref,
    att_out,
    q_ref,
    k_ref,
    v_ref,
    lse_ref,
    got_ref,
    cf_ref,
    xn_ref,
    bias_ref,
    att,
    others,
    wof,
    wr,
    hot,
    msg,
    peaks,
    ssem,
    rsem,
    wsend,
    wrecv,
    msend,
    mrecv,
    msem,
    c_send,
    c_recv,
    c_own,
    flush_sem,
):
    T, D = x_ref.shape
    trees = got_ref.shape[0]
    heads, _, hd = q_ref.shape
    kvs = k_ref.shape[0]
    group = heads // kvs
    width = heads * hd
    kwidth = kvs * hd
    scale = hd ** (-0.5)
    half = T // 2
    Q = T // 4
    p = lax.axis_index("dp")
    t = lax.axis_index("tensor")
    xq = t // 2
    c = t % 2
    x_dev = (p, (1 - xq) * 2 + c)
    c_dev = (p, xq * 2 + 1 - c)
    peers = [((p + j) % trees, t) for j in range(1, trees)]
    c_start, _, _, c_done, c_sent, pump, _ = gatherer(
        cf_ref, early_ref, c_send, c_recv, c_own, 0, EARLY, *EARLY_ROWS
    )
    sync_with(peers + [x_dev, c_dev])
    cf_ref[...] = c_ref[...].astype(F32)
    flushes = [
        pltpu.make_async_copy(one, two, flush_sem.at[i])
        for i, (one, two) in enumerate(((cf_ref, cf_out), (xn_ref, xn_out), (bias_ref, bias_out)))
    ]
    flushes[0].start()
    c_start(0)
    wof[t] = wo_ref[...].astype(F32)
    w_x = send(wof.at[t], wof.at[t], wsend.at[0], wrecv.at[0], x_dev)
    w_c = send(wof.at[t], wof.at[t], wsend.at[1], wrecv.at[1], c_dev)
    far = (1 - xq) * 2 + c
    w_on = send(wof.at[far], wof.at[far], wsend.at[2], wrecv.at[2], c_dev)
    w_x.start()
    w_c.start()

    row = lax.broadcasted_iota(jnp.int32, (width, width), 0)
    col = lax.broadcasted_iota(jnp.int32, (width, width), 1)
    low = (col % hd) < hd // 2
    turn = jnp.where(low & (row == col + hd // 2), -1.0, jnp.where(~low & (row == col - hd // 2), 1.0, 0.0))
    turn = turn.astype(BF)
    wr[:, :width] = dot(wq_ref[...], turn).astype(BF)
    wr[:, width:] = dot(wk_ref[...], turn[:kwidth, :kwidth]).astype(BF)

    token = lax.broadcasted_iota(jnp.int32, (T, 128), 0)
    seg = lax.broadcasted_iota(jnp.int32, (T, 128), 1)
    begin = jnp.where(seg == 0, 0, TRUNK + (seg - 1) * SEG)
    end = TRUNK + seg * SEG
    hot[...] = ((token >= begin) & (token < end)).astype(F32).astype(BF)

    def project(i, _):
        rows = pl.ds(pl.multiple_of(i * Q, 16), Q)
        x32 = x_ref[rows, :].astype(F32)
        inverse = lax.rsqrt(jnp.mean(x32 * x32, axis=-1, keepdims=True) + epsilon)
        xn = (x32 * inverse * gain1_ref[...]).astype(BF)
        xn_ref[rows, :] = xn
        cosine = cos_ref[rows, :]
        sine = sin_ref[rows, :]
        turned = dot(xn, wr[...])
        query = dot(xn, wq_ref[...])
        query = query * jnp.concatenate([cosine] * (width // 128), axis=1) + turned[:, :width] * jnp.concatenate(
            [sine] * (width // 128), axis=1
        )
        key = dot(xn, wk_ref[...]) * cosine + turned[:, width:] * sine
        value = dot(xn, wv_ref[...])
        for h in range(heads):
            q_ref[h, rows, :] = query[:, h * hd : (h + 1) * hd].astype(BF)
        for g in range(kvs):
            k_ref[g, rows, :] = key[:, g * hd : (g + 1) * hd].astype(BF)
            v_ref[g, rows, :] = value[:, g * hd : (g + 1) * hd].astype(BF)
        mine = hot[rows, :]
        reach = dot(mine, visible_ref[...]).astype(BF)
        near = dot_t(reach, hot[...]) > 0.5
        same = dot_t(mine, hot[...]) > 0.5
        qi = lax.broadcasted_iota(jnp.int32, (Q, T), 0) + i * Q
        kj = lax.broadcasted_iota(jnp.int32, (Q, T), 1)
        seen = near & (~same | (kj <= qi))
        bias_ref[rows, :] = jnp.where(seen, 0.0, -1e30).astype(BF)
        return 0

    lax.fori_loop(0, 4, project, 0)
    flushes[1].start()
    flushes[2].start()
    pump(0)
    peaks[...] = jnp.full_like(peaks, -1e30)
    lane = lax.broadcasted_iota(jnp.int32, (1, 128), 1)

    def attend(i, _):
        rows = pl.ds(pl.multiple_of(i * Q, 16), Q)
        bias = bias_ref[rows, :].astype(F32)
        for h in range(heads):
            g = h // group
            scores = dot_t(q_ref[h, rows, :], k_ref[g]) * scale + bias
            top = jnp.max(scores, axis=-1, keepdims=True)
            expo = jnp.exp(scores - top)
            total = jnp.sum(expo, axis=-1, keepdims=True)
            probs = (expo / total).astype(BF)
            out = dot(probs, v_ref[g]).astype(BF)
            att_out[rows, h * hd : (h + 1) * hd] = out
            att[rows, h * hd : (h + 1) * hd] = out.astype(F32)
            lse_ref[rows, h : h + 1] = top + jnp.log(total)
            peak = jnp.max(top, axis=0, keepdims=True)
            peaks[0:1, :] = jnp.maximum(peaks[0:1, :], jnp.where(lane == h, peak, -1e30))
        return 0

    rows = [pl.ds(i * half, half) for i in range(2)]
    to_x = [send(att.at[r], others.at[1, r], ssem.at[0, i], rsem.at[0, i], x_dev) for i, r in enumerate(rows)]
    to_c = [send(att.at[r], others.at[0, r], ssem.at[1, i], rsem.at[1, i], c_dev) for i, r in enumerate(rows)]
    on = [send(others.at[1, r], others.at[2, r], ssem.at[2, i], rsem.at[2, i], c_dev) for i, r in enumerate(rows)]
    lax.fori_loop(0, 2, attend, 0)
    to_x[0].start()
    to_c[0].start()
    pump(1)
    lax.fori_loop(2, 4, attend, 0)
    to_x[1].start()
    to_c[1].start()
    pump(2)
    msg[...] = gates_ref[...]
    msg[:, 7:8, 0:128] = jnp.broadcast_to(peaks[0:1, :][None], (trees, 1, 128))
    messages = [
        send(msg.at[dev[0]], got_ref.at[j], msend.at[j], mrecv.at[j], dev) for j, dev in enumerate(peers, 1)
    ]
    for copy in messages:
        copy.start()
    mine = pltpu.make_async_copy(msg.at[p], got_ref.at[0], msem)
    mine.start()
    w_x.wait()
    w_on.start()
    w_c.wait()

    def proj(block, owner):
        return dot(block.astype(BF), wof[owner].astype(BF))

    for i, r in enumerate(rows):
        hidden_ref[r, :] = x_ref[r, :].astype(F32) + proj(att[r, :], t)
    for i, r in enumerate(rows):
        to_c[i].wait()
        hidden_ref[r, :] += proj(others[0, r, :], xq * 2 + 1 - c)
    pump(3)
    for i, r in enumerate(rows):
        to_x[i].wait()
        on[i].start()
        hidden_ref[r, :] += proj(others[1, r, :], far)
    pump(4)
    w_on.wait()
    for i, r in enumerate(rows):
        on[i].wait()
        hidden = hidden_ref[r, :] + proj(others[2, r, :], (1 - xq) * 2 + 1 - c)
        hidden_ref[r, :] = hidden
        inverse = lax.rsqrt(jnp.mean(hidden * hidden, axis=-1, keepdims=True) + epsilon)
        low_x = (hidden * inverse * gain2_ref[...]).astype(BF)
        xb_ref[r, :] = low_x
        xf_ref[r, :] = low_x.astype(F32)
    for copy in messages:
        copy.wait()
    mine.wait()
    for s in range(5, EARLY + 3):
        pump(s)
    for copy in flushes:
        copy.wait()
    for k in range(EARLY):
        c_done(k)
        c_sent(k)


def front(x, c, gain1, gain2, wq, wk, wv, wo, visible, cosine, sine, gates_out):
    T, D = x.shape
    trees = gates_out.shape[0]
    A = trees // 2
    heads = wq.shape[1] // HEAD_DIM
    kvs = wk.shape[1] // HEAD_DIM
    width = wq.shape[1]
    S = jax.ShapeDtypeStruct
    V = pltpu.VMEM
    return pl.pallas_call(
        front_kernel,
        in_specs=[VMEM] * 12,
        out_specs=[HBM] * 4 + [VMEM] * 9,
        out_shape=[
            S((A, 2, T, D), F32),
            S((T, D), F32),
            S((T, D), BF),
            S((T, T), BF),
            S((T, D), F32),
            S((T, D), BF),
            S((T, D), F32),
            S((T, width), BF),
            S((heads, T, HEAD_DIM), BF),
            S((kvs, T, HEAD_DIM), BF),
            S((kvs, T, HEAD_DIM), BF),
            S((T, 128), F32),
            S(gates_out.shape, F32),
        ],
        scratch_shapes=[
            V((T, D), F32),
            V((T, D), BF),
            V((T, T), BF),
            V((T, width), F32),
            V((3, T, width), F32),
            V((4, width, D), F32),
            V((D, width + wk.shape[1]), BF),
            V((T, 128), BF),
            V(gates_out.shape, F32),
            V((8, 128), F32),
            DMA((3, 2)),
            DMA((3, 2)),
            DMA((3,)),
            DMA((3,)),
            DMA((trees,)),
            DMA((trees,)),
            DMA(()),
            DMA((4, EARLY)),
            DMA((4, EARLY)),
            DMA((2, EARLY)),
            DMA((3,)),
        ],
        compiler_params=pltpu.CompilerParams(
            collective_id=1, has_side_effects=True, vmem_limit_bytes=58 * 2**20
        ),
    )(x, c, gain1.reshape(1, D), gain2.reshape(1, D), wq, wk, wv, wo, visible, cosine, sine, gates_out)


def last_kernel(hid_ref, mix_ref, got_ref, limit_ref, wq_ref, wk_ref, *refs):
    n = (len(refs) - 9) // 3
    out_ref, factor_ref, qs_ref, ks_ref = refs[n : n + 4]
    hid, mix, held = refs[2 * n + 4], refs[2 * n + 5], refs[2 * n + 6 : 3 * n + 6]
    in_sem, sem, big_sem = refs[3 * n + 6 :]
    big = [pltpu.make_async_copy(hid_ref, hid, big_sem.at[0]), pltpu.make_async_copy(mix_ref, mix, big_sem.at[1])]
    ins = [pltpu.make_async_copy(refs[i], held[i], in_sem.at[i]) for i in range(n)]
    outs = [pltpu.make_async_copy(held[i], refs[n + 4 + i], sem.at[i]) for i in range(n)]
    for copy in big + ins:
        copy.start()
    heads = limit_ref.shape[1]
    limits = limit_ref[...]
    peaks = jnp.max(got_ref[:, 7, 0:128], axis=0, keepdims=True)[:, 0:heads]
    factors = limits / jnp.maximum(peaks, limits)
    factor_ref[...] = factors
    group = wq_ref.shape[1] // wk_ref.shape[1]
    roots = [jnp.sqrt(factors[:, h : h + 1]) for h in range(heads)]
    least = [
        jnp.sqrt(jnp.min(factors[:, g * group : (g + 1) * group], axis=1, keepdims=True)) for g in range(heads // group)
    ]

    def scaled(w_ref, values):
        head = lax.broadcasted_iota(jnp.int32, (1, w_ref.shape[1]), 1) // HEAD_DIM
        row = jnp.zeros((1, w_ref.shape[1]), F32)
        for h, value in enumerate(values):
            row = jnp.where(head == h, value, row)
        return (w_ref[...].astype(F32) * row).astype(BF)

    qs_ref[...] = scaled(wq_ref, roots)
    ks_ref[...] = scaled(wk_ref, least)
    for copy in big:
        copy.wait()
    out_ref[...] = (hid[...] + mix[...]).astype(BF)
    for i in range(n):
        ins[i].wait()
        outs[i].start()
    for copy in outs:
        copy.wait()


def last(hidden, mixture, got, limits, wq, wk, *rest):
    T, D = hidden.shape
    S = jax.ShapeDtypeStruct
    n = len(rest)
    return pl.pallas_call(
        last_kernel,
        in_specs=[HBM] * 2 + [VMEM] * 4 + [HBM] * n,
        out_specs=[VMEM] * 4 + [HBM] * n,
        out_shape=[
            S((T, D), BF),
            S((1, limits.shape[0]), F32),
            S(wq.shape, BF),
            S(wk.shape, BF),
        ]
        + [S(r.shape, r.dtype) for r in rest],
        scratch_shapes=[pltpu.VMEM((T, D), F32)] * 2
        + [pltpu.VMEM(r.shape, r.dtype) for r in rest]
        + [DMA((n,)), DMA((n,)), DMA((2,))],
        compiler_params=pltpu.CompilerParams(vmem_limit_bytes=62 * 2**20),
    )(hidden, mixture.reshape(T, D), got, limits.reshape(1, -1), wq, wk, *rest)


def local(
    block_input,
    norm_first,
    norm_second,
    w_query,
    w_key,
    w_value,
    w_out,
    w_gate,
    w_up,
    w_down,
    routes,
    gates,
    parents,
    clip_limits,
    cotangent,
):
    count, width = block_input.shape
    head_dim = HEAD_DIM
    query_cols = w_query.shape[1]
    key_cols = w_key.shape[1]
    query_heads = query_cols // head_dim
    kv_heads = key_cols // head_dim
    trees = lax.axis_size("dp")
    own = EXPERTS // trees
    position, visible = tree_tables(parents[0], count)
    visible = jnp.pad(visible.astype(jnp.bfloat16), ((0, 128 - SEGS), (0, 128 - SEGS)))
    cosine, sine = rotary_tables(position, head_dim)
    wide_cosine = jnp.tile(cosine[:, 0], (1, 128 * 2 // head_dim))
    wide_sine = jnp.tile(sine[:, 0], (1, 128 * 2 // head_dim))
    routed = routes[:, :, None] == jnp.arange(EXPERTS, dtype=jnp.int32)[None, None, :]
    dense_gates = jnp.sum(jnp.where(routed, gates[:, :, None], 0.0), axis=1)
    gates_out = jnp.pad(dense_gates.T.reshape(trees, own, count), ((0, 0), (0, 8 - own), (0, 0)))
    (
        early,
        c_wide,
        input_first,
        bias,
        hidden,
        input_second,
        x_wide,
        attended_parts,
        queries,
        keys,
        values,
        log_norms,
        got,
    ) = front(
        block_input,
        cotangent,
        norm_first,
        norm_second,
        w_query,
        w_key,
        w_value,
        w_out,
        visible,
        wide_cosine,
        wide_sine,
        gates_out,
    )
    order = (lax.axis_index("dp") - jnp.arange(trees)) % trees
    hot = (order[:, None] == jnp.arange(trees)[None, :]).astype(jnp.float32)
    own_gates = jnp.sum(hot[:, :, None, None] * got[:, None], axis=0)
    (
        mixture,
        grad_x,
        gate_shard,
        up_shard,
        down_shard,
        first_gain_grad,
        second_shard,
        out_shard,
        query_shard,
        key_shard,
        value_shard,
    ) = experts(
        x_wide,
        c_wide,
        early,
        input_second,
        cotangent,
        dense_gates,
        own_gates,
        w_gate,
        w_up,
        w_down,
        hidden,
        block_input,
        input_first,
        norm_first,
        norm_second,
        queries,
        keys,
        values,
        log_norms,
        bias,
        w_out,
        attended_parts,
        w_query,
        w_key,
        w_value,
        wide_cosine,
        wide_sine,
        trees,
    )
    block_out, factors, query_scaled, key_scaled, *rest = last(
        hidden,
        mixture,
        got,
        clip_limits,
        w_query,
        w_key,
        grad_x,
        first_gain_grad,
        second_shard,
        query_shard,
        key_shard,
        value_shard,
        out_shard,
        gate_shard,
        up_shard,
        down_shard,
    )
    grad_x, first_gain_grad, second_shard = rest[:3]
    return (
        block_out,
        grad_x,
        first_gain_grad.reshape(width // trees),
        second_shard.reshape(width // trees),
        *rest[3:],
        factors.reshape(query_heads),
        query_scaled,
        key_scaled,
    )


def solution(mesh):
    placed = (
        P("dp", None),
        P(),
        P(),
        P(None, "tensor"),
        P(None, "tensor"),
        P(None, "tensor"),
        P("tensor", None),
        P(None, None, "tensor"),
        P(None, None, "tensor"),
        P(None, "tensor", None),
        P("dp", None),
        P("dp", None),
        P("dp", None),
        P("tensor"),
        P("dp", None),
    )
    return jax.shard_map(
        local,
        mesh=mesh,
        in_specs=placed,
        out_specs=(
            P("dp", None),
            P(("dp", "tensor"), None),
            P("dp"),
            P("dp"),
            P("dp", "tensor"),
            P("dp", "tensor"),
            P("dp", "tensor"),
            P("dp", "tensor"),
            P("dp", None, "tensor"),
            P("dp", None, "tensor"),
            P("dp", "tensor", None),
            P("tensor"),
            P(None, "tensor"),
            P(None, "tensor"),
        ),
        check_vma=False,
    )
```

```python
import functools

import jax
import jax.numpy as jnp
from jax import lax
from jax.experimental import pallas as pl
from jax.experimental.pallas import tpu as pltpu
from jax.sharding import PartitionSpec as P

HEAD_DIM = 64
EXPERTS = 32
TOPK = 8
TRUNK = 256
SEG = 48
SEGS = 13


epsilon = 1e-06
theta_base = 10000.0
expert_group = 4


def tree_tables(parent_row, count):
    slot_ids = jnp.arange(SEGS, dtype=jnp.int32)
    safe_parent = jnp.maximum(parent_row, 0)
    hot_parent = (safe_parent[:, None] == slot_ids[None, :]).astype(jnp.int32)
    grand_raw = jnp.sum(hot_parent * parent_row[None, :], axis=1)
    grand_parent = jnp.where(parent_row >= 0, grand_raw, -1)
    visible = (
        (slot_ids[:, None] == slot_ids[None, :])
        | (slot_ids[None, :] == parent_row[:, None])
        | (slot_ids[None, :] == grand_parent[:, None])
    )
    depth = (parent_row >= 0).astype(jnp.int32) + (grand_parent >= 0).astype(jnp.int32)
    token_ids = jnp.arange(count, dtype=jnp.int32)
    segment = jnp.where(token_ids < TRUNK, 0, 1 + (token_ids - TRUNK) // SEG)
    local_index = jnp.where(token_ids < TRUNK, token_ids, (token_ids - TRUNK) % SEG)
    seg_match = segment[:, None] == slot_ids[None, :]
    token_depth = jnp.sum(seg_match.astype(jnp.int32) * depth[None, :], axis=1)
    position = jnp.where(segment == 0, token_ids, TRUNK + (token_depth - 1) * SEG + local_index)
    return position, visible


def rotary_tables(position, head_dim):
    half = head_dim // 2
    inverse = theta_base ** (-(jnp.arange(half, dtype=jnp.float32) * 2.0 / head_dim))
    angle = position.astype(jnp.float32)[:, None] * inverse[None, :]
    return (jnp.cos(angle)[:, None, :], jnp.sin(angle)[:, None, :])


F32 = jnp.float32
BF = jnp.bfloat16
MESH = pl.DeviceIdType.MESH
CHUNK = 64
PART = 8
BOTH = 16
EG = 4
LAG = 4
EARLY = 2
QUARTER_AT = 3
SHARED_AT = 6
MIX_AT = 6
EARLY_ROWS = (0, 32)


def dot(a, b):
    return jnp.dot(a, b, preferred_element_type=F32)


def dot_t(a, b):
    return lax.dot_general(a, b, (((1,), (1,)), ((), ())), preferred_element_type=F32)


def dot_l(a, b):
    return lax.dot_general(a, b, (((0,), (0,)), ((), ())), preferred_element_type=F32)


def expert_core(x, c, g, wcat, wdcat):
    n = len(g)
    f = wdcat.shape[0]
    both = dot(x, wcat)
    gate = both[:, :f]
    up = both[:, f:]
    d_act = dot_t(c, wdcat)
    wide = jnp.concatenate([jnp.broadcast_to(v, (x.shape[0], f // n)) for v in g], axis=1)
    sigma = jax.nn.sigmoid(gate)
    silu = gate * sigma
    act = ((silu * up).astype(BF).astype(F32) * wide).astype(BF)
    d_act = d_act * wide
    d_gate = (d_act * up * (sigma + silu * (1.0 - sigma))).astype(BF)
    d_up = (d_act * silu).astype(BF)
    return act, jnp.concatenate([d_gate, d_up], axis=1)


VMEM = pl.BlockSpec(memory_space=pltpu.VMEM)
HBM = pl.BlockSpec(memory_space=pl.ANY)
DMA = pltpu.SemaphoreType.DMA


def sync_with(devices):
    barrier = pltpu.get_barrier_semaphore()
    for dev in devices:
        pl.semaphore_signal(barrier, inc=1, device_id=dev, device_id_type=MESH)
    pl.semaphore_wait(barrier, len(devices))


def send(src, dst, out_sem, in_sem, dev):
    return pltpu.make_async_remote_copy(
        src_ref=src,
        dst_ref=dst,
        send_sem=out_sem,
        recv_sem=in_sem,
        device_id=dev,
        device_id_type=MESH,
    )


def gatherer(src, dst, send_sem, recv_sem, own_sem, first, last, part, both):
    A = dst.shape[0]
    p = lax.axis_index("dp")
    t = lax.axis_index("tensor")
    a = p // 2
    b = p % 2
    xq = t // 2
    c = t % 2
    y_dev = (a * 2 + 1 - b, t)
    x_dev = (p, (1 - xq) * 2 + c)
    c_dev = (p, xq * 2 + 1 - c)
    z_devs = [(((a + j) % A) * 2 + b, t) for j in range(1, A)]

    def rows1(k):
        return pl.ds(pl.multiple_of(k * CHUNK + (c * 2 + xq) * part, 8), part)

    def rows_pair(k):
        return pl.ds(pl.multiple_of(k * CHUNK + c * 2 * part, 8), 2 * part)

    def rows2(k):
        return pl.ds(pl.multiple_of(k * CHUNK + 4 * part + c * both, 8), both)

    def mine(k):
        return [rows1(k), rows2(k)] if part and both else [rows1(k)] if part else [rows2(k)]

    def of_core(k):
        return [rows_pair(k), rows2(k)] if part and both else [rows_pair(k)] if part else [rows2(k)]

    def remote(one, two, stage, k, dev):
        return pltpu.make_async_remote_copy(
            src_ref=one,
            dst_ref=two,
            send_sem=send_sem.at[stage, k - first],
            recv_sem=recv_sem.at[stage, k - first],
            device_id=dev,
            device_id_type=MESH,
        )

    sizes = [
        dst.at[pl.ds(0, A - 1), 0, pl.ds(0, part + both)],
        dst.at[:, 0, pl.ds(0, part + both)],
        dst.at[:, :, pl.ds(0, max(part, 8))],
        dst.at[:, :, pl.ds(0, 2 * part + both)],
    ]

    def took(stage, k, sem):
        pltpu.make_async_copy(sizes[stage], sizes[stage], sem.at[stage, k - first]).wait()

    def own(k, i):
        rows = mine(k)[i]
        return pltpu.make_async_copy(src.at[rows], dst.at[a, b, rows], own_sem.at[i, k - first])

    def start(k):
        for i, rows in enumerate(mine(k)):
            for dev in z_devs:
                remote(src.at[rows], dst.at[a, b, rows], 0, k, dev).start()
            own(k, i).start()

    def second(k):
        took(0, k, recv_sem)
        for i, rows in enumerate(mine(k)):
            own(k, i).wait()
            remote(dst.at[:, b, rows], dst.at[:, b, rows], 1, k, y_dev).start()

    def to_core(k):
        for rows in of_core(k):
            remote(dst.at[:, :, rows], dst.at[:, :, rows], 3, k, c_dev).start()

    def third(k):
        took(1, k, recv_sem)
        if not part:
            to_core(k)
            return
        rows = rows1(k)
        remote(dst.at[:, :, rows], dst.at[:, :, rows], 2, k, x_dev).start()

    def fourth(k):
        took(2, k, recv_sem)
        to_core(k)

    def done(k):
        took(3, k, recv_sem)

    def sent(k):
        for stage in (0, 1, 2, 3) if part else (0, 1, 3):
            took(stage, k, send_sem)

    def pump(s):
        steps = ((3, fourth), (2, third), (1, second), (-1, start))
        for back, stage in steps if part else steps[1:]:
            k = first + s - back
            if isinstance(s, int):
                if first <= k < last:
                    stage(k)
            else:

                @pl.when((k >= first) & (k < last))
                def _(k=k, stage=stage):
                    stage(k)

    return start, second, third, done, sent, pump, z_devs + [y_dev, x_dev, c_dev]


def experts_kernel(
    xf_ref,
    cf_ref,
    early_ref,
    xb_ref,
    c_ref,
    g_ref,
    og_ref,
    wg_ref,
    wu_ref,
    wd_ref,
    hid_ref,
    xin_ref,
    xn_ref,
    gain1_ref,
    gain_ref,
    q_ref,
    k_ref,
    v_ref,
    lse_ref,
    bias_ref,
    wo_ref,
    att_ref,
    wq_ref,
    wk_ref,
    wv_ref,
    cos_ref,
    sin_ref,
    all_x,
    all_c,
    mix_ref,
    gx_ref,
    gg_ref,
    gu_ref,
    gd_ref,
    g1_ref,
    g2_ref,
    go_ref,
    gq_ref,
    gk_ref,
    gv_ref,
    x_ref,
    wc,
    wbd,
    mixp,
    part,
    half_in,
    quarter_in,
    tot,
    mhalf_in,
    mquarter_in,
    grads,
    ybuf,
    zbuf,
    hidq,
    d_att,
    dq_ref,
    dk_ref,
    dv_ref,
    dqkv,
    xrows,
    gvec,
    gvec_in,
    msg,
    msg_in,
    acc,
    accd,
    ux,
    uc,
    w_sem,
    in_sem,
    load_sem,
    out_sem,
    x_send,
    x_recv,
    x_own,
    c_send,
    c_recv,
    c_own,
    mix_sem,
    ysem,
    yrsem,
    zsem,
    zrsem,
    vsem,
    vrsem,
    msem,
    mrsem,
    ssend,
    srecv,
):
    T, D = x_ref.shape
    A = all_x.shape[0]
    E, _, f = wg_ref.shape
    n_own = gg_ref.shape[0]
    chunks = T // CHUNK
    p = lax.axis_index("dp")
    t = lax.axis_index("tensor")
    xq = t // 2
    c = t % 2
    x_dev = (p, (1 - xq) * 2 + c)
    c_dev = (p, xq * 2 + 1 - c)
    f_dev = (p, (1 - xq) * 2 + 1 - c)
    trees = msg.shape[0]
    peers = [((p + j) % trees, t) for j in range(1, trees)]
    x_start, _, _, x_done, x_sent, x_pump, _ = gatherer(
        xf_ref, all_x, x_send, x_recv, x_own, 0, chunks, PART, BOTH
    )
    c_start, _, _, c_done, c_sent, c_pump, _ = gatherer(
        cf_ref, all_c, c_send, c_recv, c_own, EARLY, chunks, PART, BOTH
    )
    xb_load = pltpu.make_async_copy(xb_ref, x_ref, in_sem.at[0])
    xb_load.start()
    sync_with(peers + [x_dev, c_dev, f_dev])

    def pump(s):
        c_pump(s)
        x_pump(s)

    x_start(0)
    c_start(EARLY)

    first_own = p * n_own
    own_loads = [pltpu.make_async_copy(wd_ref.at[pl.ds(first_own, n_own)], wbd.at[0, pl.ds(0, n_own)], w_sem.at[0, 0])]
    for i in range(n_own):
        for h, src in enumerate((wg_ref, wu_ref)):
            dst = wc.at[0, :, pl.ds((h * n_own + i) * f, f)]
            own_loads.append(pltpu.make_async_copy(src.at[first_own + i], dst, w_sem.at[1 + 2 * i + h, 0]))

    def w_loads(i, slot):
        loads = [pltpu.make_async_copy(wd_ref.at[pl.ds(i * EG, EG)], wbd.at[slot], w_sem.at[0, slot])]
        for j in range(EG):
            for h, src in enumerate((wg_ref, wu_ref)):
                dst = wc.at[slot, :, pl.ds((h * EG + j) * f, f)]
                loads.append(pltpu.make_async_copy(src.at[i * EG + j], dst, w_sem.at[1 + 2 * j + h, slot]))
        return loads

    for copy in w_loads(0, 0):
        copy.start()
    part[...] = jnp.zeros_like(part)
    xb_load.wait()
    mixp[...] = jnp.zeros_like(mixp)
    groups = E // EG
    rows_at = T // 2
    lanes = g_ref.shape[1]

    def group_step(i, _):
        slot = i % 2

        @pl.when(i + 1 < groups)
        def _():
            for copy in w_loads(i + 1, 1 - slot):
                copy.start()

        @pl.when(i + 1 == groups)
        def _():
            for copy in own_loads:
                copy.start()

        @pl.when(i % 2 == 0)
        def _():
            pump(i // 2)

        for copy in w_loads(i, slot):
            copy.wait()
        wd = wbd[slot].reshape(EG * f, D)

        def rows_step(r, _):
            rows = pl.ds(pl.multiple_of(r * rows_at, 16), rows_at)
            turned = pltpu.roll(g_ref[rows, :], lanes - i * EG, 1)
            g = [turned[:, j : j + 1] for j in range(EG)]
            act, dgu = expert_core(x_ref[rows, :], c_ref[rows, :], g, wc[slot], wd)
            mixp[r] += dot(act, wd).reshape(2, rows_at // 2, D)
            part[r] += dot_t(dgu, wc[slot]).reshape(2, rows_at // 2, D)
            return 0

        lax.fori_loop(0, 2, rows_step, 0)
        return 0

    lax.fori_loop(0, groups, group_step, 0)

    acc[...] = jnp.zeros_like(acc)
    accd[...] = jnp.zeros_like(accd)

    Q = T // 4
    my_rows = pl.ds(pl.multiple_of(t * Q, 16), Q)
    hid_load = pltpu.make_async_copy(hid_ref.at[my_rows], hidq, in_sem.at[1])
    hid_load.start()
    xrows_load = pltpu.make_async_copy(xin_ref.at[my_rows], xrows, in_sem.at[2])
    xrows_load.start()
    xn_load = pltpu.make_async_copy(xn_ref, x_ref, in_sem.at[3])

    def summing(src, dst, i, dev):
        return pltpu.make_async_remote_copy(
            src_ref=src,
            dst_ref=dst,
            send_sem=ssend.at[i],
            recv_sem=srecv.at[i],
            device_id=dev,
            device_id_type=MESH,
        )

    sum_copies = [
        summing(part.at[:, 1 - c], half_in, 0, c_dev),
        summing(part.at[1 - xq, c], quarter_in, 1, x_dev),
        summing(tot.at[xq, c], tot.at[xq, c], 2, x_dev),
        summing(tot.at[:, c], tot.at[:, c], 3, c_dev),
    ]
    mix_copies = [
        summing(mixp.at[:, 1 - c], mhalf_in, 4, c_dev),
        summing(mixp.at[1 - xq, c], mquarter_in, 5, x_dev),
        summing(mixp.at[xq, c], mix_ref.at[xq, c], 6, x_dev),
        summing(mix_ref.at[:, c], mix_ref.at[:, c], 7, c_dev),
    ]
    mix_own = pltpu.make_async_copy(mixp.at[xq, c], mix_ref.at[xq, c], mix_sem)
    core_first = summing(part.at[:, 1 - c], half_in, 8, c_dev)
    x_first = summing(part.at[1 - xq, c], quarter_in, 9, x_dev)
    gx_out = pltpu.make_async_copy(hidq, gx_ref, in_sem.at[4])

    a = p // 2
    b = p % 2
    pieces, _, _, R, W = grads.shape
    y_dev = (a * 2 + 1 - b, t)

    def to_y(i):
        return send(grads.at[i, :, 1 - b], ybuf.at[i], ysem.at[i], yrsem.at[i], y_dev)

    def to_z(i):
        return [
            send(
                grads.at[i, (a + j) % A, b],
                zbuf.at[i, j - 1],
                zsem.at[i, j - 1],
                zrsem.at[i, j - 1],
                (((a + j) % A) * 2 + b, t),
            )
            for j in range(1, A)
        ]

    def y_done(i):
        to_y(i).wait()
        grads[i, :, b] += ybuf[i]
        for copy in to_z(i):
            copy.start()

    def z_done(i):
        for copy in to_z(i):
            copy.wait()
        whole = grads[i, a, b]
        for j in range(A - 1):
            whole += zbuf[i, j]
        return whole

    v_sends = [
        send(gvec, gvec_in.at[j], vsem.at[j], vrsem.at[j], dev) for j, dev in enumerate((x_dev, c_dev, f_dev))
    ]
    m_sends = [
        send(msg.at[dev[0]], msg_in.at[j], msem.at[j], mrsem.at[j], dev) for j, dev in enumerate(peers)
    ]

    first = groups // 2
    units = A // 4
    group_trees = A // units

    def part_of(ref, k, u):
        rows = pl.ds(pl.multiple_of(k * CHUNK, 8), CHUNK)
        return ref.at[pl.ds(u * group_trees, group_trees), :, rows]

    def load_x(k, u, slot):
        return pltpu.make_async_copy(part_of(all_x, k, u), ux.at[slot], load_sem.at[0, slot])

    def load_c(ref, k, u, slot):
        return pltpu.make_async_copy(part_of(ref, k, u), uc.at[slot], load_sem.at[1, slot])

    def load(k, u, slot):
        load_x(k, u, slot).start()

        @pl.when(k < EARLY)
        def _():
            load_c(early_ref, k, u, slot).start()

        @pl.when(k >= EARLY)
        def _():
            load_c(all_c, k, u, slot).start()

    for copy in own_loads:
        copy.wait()
    wdo = wbd[0, 0:n_own].reshape(n_own * f, D)

    def own_unit(k, u, slot):
        load_x(k, u, slot).wait()
        load_c(all_c, k, u, slot).wait()
        size = group_trees * 2 * CHUNK
        xs = ux[slot].reshape(size, D).astype(BF)
        cs = uc[slot].reshape(size, D).astype(BF)
        turned = og_ref[k, u].T
        g = [turned[:, j : j + 1] for j in range(n_own)]
        act, dgu = expert_core(xs, cs, g, wc[0, :, 0 : 2 * n_own * f], wdo)
        acc[...] += dot_l(xs, dgu)
        accd[...] += dot_l(act, cs)

    heads, _, hd = q_ref.shape
    group = heads // k_ref.shape[0]
    scale = hd ** (-0.5)
    dk_ref[...] = jnp.zeros_like(dk_ref)
    dv_ref[...] = jnp.zeros_like(dv_ref)

    def attention_back(h):
        g = h // group

        def block(i, _):
            rows = pl.ds(pl.multiple_of(i * Q, 16), Q)
            q = q_ref[h, rows, :]
            da = d_att[h, rows, :]
            lse = pltpu.roll(lse_ref[rows, :], lse_ref.shape[1] - h, 1)[:, 0:1]
            scores = dot_t(q, k_ref[g]) * scale + bias_ref[rows, :].astype(F32)
            probs = jnp.exp(scores - lse)
            d_probs = dot_t(da, v_ref[g])
            row_dot = jnp.sum(probs * d_probs, axis=-1, keepdims=True)
            d_scores = (probs * (d_probs - row_dot) * scale).astype(BF)
            dq_ref[h, rows, :] = dot(d_scores, k_ref[g])
            dk_ref[g] += dot_l(d_scores, q)
            dv_ref[g] += dot_l(probs.astype(BF), da)
            return 0

        lax.fori_loop(0, 4, block, 0)

    width = heads * hd
    kwidth = k_ref.shape[0] * hd

    def finish_start():
        lane = lax.broadcasted_iota(jnp.int32, (T, hd), 1)
        cosine = cos_ref[:, 0:hd]
        sine = jnp.where(lane < hd // 2, sin_ref[:, 0:hd], -sin_ref[:, 0:hd])

        def turned_back(d):
            swapped = jnp.concatenate([d[:, hd // 2 :], d[:, : hd // 2]], axis=1)
            return (d * cosine + swapped * sine).astype(BF)

        for h in range(heads):
            dqkv[:, h * hd : (h + 1) * hd] = turned_back(dq_ref[h])
        for g in range(k_ref.shape[0]):
            at = width + g * hd
            dqkv[:, at : at + hd] = turned_back(dk_ref[g])
            at = width + kwidth + g * hd
            dqkv[:, at : at + hd] = dv_ref[g].astype(BF)
        xn_load.wait()
        for i in range(width // W, pieces):
            at = (i - width // W) * W
            grads[i] = dot_l(x_ref[...], dqkv[:, at : at + W]).reshape(A, 2, R, W)
            to_y(i).start()
        for r in range(2):
            rows = pl.ds(r * 2 * Q, 2 * Q)
            total = dot_t(dqkv[rows, 0:width], wq_ref[...])
            total += dot_t(dqkv[rows, width : width + kwidth], wk_ref[...])
            total += dot_t(dqkv[rows, width + kwidth :], wv_ref[...])
            part[r] = total.reshape(2, Q, D)
        core_first.start()

    def slot_step(s, _):
        pump(s)

        k = s - LAG

        @pl.when((k >= 0) & (k < chunks))
        def _():
            x_done(k)

            @pl.when(k >= EARLY)
            def _():
                c_done(k)

            load(k, 0, 0)

        @pl.when(s == first)
        def _():
            sum_copies[0].start()
            sum_copies[0].wait()
            part[:, c] += half_in[...]
            sum_copies[1].start()

        @pl.when(s == first + QUARTER_AT)
        def _():
            sum_copies[1].wait()
            hid_load.wait()
            hidden = hidq[...]
            inverse = lax.rsqrt(jnp.mean(hidden * hidden, axis=-1, keepdims=True) + epsilon)
            normal = hidden * inverse
            d_in = part[xq, c] + quarter_in[...]
            gvec[1:2, :] = jnp.sum(d_in * normal, axis=0, keepdims=True)
            scaled = d_in * gain_ref[...]
            tot[xq, c] = c_ref[my_rows, :].astype(F32) + inverse * (
                scaled - normal * jnp.mean(scaled * normal, axis=-1, keepdims=True)
            )
            sum_copies[2].start()

        @pl.when(s == first + SHARED_AT)
        def _():
            mix_copies[0].start()
            sum_copies[2].wait()
            sum_copies[3].start()
            sum_copies[3].wait()
            x_ref[...] = tot[...].reshape(T, D).astype(BF)
            for h in range(heads):
                w = wo_ref[h * hd : (h + 1) * hd, :]
                d_att[h] = dot_t(x_ref[...], w).astype(BF)
            for i in range(width // W):
                out_grad = dot_l(x_ref[...], att_ref[:, i * W : (i + 1) * W])
                grads[i] = out_grad.reshape(A, 2, R, W)
                to_y(i).start()
            xn_load.start()
            mix_copies[0].wait()
            mixp[:, c] += mhalf_in[...]

        @pl.when(s == first + SHARED_AT + 1)
        def _():
            for i in range(width // W):
                y_done(i)

        @pl.when(s == first + SHARED_AT + 2)
        def _():
            finish_start()
            core_first.wait()
            part[:, c] += half_in[...]
            x_first.start()

        @pl.when(s == first + SHARED_AT + 3)
        def _():
            for i in range(width // W, pieces):
                y_done(i)

        @pl.when(s == first + SHARED_AT + 4)
        def _():
            xrows_load.wait()
            x32 = xrows[...].astype(F32)
            inverse = lax.rsqrt(jnp.mean(x32 * x32, axis=-1, keepdims=True) + epsilon)
            normal = x32 * inverse
            x_first.wait()
            d_first = part[xq, c] + quarter_in[...]
            gvec[0:1, :] = jnp.sum(d_first * normal, axis=0, keepdims=True)
            for copy in v_sends:
                copy.start()
            scaled = d_first * gain1_ref[...]
            hidq[...] = tot[xq, c] + inverse * (
                scaled - normal * jnp.mean(scaled * normal, axis=-1, keepdims=True)
            )
            gx_out.start()

        @pl.when(s == first + MIX_AT)
        def _():
            mix_copies[1].start()

        @pl.when(s == first + MIX_AT + 2)
        def _():
            mix_copies[1].wait()
            mixp[xq, c] += mquarter_in[...]

        @pl.when(s == first + MIX_AT + 3)
        def _():
            mix_own.start()
            mix_copies[2].start()

        @pl.when(s == first + MIX_AT + 5)
        def _():
            mix_own.wait()
            mix_copies[2].wait()
            mix_copies[3].start()

        @pl.when(s == first + SHARED_AT + 5)
        def _():
            for copy in v_sends:
                copy.wait()
            total = gvec[0:2, :] + gvec_in[0, 0:2, :] + gvec_in[1, 0:2, :] + gvec_in[2, 0:2, :]
            for i in range(trees):
                msg[i, 0:2, :] = total[:, i * R : (i + 1) * R]
            for copy in m_sends:
                copy.start()

        @pl.when((s == first + SHARED_AT) | (s == first + SHARED_AT + 1))
        def _():
            attention_back((s - first - SHARED_AT) * 2)
            attention_back((s - first - SHARED_AT) * 2 + 1)

        @pl.when((k >= 0) & (k < chunks))
        def _():
            for u in range(units):
                if u + 1 < units:
                    load(k, u + 1, (u + 1) % 2)
                own_unit(k, u, u % 2)

        return 0

    lax.fori_loop(first, chunks + LAG, slot_step, 0)

    outs = []
    for j in range(n_own):
        outs += [
            pltpu.make_async_copy(acc.at[:, pl.ds(j * f, f)], gg_ref.at[j], out_sem.at[0, j]),
            pltpu.make_async_copy(acc.at[:, pl.ds((n_own + j) * f, f)], gu_ref.at[j], out_sem.at[1, j]),
            pltpu.make_async_copy(accd.at[pl.ds(j * f, f)], gd_ref.at[j], out_sem.at[2, j]),
        ]
    for copy in outs:
        copy.start()
    per = width // W
    for i in range(per):
        go_ref[:, i * W : (i + 1) * W] = z_done(i)
        gq_ref[:, i * W : (i + 1) * W] = z_done(per + i)
    gk_ref[...] = z_done(2 * per)
    gv_ref[...] = z_done(2 * per + 1)
    for copy in m_sends:
        copy.wait()
    mine = msg[p]
    for j in range(trees - 1):
        mine += msg_in[j]
    g1_ref[...] = mine[0:1]
    g2_ref[...] = mine[1:2]
    gx_out.wait()
    mix_copies[3].wait()

    def sends(k, _):
        x_sent(k)

        @pl.when(k >= EARLY)
        def _():
            c_sent(k)

        return 0

    lax.fori_loop(0, chunks, sends, 0)
    for copy in outs:
        copy.wait()


def experts(
    xf, cf, early, xb, c, dense_gates, own_gates, wg, wu, wd, hidden, x, xn, gain1, gain2, q, k, v, lse, bias,
    wo, att, wq, wk, wv, cosine, sine, trees,
):
    T, D = c.shape
    E, _, f = wg.shape
    own = E // trees
    chunks = T // CHUNK
    A = trees // 2
    Q = T // 4
    R = D // trees
    W = wk.shape[1]
    pieces = 2 * (wq.shape[1] // W) + 2
    gates_in = jnp.pad(dense_gates, ((0, 0), (0, 128 - E)))
    units = A // 4
    og = own_gates.reshape(units, trees // units, 8, chunks, CHUNK).transpose(3, 0, 2, 1, 4)
    og = og.reshape(chunks, units, 8, trees // units * CHUNK)
    slots = 2 if A > 4 else 1
    S = jax.ShapeDtypeStruct
    V = pltpu.VMEM
    out = pl.pallas_call(
        experts_kernel,
        in_specs=[HBM] * 4 + [VMEM] * 3 + [HBM] * 6 + [VMEM] * 14,
        out_specs=[HBM] * 7 + [VMEM] * 6,
        out_shape=[
            S((A, 2, T, D), F32),
            S((A, 2, T, D), F32),
            S((2, 2, Q, D), F32),
            S((Q, D), F32),
            S((own, D, f), F32),
            S((own, D, f), F32),
            S((own, f, D), F32),
            S((1, R), F32),
            S((1, R), F32),
            S((R, wq.shape[1]), F32),
            S((R, wq.shape[1]), F32),
            S((R, W), F32),
            S((R, W), F32),
        ],
        scratch_shapes=[
            V((T, D), BF),
            V((2, D, 2 * EG * f), BF),
            V((2, EG, f, D), BF),
            V((2, 2, Q, D), F32),
            V((2, 2, Q, D), F32),
            V((2, Q, D), F32),
            V((Q, D), F32),
            V((2, 2, Q, D), F32),
            V((2, Q, D), F32),
            V((Q, D), F32),
            V((pieces, A, 2, R, W), F32),
            V((pieces, A, R, W), F32),
            V((pieces, A - 1, R, W), F32),
            V((Q, D), F32),
            V(q.shape, BF),
            V(q.shape, F32),
            V(k.shape, F32),
            V(v.shape, F32),
            V((T, wq.shape[1] + 2 * W), BF),
            V((Q, D), BF),
            V((8, D), F32),
            V((3, 8, D), F32),
            V((trees, 8, R), F32),
            V((trees - 1, 8, R), F32),
            V((D, 2 * own * f), F32),
            V((own * f, D), F32),
            V((slots, 4, 2, CHUNK, D), F32),
            V((slots, 4, 2, CHUNK, D), F32),
            DMA((1 + 2 * EG, 2)),
            DMA((5,)),
            DMA((2, 2)),
            DMA((3, own)),
            DMA((4, chunks)),
            DMA((4, chunks)),
            DMA((2, chunks)),
            DMA((4, chunks - EARLY)),
            DMA((4, chunks - EARLY)),
            DMA((2, chunks - EARLY)),
            DMA(()),
            DMA((pieces,)),
            DMA((pieces,)),
            DMA((pieces, A - 1)),
            DMA((pieces, A - 1)),
            DMA((3,)),
            DMA((3,)),
            DMA((trees - 1,)),
            DMA((trees - 1,)),
            DMA((10,)),
            DMA((10,)),
        ],
        compiler_params=pltpu.CompilerParams(
            collective_id=0, has_side_effects=True, vmem_limit_bytes=62 * 2**20
        ),
    )(
        xf, cf, early, xb, c, gates_in, og, wg, wu, wd, hidden, x, xn, gain1.reshape(1, D), gain2.reshape(1, D),
        q, k, v, lse, bias, wo, att, wq, wk, wv, cosine, sine,
    )
    return out[2:]


def front_kernel(
    x_ref,
    c_ref,
    gain1_ref,
    gain2_ref,
    wq_ref,
    wk_ref,
    wv_ref,
    wo_ref,
    visible_ref,
    cos_ref,
    sin_ref,
    gates_ref,
    early_ref,
    cf_out,
    xn_out,
    bias_out,
    hidden_ref,
    xb_ref,
    xf_ref,
    att_out,
    q_ref,
    k_ref,
    v_ref,
    lse_ref,
    got_ref,
    cf_ref,
    xn_ref,
    bias_ref,
    att,
    others,
    wof,
    wr,
    hot,
    msg,
    peaks,
    ssem,
    rsem,
    wsend,
    wrecv,
    msend,
    mrecv,
    msem,
    c_send,
    c_recv,
    c_own,
    flush_sem,
):
    T, D = x_ref.shape
    trees = got_ref.shape[0]
    heads, _, hd = q_ref.shape
    kvs = k_ref.shape[0]
    group = heads // kvs
    width = heads * hd
    kwidth = kvs * hd
    scale = hd ** (-0.5)
    half = T // 2
    Q = T // 4
    p = lax.axis_index("dp")
    t = lax.axis_index("tensor")
    xq = t // 2
    c = t % 2
    x_dev = (p, (1 - xq) * 2 + c)
    c_dev = (p, xq * 2 + 1 - c)
    peers = [((p + j) % trees, t) for j in range(1, trees)]
    c_start, _, _, c_done, c_sent, pump, _ = gatherer(
        cf_ref, early_ref, c_send, c_recv, c_own, 0, EARLY, *EARLY_ROWS
    )
    sync_with(peers + [x_dev, c_dev])
    cf_ref[...] = c_ref[...].astype(F32)
    flushes = [
        pltpu.make_async_copy(one, two, flush_sem.at[i])
        for i, (one, two) in enumerate(((cf_ref, cf_out), (xn_ref, xn_out), (bias_ref, bias_out)))
    ]
    flushes[0].start()
    c_start(0)
    wof[t] = wo_ref[...].astype(F32)
    w_x = send(wof.at[t], wof.at[t], wsend.at[0], wrecv.at[0], x_dev)
    w_c = send(wof.at[t], wof.at[t], wsend.at[1], wrecv.at[1], c_dev)
    far = (1 - xq) * 2 + c
    w_on = send(wof.at[far], wof.at[far], wsend.at[2], wrecv.at[2], c_dev)
    w_x.start()
    w_c.start()

    row = lax.broadcasted_iota(jnp.int32, (width, width), 0)
    col = lax.broadcasted_iota(jnp.int32, (width, width), 1)
    low = (col % hd) < hd // 2
    turn = jnp.where(low & (row == col + hd // 2), -1.0, jnp.where(~low & (row == col - hd // 2), 1.0, 0.0))
    turn = turn.astype(BF)
    wr[:, :width] = dot(wq_ref[...], turn).astype(BF)
    wr[:, width:] = dot(wk_ref[...], turn[:kwidth, :kwidth]).astype(BF)

    token = lax.broadcasted_iota(jnp.int32, (T, 128), 0)
    seg = lax.broadcasted_iota(jnp.int32, (T, 128), 1)
    begin = jnp.where(seg == 0, 0, TRUNK + (seg - 1) * SEG)
    end = TRUNK + seg * SEG
    hot[...] = ((token >= begin) & (token < end)).astype(F32).astype(BF)

    def project(i, _):
        rows = pl.ds(pl.multiple_of(i * Q, 16), Q)
        x32 = x_ref[rows, :].astype(F32)
        inverse = lax.rsqrt(jnp.mean(x32 * x32, axis=-1, keepdims=True) + epsilon)
        xn = (x32 * inverse * gain1_ref[...]).astype(BF)
        xn_ref[rows, :] = xn
        cosine = cos_ref[rows, :]
        sine = sin_ref[rows, :]
        turned = dot(xn, wr[...])
        query = dot(xn, wq_ref[...])
        query = query * jnp.concatenate([cosine] * (width // 128), axis=1) + turned[:, :width] * jnp.concatenate(
            [sine] * (width // 128), axis=1
        )
        key = dot(xn, wk_ref[...]) * cosine + turned[:, width:] * sine
        value = dot(xn, wv_ref[...])
        for h in range(heads):
            q_ref[h, rows, :] = query[:, h * hd : (h + 1) * hd].astype(BF)
        for g in range(kvs):
            k_ref[g, rows, :] = key[:, g * hd : (g + 1) * hd].astype(BF)
            v_ref[g, rows, :] = value[:, g * hd : (g + 1) * hd].astype(BF)
        mine = hot[rows, :]
        reach = dot(mine, visible_ref[...]).astype(BF)
        near = dot_t(reach, hot[...]) > 0.5
        same = dot_t(mine, hot[...]) > 0.5
        qi = lax.broadcasted_iota(jnp.int32, (Q, T), 0) + i * Q
        kj = lax.broadcasted_iota(jnp.int32, (Q, T), 1)
        seen = near & (~same | (kj <= qi))
        bias_ref[rows, :] = jnp.where(seen, 0.0, -1e30).astype(BF)
        return 0

    lax.fori_loop(0, 4, project, 0)
    flushes[1].start()
    flushes[2].start()
    pump(0)
    peaks[...] = jnp.full_like(peaks, -1e30)
    lane = lax.broadcasted_iota(jnp.int32, (1, 128), 1)

    def attend(i, _):
        rows = pl.ds(pl.multiple_of(i * Q, 16), Q)
        bias = bias_ref[rows, :].astype(F32)
        for h in range(heads):
            g = h // group
            scores = dot_t(q_ref[h, rows, :], k_ref[g]) * scale + bias
            top = jnp.max(scores, axis=-1, keepdims=True)
            expo = jnp.exp(scores - top)
            total = jnp.sum(expo, axis=-1, keepdims=True)
            probs = (expo / total).astype(BF)
            out = dot(probs, v_ref[g]).astype(BF)
            att_out[rows, h * hd : (h + 1) * hd] = out
            att[rows, h * hd : (h + 1) * hd] = out.astype(F32)
            lse_ref[rows, h : h + 1] = top + jnp.log(total)
            peak = jnp.max(top, axis=0, keepdims=True)
            peaks[0:1, :] = jnp.maximum(peaks[0:1, :], jnp.where(lane == h, peak, -1e30))
        return 0

    rows = [pl.ds(i * half, half) for i in range(2)]
    to_x = [send(att.at[r], others.at[1, r], ssem.at[0, i], rsem.at[0, i], x_dev) for i, r in enumerate(rows)]
    to_c = [send(att.at[r], others.at[0, r], ssem.at[1, i], rsem.at[1, i], c_dev) for i, r in enumerate(rows)]
    on = [send(others.at[1, r], others.at[2, r], ssem.at[2, i], rsem.at[2, i], c_dev) for i, r in enumerate(rows)]
    lax.fori_loop(0, 2, attend, 0)
    to_x[0].start()
    to_c[0].start()
    pump(1)
    lax.fori_loop(2, 4, attend, 0)
    to_x[1].start()
    to_c[1].start()
    pump(2)
    msg[...] = gates_ref[...]
    msg[:, 7:8, 0:128] = jnp.broadcast_to(peaks[0:1, :][None], (trees, 1, 128))
    messages = [
        send(msg.at[dev[0]], got_ref.at[j], msend.at[j], mrecv.at[j], dev) for j, dev in enumerate(peers, 1)
    ]
    for copy in messages:
        copy.start()
    mine = pltpu.make_async_copy(msg.at[p], got_ref.at[0], msem)
    mine.start()
    w_x.wait()
    w_on.start()
    w_c.wait()

    def proj(block, owner):
        return dot(block.astype(BF), wof[owner].astype(BF))

    for i, r in enumerate(rows):
        hidden_ref[r, :] = x_ref[r, :].astype(F32) + proj(att[r, :], t)
    for i, r in enumerate(rows):
        to_c[i].wait()
        hidden_ref[r, :] += proj(others[0, r, :], xq * 2 + 1 - c)
    pump(3)
    for i, r in enumerate(rows):
        to_x[i].wait()
        on[i].start()
        hidden_ref[r, :] += proj(others[1, r, :], far)
    pump(4)
    w_on.wait()
    for i, r in enumerate(rows):
        on[i].wait()
        hidden = hidden_ref[r, :] + proj(others[2, r, :], (1 - xq) * 2 + 1 - c)
        hidden_ref[r, :] = hidden
        inverse = lax.rsqrt(jnp.mean(hidden * hidden, axis=-1, keepdims=True) + epsilon)
        low_x = (hidden * inverse * gain2_ref[...]).astype(BF)
        xb_ref[r, :] = low_x
        xf_ref[r, :] = low_x.astype(F32)
    for copy in messages:
        copy.wait()
    mine.wait()
    for s in range(5, EARLY + 3):
        pump(s)
    for copy in flushes:
        copy.wait()
    for k in range(EARLY):
        c_done(k)
        c_sent(k)


def front(x, c, gain1, gain2, wq, wk, wv, wo, visible, cosine, sine, gates_out):
    T, D = x.shape
    trees = gates_out.shape[0]
    A = trees // 2
    heads = wq.shape[1] // HEAD_DIM
    kvs = wk.shape[1] // HEAD_DIM
    width = wq.shape[1]
    S = jax.ShapeDtypeStruct
    V = pltpu.VMEM
    return pl.pallas_call(
        front_kernel,
        in_specs=[VMEM] * 12,
        out_specs=[HBM] * 4 + [VMEM] * 9,
        out_shape=[
            S((A, 2, T, D), F32),
            S((T, D), F32),
            S((T, D), BF),
            S((T, T), BF),
            S((T, D), F32),
            S((T, D), BF),
            S((T, D), F32),
            S((T, width), BF),
            S((heads, T, HEAD_DIM), BF),
            S((kvs, T, HEAD_DIM), BF),
            S((kvs, T, HEAD_DIM), BF),
            S((T, 128), F32),
            S(gates_out.shape, F32),
        ],
        scratch_shapes=[
            V((T, D), F32),
            V((T, D), BF),
            V((T, T), BF),
            V((T, width), F32),
            V((3, T, width), F32),
            V((4, width, D), F32),
            V((D, width + wk.shape[1]), BF),
            V((T, 128), BF),
            V(gates_out.shape, F32),
            V((8, 128), F32),
            DMA((3, 2)),
            DMA((3, 2)),
            DMA((3,)),
            DMA((3,)),
            DMA((trees,)),
            DMA((trees,)),
            DMA(()),
            DMA((4, EARLY)),
            DMA((4, EARLY)),
            DMA((2, EARLY)),
            DMA((3,)),
        ],
        compiler_params=pltpu.CompilerParams(
            collective_id=1, has_side_effects=True, vmem_limit_bytes=58 * 2**20
        ),
    )(x, c, gain1.reshape(1, D), gain2.reshape(1, D), wq, wk, wv, wo, visible, cosine, sine, gates_out)


def last_kernel(hid_ref, mix_ref, got_ref, limit_ref, wq_ref, wk_ref, *refs):
    n = (len(refs) - 9) // 3
    out_ref, factor_ref, qs_ref, ks_ref = refs[n : n + 4]
    hid, mix, held = refs[2 * n + 4], refs[2 * n + 5], refs[2 * n + 6 : 3 * n + 6]
    in_sem, sem, big_sem = refs[3 * n + 6 :]
    big = [pltpu.make_async_copy(hid_ref, hid, big_sem.at[0]), pltpu.make_async_copy(mix_ref, mix, big_sem.at[1])]
    ins = [pltpu.make_async_copy(refs[i], held[i], in_sem.at[i]) for i in range(n)]
    outs = [pltpu.make_async_copy(held[i], refs[n + 4 + i], sem.at[i]) for i in range(n)]
    for copy in big + ins:
        copy.start()
    heads = limit_ref.shape[1]
    limits = limit_ref[...]
    peaks = jnp.max(got_ref[:, 7, 0:128], axis=0, keepdims=True)[:, 0:heads]
    factors = limits / jnp.maximum(peaks, limits)
    factor_ref[...] = factors
    group = wq_ref.shape[1] // wk_ref.shape[1]
    roots = [jnp.sqrt(factors[:, h : h + 1]) for h in range(heads)]
    least = [
        jnp.sqrt(jnp.min(factors[:, g * group : (g + 1) * group], axis=1, keepdims=True)) for g in range(heads // group)
    ]

    def scaled(w_ref, values):
        head = lax.broadcasted_iota(jnp.int32, (1, w_ref.shape[1]), 1) // HEAD_DIM
        row = jnp.zeros((1, w_ref.shape[1]), F32)
        for h, value in enumerate(values):
            row = jnp.where(head == h, value, row)
        return (w_ref[...].astype(F32) * row).astype(BF)

    qs_ref[...] = scaled(wq_ref, roots)
    ks_ref[...] = scaled(wk_ref, least)
    for copy in big:
        copy.wait()
    out_ref[...] = (hid[...] + mix[...]).astype(BF)
    for i in range(n):
        ins[i].wait()
        outs[i].start()
    for copy in outs:
        copy.wait()


def last(hidden, mixture, got, limits, wq, wk, *rest):
    T, D = hidden.shape
    S = jax.ShapeDtypeStruct
    n = len(rest)
    return pl.pallas_call(
        last_kernel,
        in_specs=[HBM] * 2 + [VMEM] * 4 + [HBM] * n,
        out_specs=[VMEM] * 4 + [HBM] * n,
        out_shape=[
            S((T, D), BF),
            S((1, limits.shape[0]), F32),
            S(wq.shape, BF),
            S(wk.shape, BF),
        ]
        + [S(r.shape, r.dtype) for r in rest],
        scratch_shapes=[pltpu.VMEM((T, D), F32)] * 2
        + [pltpu.VMEM(r.shape, r.dtype) for r in rest]
        + [DMA((n,)), DMA((n,)), DMA((2,))],
        compiler_params=pltpu.CompilerParams(vmem_limit_bytes=62 * 2**20),
    )(hidden, mixture.reshape(T, D), got, limits.reshape(1, -1), wq, wk, *rest)


def local(
    block_input,
    norm_first,
    norm_second,
    w_query,
    w_key,
    w_value,
    w_out,
    w_gate,
    w_up,
    w_down,
    routes,
    gates,
    parents,
    clip_limits,
    cotangent,
):
    count, width = block_input.shape
    head_dim = HEAD_DIM
    query_cols = w_query.shape[1]
    key_cols = w_key.shape[1]
    query_heads = query_cols // head_dim
    kv_heads = key_cols // head_dim
    trees = lax.axis_size("dp")
    own = EXPERTS // trees
    position, visible = tree_tables(parents[0], count)
    visible = jnp.pad(visible.astype(jnp.bfloat16), ((0, 128 - SEGS), (0, 128 - SEGS)))
    cosine, sine = rotary_tables(position, head_dim)
    wide_cosine = jnp.tile(cosine[:, 0], (1, 128 * 2 // head_dim))
    wide_sine = jnp.tile(sine[:, 0], (1, 128 * 2 // head_dim))
    routed = routes[:, :, None] == jnp.arange(EXPERTS, dtype=jnp.int32)[None, None, :]
    dense_gates = jnp.sum(jnp.where(routed, gates[:, :, None], 0.0), axis=1)
    gates_out = jnp.pad(dense_gates.T.reshape(trees, own, count), ((0, 0), (0, 8 - own), (0, 0)))
    (
        early,
        c_wide,
        input_first,
        bias,
        hidden,
        input_second,
        x_wide,
        attended_parts,
        queries,
        keys,
        values,
        log_norms,
        got,
    ) = front(
        block_input,
        cotangent,
        norm_first,
        norm_second,
        w_query,
        w_key,
        w_value,
        w_out,
        visible,
        wide_cosine,
        wide_sine,
        gates_out,
    )
    order = (lax.axis_index("dp") - jnp.arange(trees)) % trees
    hot = (order[:, None] == jnp.arange(trees)[None, :]).astype(jnp.float32)
    own_gates = jnp.sum(hot[:, :, None, None] * got[:, None], axis=0)
    (
        mixture,
        grad_x,
        gate_shard,
        up_shard,
        down_shard,
        first_gain_grad,
        second_shard,
        out_shard,
        query_shard,
        key_shard,
        value_shard,
    ) = experts(
        x_wide,
        c_wide,
        early,
        input_second,
        cotangent,
        dense_gates,
        own_gates,
        w_gate,
        w_up,
        w_down,
        hidden,
        block_input,
        input_first,
        norm_first,
        norm_second,
        queries,
        keys,
        values,
        log_norms,
        bias,
        w_out,
        attended_parts,
        w_query,
        w_key,
        w_value,
        wide_cosine,
        wide_sine,
        trees,
    )
    block_out, factors, query_scaled, key_scaled, *rest = last(
        hidden,
        mixture,
        got,
        clip_limits,
        w_query,
        w_key,
        grad_x,
        first_gain_grad,
        second_shard,
        query_shard,
        key_shard,
        value_shard,
        out_shard,
        gate_shard,
        up_shard,
        down_shard,
    )
    grad_x, first_gain_grad, second_shard = rest[:3]
    return (
        block_out,
        grad_x,
        first_gain_grad.reshape(width // trees),
        second_shard.reshape(width // trees),
        *rest[3:],
        factors.reshape(query_heads),
        query_scaled,
        key_scaled,
    )


def solution(mesh):
    placed = (
        P("dp", None),
        P(),
        P(),
        P(None, "tensor"),
        P(None, "tensor"),
        P(None, "tensor"),
        P("tensor", None),
        P(None, None, "tensor"),
        P(None, None, "tensor"),
        P(None, "tensor", None),
        P("dp", None),
        P("dp", None),
        P("dp", None),
        P("tensor"),
        P("dp", None),
    )
    return jax.shard_map(
        local,
        mesh=mesh,
        in_specs=placed,
        out_specs=(
            P("dp", None),
            P(("dp", "tensor"), None),
            P("dp"),
            P("dp"),
            P("dp", "tensor"),
            P("dp", "tensor"),
            P("dp", "tensor"),
            P("dp", "tensor"),
            P("dp", None, "tensor"),
            P("dp", None, "tensor"),
            P("dp", "tensor", None),
            P("tensor"),
            P(None, "tensor"),
            P(None, "tensor"),
        ),
        check_vma=False,
    )
```

```python
import functools

import jax
import jax.numpy as jnp
from jax import lax
from jax.experimental import pallas as pl
from jax.experimental.pallas import tpu as pltpu
from jax.sharding import PartitionSpec as P

HEAD_DIM = 64
EXPERTS = 32
TOPK = 8
TRUNK = 256
SEG = 48
SEGS = 13


epsilon = 1e-06
theta_base = 10000.0
expert_group = 4


def tree_tables(parent_row, count):
    slot_ids = jnp.arange(SEGS, dtype=jnp.int32)
    safe_parent = jnp.maximum(parent_row, 0)
    hot_parent = (safe_parent[:, None] == slot_ids[None, :]).astype(jnp.int32)
    grand_raw = jnp.sum(hot_parent * parent_row[None, :], axis=1)
    grand_parent = jnp.where(parent_row >= 0, grand_raw, -1)
    visible = (
        (slot_ids[:, None] == slot_ids[None, :])
        | (slot_ids[None, :] == parent_row[:, None])
        | (slot_ids[None, :] == grand_parent[:, None])
    )
    depth = (parent_row >= 0).astype(jnp.int32) + (grand_parent >= 0).astype(jnp.int32)
    token_ids = jnp.arange(count, dtype=jnp.int32)
    segment = jnp.where(token_ids < TRUNK, 0, 1 + (token_ids - TRUNK) // SEG)
    local_index = jnp.where(token_ids < TRUNK, token_ids, (token_ids - TRUNK) % SEG)
    seg_match = segment[:, None] == slot_ids[None, :]
    token_depth = jnp.sum(seg_match.astype(jnp.int32) * depth[None, :], axis=1)
    position = jnp.where(segment == 0, token_ids, TRUNK + (token_depth - 1) * SEG + local_index)
    return position, visible


def rotary_tables(position, head_dim):
    half = head_dim // 2
    inverse = theta_base ** (-(jnp.arange(half, dtype=jnp.float32) * 2.0 / head_dim))
    angle = position.astype(jnp.float32)[:, None] * inverse[None, :]
    return (jnp.cos(angle)[:, None, :], jnp.sin(angle)[:, None, :])


F32 = jnp.float32
BF = jnp.bfloat16
MESH = pl.DeviceIdType.MESH
CHUNK = 64
PART = 8
BOTH = 16
EG = 4
LAG = 4
EARLY = 2
QUARTER_AT = 3
SHARED_AT = 6
MIX_AT = 6
EARLY_ROWS = (0, 32)


def dot(a, b):
    return jnp.dot(a, b, preferred_element_type=F32)


def dot_t(a, b):
    return lax.dot_general(a, b, (((1,), (1,)), ((), ())), preferred_element_type=F32)


def dot_l(a, b):
    return lax.dot_general(a, b, (((0,), (0,)), ((), ())), preferred_element_type=F32)


def expert_core(x, c, g, wcat, wdcat):
    n = len(g)
    f = wdcat.shape[0]
    both = dot(x, wcat)
    gate = both[:, :f]
    up = both[:, f:]
    d_act = dot_t(c, wdcat)
    wide = jnp.concatenate([jnp.broadcast_to(v, (x.shape[0], f // n)) for v in g], axis=1)
    sigma = jax.nn.sigmoid(gate)
    silu = gate * sigma
    act = ((silu * up).astype(BF).astype(F32) * wide).astype(BF)
    d_act = d_act * wide
    d_gate = (d_act * up * (sigma + silu * (1.0 - sigma))).astype(BF)
    d_up = (d_act * silu).astype(BF)
    return act, jnp.concatenate([d_gate, d_up], axis=1)


VMEM = pl.BlockSpec(memory_space=pltpu.VMEM)
HBM = pl.BlockSpec(memory_space=pl.ANY)
DMA = pltpu.SemaphoreType.DMA


def sync_with(devices):
    barrier = pltpu.get_barrier_semaphore()
    for dev in devices:
        pl.semaphore_signal(barrier, inc=1, device_id=dev, device_id_type=MESH)
    pl.semaphore_wait(barrier, len(devices))


def send(src, dst, out_sem, in_sem, dev):
    return pltpu.make_async_remote_copy(
        src_ref=src,
        dst_ref=dst,
        send_sem=out_sem,
        recv_sem=in_sem,
        device_id=dev,
        device_id_type=MESH,
    )


def gatherer(src, dst, send_sem, recv_sem, own_sem, first, last, part, both):
    A = dst.shape[0]
    p = lax.axis_index("dp")
    t = lax.axis_index("tensor")
    a = p // 2
    b = p % 2
    xq = t // 2
    c = t % 2
    y_dev = (a * 2 + 1 - b, t)
    x_dev = (p, (1 - xq) * 2 + c)
    c_dev = (p, xq * 2 + 1 - c)
    z_devs = [(((a + j) % A) * 2 + b, t) for j in range(1, A)]

    def rows1(k):
        return pl.ds(pl.multiple_of(k * CHUNK + (c * 2 + xq) * part, 8), part)

    def rows_pair(k):
        return pl.ds(pl.multiple_of(k * CHUNK + c * 2 * part, 8), 2 * part)

    def rows2(k):
        return pl.ds(pl.multiple_of(k * CHUNK + 4 * part + c * both, 8), both)

    def mine(k):
        return [rows1(k), rows2(k)] if part and both else [rows1(k)] if part else [rows2(k)]

    def of_core(k):
        return [rows_pair(k), rows2(k)] if part and both else [rows_pair(k)] if part else [rows2(k)]

    def remote(one, two, stage, k, dev):
        return pltpu.make_async_remote_copy(
            src_ref=one,
            dst_ref=two,
            send_sem=send_sem.at[stage, k - first],
            recv_sem=recv_sem.at[stage, k - first],
            device_id=dev,
            device_id_type=MESH,
        )

    sizes = [
        dst.at[pl.ds(0, A - 1), 0, pl.ds(0, part + both)],
        dst.at[:, 0, pl.ds(0, part + both)],
        dst.at[:, :, pl.ds(0, max(part, 8))],
        dst.at[:, :, pl.ds(0, 2 * part + both)],
    ]

    def took(stage, k, sem):
        pltpu.make_async_copy(sizes[stage], sizes[stage], sem.at[stage, k - first]).wait()

    def own(k, i):
        rows = mine(k)[i]
        return pltpu.make_async_copy(src.at[rows], dst.at[a, b, rows], own_sem.at[i, k - first])

    def start(k):
        for i, rows in enumerate(mine(k)):
            for dev in z_devs:
                remote(src.at[rows], dst.at[a, b, rows], 0, k, dev).start()
            own(k, i).start()

    def second(k):
        took(0, k, recv_sem)
        for i, rows in enumerate(mine(k)):
            own(k, i).wait()
            remote(dst.at[:, b, rows], dst.at[:, b, rows], 1, k, y_dev).start()

    def to_core(k):
        for rows in of_core(k):
            remote(dst.at[:, :, rows], dst.at[:, :, rows], 3, k, c_dev).start()

    def third(k):
        took(1, k, recv_sem)
        if not part:
            to_core(k)
            return
        rows = rows1(k)
        remote(dst.at[:, :, rows], dst.at[:, :, rows], 2, k, x_dev).start()

    def fourth(k):
        took(2, k, recv_sem)
        to_core(k)

    def done(k):
        took(3, k, recv_sem)

    def sent(k):
        for stage in (0, 1, 2, 3) if part else (0, 1, 3):
            took(stage, k, send_sem)

    def pump(s):
        steps = ((3, fourth), (2, third), (1, second), (-1, start))
        for back, stage in steps if part else steps[1:]:
            k = first + s - back
            if isinstance(s, int):
                if first <= k < last:
                    stage(k)
            else:

                @pl.when((k >= first) & (k < last))
                def _(k=k, stage=stage):
                    stage(k)

    return start, second, third, done, sent, pump, z_devs + [y_dev, x_dev, c_dev]


def experts_kernel(
    xf_ref,
    cf_ref,
    early_ref,
    xb_ref,
    c_ref,
    g_ref,
    og_ref,
    wg_ref,
    wu_ref,
    wd_ref,
    hid_ref,
    xin_ref,
    xn_ref,
    gain1_ref,
    gain_ref,
    q_ref,
    k_ref,
    v_ref,
    lse_ref,
    bias_ref,
    wo_ref,
    att_ref,
    wq_ref,
    wk_ref,
    wv_ref,
    cos_ref,
    sin_ref,
    all_x,
    all_c,
    mix_ref,
    gx_ref,
    gg_ref,
    gu_ref,
    gd_ref,
    g1_ref,
    g2_ref,
    go_ref,
    gq_ref,
    gk_ref,
    gv_ref,
    x_ref,
    wc,
    wbd,
    mixp,
    part,
    half_in,
    quarter_in,
    tot,
    mhalf_in,
    mquarter_in,
    grads,
    ybuf,
    zbuf,
    hidq,
    d_att,
    dq_ref,
    dk_ref,
    dv_ref,
    dqkv,
    xrows,
    gvec,
    gvec_in,
    msg,
    msg_in,
    acc,
    accd,
    ux,
    uc,
    w_sem,
    in_sem,
    load_sem,
    out_sem,
    x_send,
    x_recv,
    x_own,
    c_send,
    c_recv,
    c_own,
    mix_sem,
    ysem,
    yrsem,
    zsem,
    zrsem,
    vsem,
    vrsem,
    msem,
    mrsem,
    ssend,
    srecv,
):
    T, D = x_ref.shape
    A = all_x.shape[0]
    E, _, f = wg_ref.shape
    n_own = gg_ref.shape[0]
    chunks = T // CHUNK
    p = lax.axis_index("dp")
    t = lax.axis_index("tensor")
    xq = t // 2
    c = t % 2
    x_dev = (p, (1 - xq) * 2 + c)
    c_dev = (p, xq * 2 + 1 - c)
    f_dev = (p, (1 - xq) * 2 + 1 - c)
    trees = msg.shape[0]
    peers = [((p + j) % trees, t) for j in range(1, trees)]
    x_start, _, _, x_done, x_sent, x_pump, _ = gatherer(
        xf_ref, all_x, x_send, x_recv, x_own, 0, chunks, PART, BOTH
    )
    c_start, _, _, c_done, c_sent, c_pump, _ = gatherer(
        cf_ref, all_c, c_send, c_recv, c_own, EARLY, chunks, PART, BOTH
    )
    xb_load = pltpu.make_async_copy(xb_ref, x_ref, in_sem.at[0])
    xb_load.start()
    sync_with(peers + [x_dev, c_dev, f_dev])

    def pump(s):
        c_pump(s)
        x_pump(s)

    x_start(0)
    c_start(EARLY)

    first_own = p * n_own
    own_loads = [pltpu.make_async_copy(wd_ref.at[pl.ds(first_own, n_own)], wbd.at[0, pl.ds(0, n_own)], w_sem.at[0, 0])]
    for i in range(n_own):
        for h, src in enumerate((wg_ref, wu_ref)):
            dst = wc.at[0, :, pl.ds((h * n_own + i) * f, f)]
            own_loads.append(pltpu.make_async_copy(src.at[first_own + i], dst, w_sem.at[1 + 2 * i + h, 0]))

    def w_loads(i, slot):
        loads = [pltpu.make_async_copy(wd_ref.at[pl.ds(i * EG, EG)], wbd.at[slot], w_sem.at[0, slot])]
        for j in range(EG):
            for h, src in enumerate((wg_ref, wu_ref)):
                dst = wc.at[slot, :, pl.ds((h * EG + j) * f, f)]
                loads.append(pltpu.make_async_copy(src.at[i * EG + j], dst, w_sem.at[1 + 2 * j + h, slot]))
        return loads

    for copy in w_loads(0, 0):
        copy.start()
    part[...] = jnp.zeros_like(part)
    xb_load.wait()
    mixp[...] = jnp.zeros_like(mixp)
    groups = E // EG
    rows_at = T // 2
    lanes = g_ref.shape[1]

    def group_step(i, _):
        slot = i % 2

        @pl.when(i + 1 < groups)
        def _():
            for copy in w_loads(i + 1, 1 - slot):
                copy.start()

        @pl.when(i + 1 == groups)
        def _():
            for copy in own_loads:
                copy.start()

        @pl.when(i % 2 == 0)
        def _():
            pump(i // 2)

        for copy in w_loads(i, slot):
            copy.wait()
        wd = wbd[slot].reshape(EG * f, D)

        def rows_step(r, _):
            rows = pl.ds(pl.multiple_of(r * rows_at, 16), rows_at)
            turned = pltpu.roll(g_ref[rows, :], lanes - i * EG, 1)
            g = [turned[:, j : j + 1] for j in range(EG)]
            act, dgu = expert_core(x_ref[rows, :], c_ref[rows, :], g, wc[slot], wd)
            mixp[r] += dot(act, wd).reshape(2, rows_at // 2, D)
            part[r] += dot_t(dgu, wc[slot]).reshape(2, rows_at // 2, D)
            return 0

        lax.fori_loop(0, 2, rows_step, 0)
        return 0

    lax.fori_loop(0, groups, group_step, 0)

    acc[...] = jnp.zeros_like(acc)
    accd[...] = jnp.zeros_like(accd)

    Q = T // 4
    my_rows = pl.ds(pl.multiple_of(t * Q, 16), Q)
    hid_load = pltpu.make_async_copy(hid_ref.at[my_rows], hidq, in_sem.at[1])
    hid_load.start()
    xrows_load = pltpu.make_async_copy(xin_ref.at[my_rows], xrows, in_sem.at[2])
    xrows_load.start()
    xn_load = pltpu.make_async_copy(xn_ref, x_ref, in_sem.at[3])

    def summing(src, dst, i, dev):
        return pltpu.make_async_remote_copy(
            src_ref=src,
            dst_ref=dst,
            send_sem=ssend.at[i],
            recv_sem=srecv.at[i],
            device_id=dev,
            device_id_type=MESH,
        )

    sum_copies = [
        summing(part.at[:, 1 - c], half_in, 0, c_dev),
        summing(part.at[1 - xq, c], quarter_in, 1, x_dev),
        summing(tot.at[xq, c], tot.at[xq, c], 2, x_dev),
        summing(tot.at[:, c], tot.at[:, c], 3, c_dev),
    ]
    mix_copies = [
        summing(mixp.at[:, 1 - c], mhalf_in, 4, c_dev),
        summing(mixp.at[1 - xq, c], mquarter_in, 5, x_dev),
        summing(mixp.at[xq, c], mix_ref.at[xq, c], 6, x_dev),
        summing(mix_ref.at[:, c], mix_ref.at[:, c], 7, c_dev),
    ]
    mix_own = pltpu.make_async_copy(mixp.at[xq, c], mix_ref.at[xq, c], mix_sem)
    core_first = summing(part.at[:, 1 - c], half_in, 8, c_dev)
    x_first = summing(part.at[1 - xq, c], quarter_in, 9, x_dev)
    gx_out = pltpu.make_async_copy(hidq, gx_ref, in_sem.at[4])

    a = p // 2
    b = p % 2
    pieces, _, _, R, W = grads.shape
    y_dev = (a * 2 + 1 - b, t)

    def to_y(i):
        return send(grads.at[i, :, 1 - b], ybuf.at[i], ysem.at[i], yrsem.at[i], y_dev)

    def to_z(i):
        return [
            send(
                grads.at[i, (a + j) % A, b],
                zbuf.at[i, j - 1],
                zsem.at[i, j - 1],
                zrsem.at[i, j - 1],
                (((a + j) % A) * 2 + b, t),
            )
            for j in range(1, A)
        ]

    def y_done(i):
        to_y(i).wait()
        grads[i, :, b] += ybuf[i]
        for copy in to_z(i):
            copy.start()

    def z_done(i):
        for copy in to_z(i):
            copy.wait()
        whole = grads[i, a, b]
        for j in range(A - 1):
            whole += zbuf[i, j]
        return whole

    v_sends = [
        send(gvec, gvec_in.at[j], vsem.at[j], vrsem.at[j], dev) for j, dev in enumerate((x_dev, c_dev, f_dev))
    ]
    m_sends = [
        send(msg.at[dev[0]], msg_in.at[j], msem.at[j], mrsem.at[j], dev) for j, dev in enumerate(peers)
    ]

    first = groups // 2
    units = A // 4
    group_trees = A // units

    def part_of(ref, k, u):
        rows = pl.ds(pl.multiple_of(k * CHUNK, 8), CHUNK)
        return ref.at[pl.ds(u * group_trees, group_trees), :, rows]

    def load_x(k, u, slot):
        return pltpu.make_async_copy(part_of(all_x, k, u), ux.at[slot], load_sem.at[0, slot])

    def load_c(ref, k, u, slot):
        return pltpu.make_async_copy(part_of(ref, k, u), uc.at[slot], load_sem.at[1, slot])

    def load(k, u, slot):
        load_x(k, u, slot).start()

        @pl.when(k < EARLY)
        def _():
            load_c(early_ref, k, u, slot).start()

        @pl.when(k >= EARLY)
        def _():
            load_c(all_c, k, u, slot).start()

    for copy in own_loads:
        copy.wait()
    wdo = wbd[0, 0:n_own].reshape(n_own * f, D)

    def own_unit(k, u, slot):
        load_x(k, u, slot).wait()
        load_c(all_c, k, u, slot).wait()
        size = group_trees * 2 * CHUNK
        xs = ux[slot].reshape(size, D).astype(BF)
        cs = uc[slot].reshape(size, D).astype(BF)
        turned = og_ref[k, u].T
        g = [turned[:, j : j + 1] for j in range(n_own)]
        act, dgu = expert_core(xs, cs, g, wc[0, :, 0 : 2 * n_own * f], wdo)
        acc[...] += dot_l(xs, dgu)
        accd[...] += dot_l(act, cs)

    heads, _, hd = q_ref.shape
    group = heads // k_ref.shape[0]
    scale = hd ** (-0.5)
    dk_ref[...] = jnp.zeros_like(dk_ref)
    dv_ref[...] = jnp.zeros_like(dv_ref)

    def attention_back(h):
        g = h // group

        def block(i, _):
            rows = pl.ds(pl.multiple_of(i * Q, 16), Q)
            q = q_ref[h, rows, :]
            da = d_att[h, rows, :]
            lse = pltpu.roll(lse_ref[rows, :], lse_ref.shape[1] - h, 1)[:, 0:1]
            scores = dot_t(q, k_ref[g]) * scale + bias_ref[rows, :].astype(F32)
            probs = jnp.exp(scores - lse)
            d_probs = dot_t(da, v_ref[g])
            row_dot = jnp.sum(probs * d_probs, axis=-1, keepdims=True)
            d_scores = (probs * (d_probs - row_dot) * scale).astype(BF)
            dq_ref[h, rows, :] = dot(d_scores, k_ref[g])
            dk_ref[g] += dot_l(d_scores, q)
            dv_ref[g] += dot_l(probs.astype(BF), da)
            return 0

        lax.fori_loop(0, 4, block, 0)

    width = heads * hd
    kwidth = k_ref.shape[0] * hd

    def finish_start():
        lane = lax.broadcasted_iota(jnp.int32, (T, hd), 1)
        cosine = cos_ref[:, 0:hd]
        sine = jnp.where(lane < hd // 2, sin_ref[:, 0:hd], -sin_ref[:, 0:hd])

        def turned_back(d):
            swapped = jnp.concatenate([d[:, hd // 2 :], d[:, : hd // 2]], axis=1)
            return (d * cosine + swapped * sine).astype(BF)

        for h in range(heads):
            dqkv[:, h * hd : (h + 1) * hd] = turned_back(dq_ref[h])
        for g in range(k_ref.shape[0]):
            at = width + g * hd
            dqkv[:, at : at + hd] = turned_back(dk_ref[g])
            at = width + kwidth + g * hd
            dqkv[:, at : at + hd] = dv_ref[g].astype(BF)
        xn_load.wait()
        for i in range(width // W, pieces):
            at = (i - width // W) * W
            grads[i] = dot_l(x_ref[...], dqkv[:, at : at + W]).reshape(A, 2, R, W)
            to_y(i).start()
        for r in range(2):
            rows = pl.ds(r * 2 * Q, 2 * Q)
            total = dot_t(dqkv[rows, 0:width], wq_ref[...])
            total += dot_t(dqkv[rows, width : width + kwidth], wk_ref[...])
            total += dot_t(dqkv[rows, width + kwidth :], wv_ref[...])
            part[r] = total.reshape(2, Q, D)
        core_first.start()

    def slot_step(s, _):
        pump(s)

        k = s - LAG

        @pl.when((k >= 0) & (k < chunks))
        def _():
            x_done(k)

            @pl.when(k >= EARLY)
            def _():
                c_done(k)

            load(k, 0, 0)

        @pl.when(s == first)
        def _():
            sum_copies[0].start()
            sum_copies[0].wait()
            part[:, c] += half_in[...]
            sum_copies[1].start()

        @pl.when(s == first + QUARTER_AT)
        def _():
            sum_copies[1].wait()
            hid_load.wait()
            hidden = hidq[...]
            inverse = lax.rsqrt(jnp.mean(hidden * hidden, axis=-1, keepdims=True) + epsilon)
            normal = hidden * inverse
            d_in = part[xq, c] + quarter_in[...]
            gvec[1:2, :] = jnp.sum(d_in * normal, axis=0, keepdims=True)
            scaled = d_in * gain_ref[...]
            tot[xq, c] = c_ref[my_rows, :].astype(F32) + inverse * (
                scaled - normal * jnp.mean(scaled * normal, axis=-1, keepdims=True)
            )
            sum_copies[2].start()

        @pl.when(s == first + SHARED_AT)
        def _():
            mix_copies[0].start()
            sum_copies[2].wait()
            sum_copies[3].start()
            sum_copies[3].wait()
            x_ref[...] = tot[...].reshape(T, D).astype(BF)
            for h in range(heads):
                w = wo_ref[h * hd : (h + 1) * hd, :]
                d_att[h] = dot_t(x_ref[...], w).astype(BF)
            for i in range(width // W):
                out_grad = dot_l(x_ref[...], att_ref[:, i * W : (i + 1) * W])
                grads[i] = out_grad.reshape(A, 2, R, W)
                to_y(i).start()
            xn_load.start()
            mix_copies[0].wait()
            mixp[:, c] += mhalf_in[...]

        @pl.when(s == first + SHARED_AT + 1)
        def _():
            for i in range(width // W):
                y_done(i)

        @pl.when(s == first + SHARED_AT + 2)
        def _():
            finish_start()
            core_first.wait()
            part[:, c] += half_in[...]
            x_first.start()

        @pl.when(s == first + SHARED_AT + 3)
        def _():
            for i in range(width // W, pieces):
                y_done(i)

        @pl.when(s == first + SHARED_AT + 4)
        def _():
            xrows_load.wait()
            x32 = xrows[...].astype(F32)
            inverse = lax.rsqrt(jnp.mean(x32 * x32, axis=-1, keepdims=True) + epsilon)
            normal = x32 * inverse
            x_first.wait()
            d_first = part[xq, c] + quarter_in[...]
            gvec[0:1, :] = jnp.sum(d_first * normal, axis=0, keepdims=True)
            for copy in v_sends:
                copy.start()
            scaled = d_first * gain1_ref[...]
            hidq[...] = tot[xq, c] + inverse * (
                scaled - normal * jnp.mean(scaled * normal, axis=-1, keepdims=True)
            )
            gx_out.start()

        @pl.when(s == first + MIX_AT)
        def _():
            mix_copies[1].start()

        @pl.when(s == first + MIX_AT + 2)
        def _():
            mix_copies[1].wait()
            mixp[xq, c] += mquarter_in[...]

        @pl.when(s == first + MIX_AT + 3)
        def _():
            mix_own.start()
            mix_copies[2].start()

        @pl.when(s == first + MIX_AT + 5)
        def _():
            mix_own.wait()
            mix_copies[2].wait()
            mix_copies[3].start()

        @pl.when(s == first + SHARED_AT + 5)
        def _():
            for copy in v_sends:
                copy.wait()
            total = gvec[0:2, :] + gvec_in[0, 0:2, :] + gvec_in[1, 0:2, :] + gvec_in[2, 0:2, :]
            for i in range(trees):
                msg[i, 0:2, :] = total[:, i * R : (i + 1) * R]
            for copy in m_sends:
                copy.start()

        @pl.when((s == first + SHARED_AT) | (s == first + SHARED_AT + 1))
        def _():
            attention_back((s - first - SHARED_AT) * 2)
            attention_back((s - first - SHARED_AT) * 2 + 1)

        @pl.when((k >= 0) & (k < chunks))
        def _():
            for u in range(units):
                if u + 1 < units:
                    load(k, u + 1, (u + 1) % 2)
                own_unit(k, u, u % 2)

        return 0

    lax.fori_loop(first, chunks + LAG, slot_step, 0)

    outs = []
    for j in range(n_own):
        outs += [
            pltpu.make_async_copy(acc.at[:, pl.ds(j * f, f)], gg_ref.at[j], out_sem.at[0, j]),
            pltpu.make_async_copy(acc.at[:, pl.ds((n_own + j) * f, f)], gu_ref.at[j], out_sem.at[1, j]),
            pltpu.make_async_copy(accd.at[pl.ds(j * f, f)], gd_ref.at[j], out_sem.at[2, j]),
        ]
    for copy in outs:
        copy.start()
    per = width // W
    for i in range(per):
        go_ref[:, i * W : (i + 1) * W] = z_done(i)
        gq_ref[:, i * W : (i + 1) * W] = z_done(per + i)
    gk_ref[...] = z_done(2 * per)
    gv_ref[...] = z_done(2 * per + 1)
    for copy in m_sends:
        copy.wait()
    mine = msg[p]
    for j in range(trees - 1):
        mine += msg_in[j]
    g1_ref[...] = mine[0:1]
    g2_ref[...] = mine[1:2]
    gx_out.wait()
    mix_copies[3].wait()

    def sends(k, _):
        x_sent(k)

        @pl.when(k >= EARLY)
        def _():
            c_sent(k)

        return 0

    lax.fori_loop(0, chunks, sends, 0)
    for copy in outs:
        copy.wait()


def experts(
    xf, cf, early, xb, c, dense_gates, own_gates, wg, wu, wd, hidden, x, xn, gain1, gain2, q, k, v, lse, bias,
    wo, att, wq, wk, wv, cosine, sine, trees,
):
    T, D = c.shape
    E, _, f = wg.shape
    own = E // trees
    chunks = T // CHUNK
    A = trees // 2
    Q = T // 4
    R = D // trees
    W = wk.shape[1]
    pieces = 2 * (wq.shape[1] // W) + 2
    gates_in = jnp.pad(dense_gates, ((0, 0), (0, 128 - E)))
    units = A // 4
    og = own_gates.reshape(units, trees // units, 8, chunks, CHUNK).transpose(3, 0, 2, 1, 4)
    og = og.reshape(chunks, units, 8, trees // units * CHUNK)
    slots = 2 if A > 4 else 1
    S = jax.ShapeDtypeStruct
    V = pltpu.VMEM
    out = pl.pallas_call(
        experts_kernel,
        in_specs=[HBM] * 4 + [VMEM] * 3 + [HBM] * 6 + [VMEM] * 14,
        out_specs=[HBM] * 7 + [VMEM] * 6,
        out_shape=[
            S((A, 2, T, D), F32),
            S((A, 2, T, D), F32),
            S((2, 2, Q, D), F32),
            S((Q, D), F32),
            S((own, D, f), F32),
            S((own, D, f), F32),
            S((own, f, D), F32),
            S((1, R), F32),
            S((1, R), F32),
            S((R, wq.shape[1]), F32),
            S((R, wq.shape[1]), F32),
            S((R, W), F32),
            S((R, W), F32),
        ],
        scratch_shapes=[
            V((T, D), BF),
            V((2, D, 2 * EG * f), BF),
            V((2, EG, f, D), BF),
            V((2, 2, Q, D), F32),
            V((2, 2, Q, D), F32),
            V((2, Q, D), F32),
            V((Q, D), F32),
            V((2, 2, Q, D), F32),
            V((2, Q, D), F32),
            V((Q, D), F32),
            V((pieces, A, 2, R, W), F32),
            V((pieces, A, R, W), F32),
            V((pieces, A - 1, R, W), F32),
            V((Q, D), F32),
            V(q.shape, BF),
            V(q.shape, F32),
            V(k.shape, F32),
            V(v.shape, F32),
            V((T, wq.shape[1] + 2 * W), BF),
            V((Q, D), BF),
            V((8, D), F32),
            V((3, 8, D), F32),
            V((trees, 8, R), F32),
            V((trees - 1, 8, R), F32),
            V((D, 2 * own * f), F32),
            V((own * f, D), F32),
            V((slots, 4, 2, CHUNK, D), F32),
            V((slots, 4, 2, CHUNK, D), F32),
            DMA((1 + 2 * EG, 2)),
            DMA((5,)),
            DMA((2, 2)),
            DMA((3, own)),
            DMA((4, chunks)),
            DMA((4, chunks)),
            DMA((2, chunks)),
            DMA((4, chunks - EARLY)),
            DMA((4, chunks - EARLY)),
            DMA((2, chunks - EARLY)),
            DMA(()),
            DMA((pieces,)),
            DMA((pieces,)),
            DMA((pieces, A - 1)),
            DMA((pieces, A - 1)),
            DMA((3,)),
            DMA((3,)),
            DMA((trees - 1,)),
            DMA((trees - 1,)),
            DMA((10,)),
            DMA((10,)),
        ],
        compiler_params=pltpu.CompilerParams(
            collective_id=0, has_side_effects=True, vmem_limit_bytes=62 * 2**20
        ),
    )(
        xf, cf, early, xb, c, gates_in, og, wg, wu, wd, hidden, x, xn, gain1.reshape(1, D), gain2.reshape(1, D),
        q, k, v, lse, bias, wo, att, wq, wk, wv, cosine, sine,
    )
    return out[2:]


def front_kernel(
    x_ref,
    c_ref,
    gain1_ref,
    gain2_ref,
    wq_ref,
    wk_ref,
    wv_ref,
    wo_ref,
    visible_ref,
    cos_ref,
    sin_ref,
    gates_ref,
    early_ref,
    cf_out,
    xn_out,
    bias_out,
    hidden_ref,
    xb_ref,
    xf_ref,
    att_out,
    q_ref,
    k_ref,
    v_ref,
    lse_ref,
    got_ref,
    cf_ref,
    xn_ref,
    bias_ref,
    att,
    others,
    wof,
    wr,
    hot,
    msg,
    peaks,
    ssem,
    rsem,
    wsend,
    wrecv,
    msend,
    mrecv,
    msem,
    c_send,
    c_recv,
    c_own,
    flush_sem,
):
    T, D = x_ref.shape
    trees = got_ref.shape[0]
    heads, _, hd = q_ref.shape
    kvs = k_ref.shape[0]
    group = heads // kvs
    width = heads * hd
    kwidth = kvs * hd
    scale = hd ** (-0.5)
    half = T // 2
    Q = T // 4
    p = lax.axis_index("dp")
    t = lax.axis_index("tensor")
    xq = t // 2
    c = t % 2
    x_dev = (p, (1 - xq) * 2 + c)
    c_dev = (p, xq * 2 + 1 - c)
    peers = [((p + j) % trees, t) for j in range(1, trees)]
    c_start, _, _, c_done, c_sent, pump, _ = gatherer(
        cf_ref, early_ref, c_send, c_recv, c_own, 0, EARLY, *EARLY_ROWS
    )
    sync_with(peers + [x_dev, c_dev])
    cf_ref[...] = c_ref[...].astype(F32)
    flushes = [
        pltpu.make_async_copy(one, two, flush_sem.at[i])
        for i, (one, two) in enumerate(((cf_ref, cf_out), (xn_ref, xn_out), (bias_ref, bias_out)))
    ]
    flushes[0].start()
    c_start(0)
    wof[t] = wo_ref[...].astype(F32)
    w_x = send(wof.at[t], wof.at[t], wsend.at[0], wrecv.at[0], x_dev)
    w_c = send(wof.at[t], wof.at[t], wsend.at[1], wrecv.at[1], c_dev)
    far = (1 - xq) * 2 + c
    w_on = send(wof.at[far], wof.at[far], wsend.at[2], wrecv.at[2], c_dev)
    w_x.start()
    w_c.start()

    row = lax.broadcasted_iota(jnp.int32, (width, width), 0)
    col = lax.broadcasted_iota(jnp.int32, (width, width), 1)
    low = (col % hd) < hd // 2
    turn = jnp.where(low & (row == col + hd // 2), -1.0, jnp.where(~low & (row == col - hd // 2), 1.0, 0.0))
    turn = turn.astype(BF)
    wr[:, :width] = dot(wq_ref[...], turn).astype(BF)
    wr[:, width:] = dot(wk_ref[...], turn[:kwidth, :kwidth]).astype(BF)

    token = lax.broadcasted_iota(jnp.int32, (T, 128), 0)
    seg = lax.broadcasted_iota(jnp.int32, (T, 128), 1)
    begin = jnp.where(seg == 0, 0, TRUNK + (seg - 1) * SEG)
    end = TRUNK + seg * SEG
    hot[...] = ((token >= begin) & (token < end)).astype(F32).astype(BF)

    def project(i, _):
        rows = pl.ds(pl.multiple_of(i * Q, 16), Q)
        x32 = x_ref[rows, :].astype(F32)
        inverse = lax.rsqrt(jnp.mean(x32 * x32, axis=-1, keepdims=True) + epsilon)
        xn = (x32 * inverse * gain1_ref[...]).astype(BF)
        xn_ref[rows, :] = xn
        cosine = cos_ref[rows, :]
        sine = sin_ref[rows, :]
        turned = dot(xn, wr[...])
        query = dot(xn, wq_ref[...])
        query = query * jnp.concatenate([cosine] * (width // 128), axis=1) + turned[:, :width] * jnp.concatenate(
            [sine] * (width // 128), axis=1
        )
        key = dot(xn, wk_ref[...]) * cosine + turned[:, width:] * sine
        value = dot(xn, wv_ref[...])
        for h in range(heads):
            q_ref[h, rows, :] = query[:, h * hd : (h + 1) * hd].astype(BF)
        for g in range(kvs):
            k_ref[g, rows, :] = key[:, g * hd : (g + 1) * hd].astype(BF)
            v_ref[g, rows, :] = value[:, g * hd : (g + 1) * hd].astype(BF)
        mine = hot[rows, :]
        reach = dot(mine, visible_ref[...]).astype(BF)
        near = dot_t(reach, hot[...]) > 0.5
        same = dot_t(mine, hot[...]) > 0.5
        qi = lax.broadcasted_iota(jnp.int32, (Q, T), 0) + i * Q
        kj = lax.broadcasted_iota(jnp.int32, (Q, T), 1)
        seen = near & (~same | (kj <= qi))
        bias_ref[rows, :] = jnp.where(seen, 0.0, -1e30).astype(BF)
        return 0

    lax.fori_loop(0, 4, project, 0)
    flushes[1].start()
    flushes[2].start()
    pump(0)
    peaks[...] = jnp.full_like(peaks, -1e30)
    lane = lax.broadcasted_iota(jnp.int32, (1, 128), 1)

    def attend(i, _):
        rows = pl.ds(pl.multiple_of(i * Q, 16), Q)
        bias = bias_ref[rows, :].astype(F32)
        for h in range(heads):
            g = h // group
            scores = dot_t(q_ref[h, rows, :], k_ref[g]) * scale + bias
            top = jnp.max(scores, axis=-1, keepdims=True)
            expo = jnp.exp(scores - top)
            total = jnp.sum(expo, axis=-1, keepdims=True)
            probs = (expo / total).astype(BF)
            out = dot(probs, v_ref[g]).astype(BF)
            att_out[rows, h * hd : (h + 1) * hd] = out
            att[rows, h * hd : (h + 1) * hd] = out.astype(F32)
            lse_ref[rows, h : h + 1] = top + jnp.log(total)
            peak = jnp.max(top, axis=0, keepdims=True)
            peaks[0:1, :] = jnp.maximum(peaks[0:1, :], jnp.where(lane == h, peak, -1e30))
        return 0

    rows = [pl.ds(i * half, half) for i in range(2)]
    to_x = [send(att.at[r], others.at[1, r], ssem.at[0, i], rsem.at[0, i], x_dev) for i, r in enumerate(rows)]
    to_c = [send(att.at[r], others.at[0, r], ssem.at[1, i], rsem.at[1, i], c_dev) for i, r in enumerate(rows)]
    on = [send(others.at[1, r], others.at[2, r], ssem.at[2, i], rsem.at[2, i], c_dev) for i, r in enumerate(rows)]
    lax.fori_loop(0, 2, attend, 0)
    to_x[0].start()
    to_c[0].start()
    pump(1)
    lax.fori_loop(2, 4, attend, 0)
    to_x[1].start()
    to_c[1].start()
    pump(2)
    msg[...] = gates_ref[...]
    msg[:, 7:8, 0:128] = jnp.broadcast_to(peaks[0:1, :][None], (trees, 1, 128))
    messages = [
        send(msg.at[dev[0]], got_ref.at[j], msend.at[j], mrecv.at[j], dev) for j, dev in enumerate(peers, 1)
    ]
    for copy in messages:
        copy.start()
    mine = pltpu.make_async_copy(msg.at[p], got_ref.at[0], msem)
    mine.start()
    w_x.wait()
    w_on.start()
    w_c.wait()

    def proj(block, owner):
        return dot(block.astype(BF), wof[owner].astype(BF))

    for i, r in enumerate(rows):
        hidden_ref[r, :] = x_ref[r, :].astype(F32) + proj(att[r, :], t)
    for i, r in enumerate(rows):
        to_c[i].wait()
        hidden_ref[r, :] += proj(others[0, r, :], xq * 2 + 1 - c)
    pump(3)
    for i, r in enumerate(rows):
        to_x[i].wait()
        on[i].start()
        hidden_ref[r, :] += proj(others[1, r, :], far)
    pump(4)
    w_on.wait()
    for i, r in enumerate(rows):
        on[i].wait()
        hidden = hidden_ref[r, :] + proj(others[2, r, :], (1 - xq) * 2 + 1 - c)
        hidden_ref[r, :] = hidden
        inverse = lax.rsqrt(jnp.mean(hidden * hidden, axis=-1, keepdims=True) + epsilon)
        low_x = (hidden * inverse * gain2_ref[...]).astype(BF)
        xb_ref[r, :] = low_x
        xf_ref[r, :] = low_x.astype(F32)
    for copy in messages:
        copy.wait()
    mine.wait()
    for s in range(5, EARLY + 3):
        pump(s)
    for copy in flushes:
        copy.wait()
    for k in range(EARLY):
        c_done(k)
        c_sent(k)


def front(x, c, gain1, gain2, wq, wk, wv, wo, visible, cosine, sine, gates_out):
    T, D = x.shape
    trees = gates_out.shape[0]
    A = trees // 2
    heads = wq.shape[1] // HEAD_DIM
    kvs = wk.shape[1] // HEAD_DIM
    width = wq.shape[1]
    S = jax.ShapeDtypeStruct
    V = pltpu.VMEM
    return pl.pallas_call(
        front_kernel,
        in_specs=[VMEM] * 12,
        out_specs=[HBM] * 4 + [VMEM] * 9,
        out_shape=[
            S((A, 2, T, D), F32),
            S((T, D), F32),
            S((T, D), BF),
            S((T, T), BF),
            S((T, D), F32),
            S((T, D), BF),
            S((T, D), F32),
            S((T, width), BF),
            S((heads, T, HEAD_DIM), BF),
            S((kvs, T, HEAD_DIM), BF),
            S((kvs, T, HEAD_DIM), BF),
            S((T, 128), F32),
            S(gates_out.shape, F32),
        ],
        scratch_shapes=[
            V((T, D), F32),
            V((T, D), BF),
            V((T, T), BF),
            V((T, width), F32),
            V((3, T, width), F32),
            V((4, width, D), F32),
            V((D, width + wk.shape[1]), BF),
            V((T, 128), BF),
            V(gates_out.shape, F32),
            V((8, 128), F32),
            DMA((3, 2)),
            DMA((3, 2)),
            DMA((3,)),
            DMA((3,)),
            DMA((trees,)),
            DMA((trees,)),
            DMA(()),
            DMA((4, EARLY)),
            DMA((4, EARLY)),
            DMA((2, EARLY)),
            DMA((3,)),
        ],
        compiler_params=pltpu.CompilerParams(
            collective_id=1, has_side_effects=True, vmem_limit_bytes=58 * 2**20
        ),
    )(x, c, gain1.reshape(1, D), gain2.reshape(1, D), wq, wk, wv, wo, visible, cosine, sine, gates_out)


def last_kernel(hid_ref, mix_ref, got_ref, limit_ref, wq_ref, wk_ref, *refs):
    n = (len(refs) - 9) // 3
    out_ref, factor_ref, qs_ref, ks_ref = refs[n : n + 4]
    hid, mix, held = refs[2 * n + 4], refs[2 * n + 5], refs[2 * n + 6 : 3 * n + 6]
    in_sem, sem, big_sem = refs[3 * n + 6 :]
    big = [pltpu.make_async_copy(hid_ref, hid, big_sem.at[0]), pltpu.make_async_copy(mix_ref, mix, big_sem.at[1])]
    ins = [pltpu.make_async_copy(refs[i], held[i], in_sem.at[i]) for i in range(n)]
    outs = [pltpu.make_async_copy(held[i], refs[n + 4 + i], sem.at[i]) for i in range(n)]
    for copy in ins + big:
        copy.start()
    heads = limit_ref.shape[1]
    limits = limit_ref[...]
    peaks = jnp.max(got_ref[:, 7, 0:128], axis=0, keepdims=True)[:, 0:heads]
    factors = limits / jnp.maximum(peaks, limits)
    factor_ref[...] = factors
    group = wq_ref.shape[1] // wk_ref.shape[1]
    roots = [jnp.sqrt(factors[:, h : h + 1]) for h in range(heads)]
    least = [
        jnp.sqrt(jnp.min(factors[:, g * group : (g + 1) * group], axis=1, keepdims=True)) for g in range(heads // group)
    ]

    def scaled(w_ref, values):
        head = lax.broadcasted_iota(jnp.int32, (1, w_ref.shape[1]), 1) // HEAD_DIM
        row = jnp.zeros((1, w_ref.shape[1]), F32)
        for h, value in enumerate(values):
            row = jnp.where(head == h, value, row)
        return (w_ref[...].astype(F32) * row).astype(BF)

    qs_ref[...] = scaled(wq_ref, roots)
    ks_ref[...] = scaled(wk_ref, least)
    for i in range(n):
        ins[i].wait()
        outs[i].start()
    for copy in big:
        copy.wait()
    out_ref[...] = (hid[...] + mix[...]).astype(BF)
    for copy in outs:
        copy.wait()


def last(hidden, mixture, got, limits, wq, wk, *rest):
    T, D = hidden.shape
    S = jax.ShapeDtypeStruct
    n = len(rest)
    return pl.pallas_call(
        last_kernel,
        in_specs=[HBM] * 2 + [VMEM] * 4 + [HBM] * n,
        out_specs=[VMEM] * 4 + [HBM] * n,
        out_shape=[
            S((T, D), BF),
            S((1, limits.shape[0]), F32),
            S(wq.shape, BF),
            S(wk.shape, BF),
        ]
        + [S(r.shape, r.dtype) for r in rest],
        scratch_shapes=[pltpu.VMEM((T, D), F32)] * 2
        + [pltpu.VMEM(r.shape, r.dtype) for r in rest]
        + [DMA((n,)), DMA((n,)), DMA((2,))],
        compiler_params=pltpu.CompilerParams(vmem_limit_bytes=62 * 2**20),
    )(hidden, mixture.reshape(T, D), got, limits.reshape(1, -1), wq, wk, *rest)


def local(
    block_input,
    norm_first,
    norm_second,
    w_query,
    w_key,
    w_value,
    w_out,
    w_gate,
    w_up,
    w_down,
    routes,
    gates,
    parents,
    clip_limits,
    cotangent,
):
    count, width = block_input.shape
    head_dim = HEAD_DIM
    query_cols = w_query.shape[1]
    key_cols = w_key.shape[1]
    query_heads = query_cols // head_dim
    kv_heads = key_cols // head_dim
    trees = lax.axis_size("dp")
    own = EXPERTS // trees
    position, visible = tree_tables(parents[0], count)
    visible = jnp.pad(visible.astype(jnp.bfloat16), ((0, 128 - SEGS), (0, 128 - SEGS)))
    cosine, sine = rotary_tables(position, head_dim)
    wide_cosine = jnp.tile(cosine[:, 0], (1, 128 * 2 // head_dim))
    wide_sine = jnp.tile(sine[:, 0], (1, 128 * 2 // head_dim))
    routed = routes[:, :, None] == jnp.arange(EXPERTS, dtype=jnp.int32)[None, None, :]
    dense_gates = jnp.sum(jnp.where(routed, gates[:, :, None], 0.0), axis=1)
    gates_out = jnp.pad(dense_gates.T.reshape(trees, own, count), ((0, 0), (0, 8 - own), (0, 0)))
    (
        early,
        c_wide,
        input_first,
        bias,
        hidden,
        input_second,
        x_wide,
        attended_parts,
        queries,
        keys,
        values,
        log_norms,
        got,
    ) = front(
        block_input,
        cotangent,
        norm_first,
        norm_second,
        w_query,
        w_key,
        w_value,
        w_out,
        visible,
        wide_cosine,
        wide_sine,
        gates_out,
    )
    order = (lax.axis_index("dp") - jnp.arange(trees)) % trees
    hot = (order[:, None] == jnp.arange(trees)[None, :]).astype(jnp.float32)
    own_gates = jnp.sum(hot[:, :, None, None] * got[:, None], axis=0)
    (
        mixture,
        grad_x,
        gate_shard,
        up_shard,
        down_shard,
        first_gain_grad,
        second_shard,
        out_shard,
        query_shard,
        key_shard,
        value_shard,
    ) = experts(
        x_wide,
        c_wide,
        early,
        input_second,
        cotangent,
        dense_gates,
        own_gates,
        w_gate,
        w_up,
        w_down,
        hidden,
        block_input,
        input_first,
        norm_first,
        norm_second,
        queries,
        keys,
        values,
        log_norms,
        bias,
        w_out,
        attended_parts,
        w_query,
        w_key,
        w_value,
        wide_cosine,
        wide_sine,
        trees,
    )
    block_out, factors, query_scaled, key_scaled, *rest = last(
        hidden,
        mixture,
        got,
        clip_limits,
        w_query,
        w_key,
        grad_x,
        first_gain_grad,
        second_shard,
        query_shard,
        key_shard,
        value_shard,
        out_shard,
        gate_shard,
        up_shard,
        down_shard,
    )
    grad_x, first_gain_grad, second_shard = rest[:3]
    return (
        block_out,
        grad_x,
        first_gain_grad.reshape(width // trees),
        second_shard.reshape(width // trees),
        *rest[3:],
        factors.reshape(query_heads),
        query_scaled,
        key_scaled,
    )


def solution(mesh):
    placed = (
        P("dp", None),
        P(),
        P(),
        P(None, "tensor"),
        P(None, "tensor"),
        P(None, "tensor"),
        P("tensor", None),
        P(None, None, "tensor"),
        P(None, None, "tensor"),
        P(None, "tensor", None),
        P("dp", None),
        P("dp", None),
        P("dp", None),
        P("tensor"),
        P("dp", None),
    )
    return jax.shard_map(
        local,
        mesh=mesh,
        in_specs=placed,
        out_specs=(
            P("dp", None),
            P(("dp", "tensor"), None),
            P("dp"),
            P("dp"),
            P("dp", "tensor"),
            P("dp", "tensor"),
            P("dp", "tensor"),
            P("dp", "tensor"),
            P("dp", None, "tensor"),
            P("dp", None, "tensor"),
            P("dp", "tensor", None),
            P("tensor"),
            P(None, "tensor"),
            P(None, "tensor"),
        ),
        check_vma=False,
    )
```
